512 devices in a mesh: frame: 16 (over y, x), tile: 32 (over z, core).
Axes of the slice: x: 4, y: 4, z: 16, core: 2. Of those that a mesh axis runs over, the one named last changes fastest.
Arguments:
- features: bfloat16 [32, 192, 64, 128], P('frame', 'tile'), may hold values from -40 to 40
- norm_gain_weight: float32 [128], replicated, may hold values from 0.5 to 2
- norm_bias: float32 [128], replicated, may hold values from -1 to 1
- kernel: bfloat16 [3, 3, 3, 128, 128], replicated, may hold values from -0.109375 to 0.109375
- cotangent: bfloat16 [32, 192, 64, 128], P('frame', 'tile'), may hold values from -6 to 6
Outputs:
- feature_gradient: bfloat16 [32, 192, 64, 128], P('frame', 'tile')
- grad_kernel: float32 [3, 3, 3, 128, 128], replicated
- gain_gradient: float32 [128], replicated
- grad_shift: float32 [128], replicated
The draws below stay inside these ranges and needn't reach their ends.
All inputs are finite; a program needn't handle non-finite values.
Results may differ from the reference program's by a relative error of at most 0.0012.
The reference program's roundings to bfloat16 on the way (of `activated`) count: a program that leaves them out, or rounds other values in their place, can miss the bound.
Values may be sent and summed in bfloat16 or wider, within the bound.
A program may use at most 64 MiB of HBM per device.

```python
import math
import jax
import jax.numpy as jnp
from jax import lax

CH = 128
GROUPS = 32
COLS = 64
FRAMES = 32
ROWS = 192


def draw_features(key, part):
    key = jax.random.fold_in(key, 1)
    first, second, third = jax.random.split(key, 3)
    array_shape = (FRAMES, ROWS, COLS, CH)
    base = jnp.clip(jax.random.normal(first, array_shape, jnp.float32), -6.0, 6.0)
    frame_index = jnp.arange(FRAMES, dtype=jnp.float32)
    frame_scale = 1.0 + 2.0 * frame_index / max(FRAMES - 1, 1)
    chan_scale = jnp.exp(jax.random.uniform(second, (CH,), jnp.float32, math.log(0.5), math.log(2.0)))
    offset = jax.random.uniform(third, (CH,), jnp.float32, -1.0, 1.0)
    value_array = base * frame_scale[:, None, None, None] * chan_scale + offset
    value_array = jnp.clip(value_array, -40.0, 40.0)
    return value_array.astype(jnp.bfloat16)


def block_scale(key, shape, cuts, smallest, top_value):
    def one(position, blocks):
        draws = jax.random.uniform(jax.random.fold_in(jax.random.fold_in(key, 6), position), (blocks,), jnp.float32, smallest / len(cuts), top_value / len(cuts))
        return jnp.repeat(jnp.exp(draws), shape[position] // blocks).reshape((-1,) + (1,) * (len(shape) - position - 1))

    factor_of = one(*cuts[0])
    for cut in cuts[1:]:
        factor_of = factor_of * one(*cut)
    return factor_of


def noise(stream_key, dims, width, limit, pieces=(), kind=jnp.bfloat16):
    entries = jax.random.normal(stream_key, dims, jnp.float32) * width
    if len(pieces) > 0:
        entries = block_scale(stream_key, dims, pieces, -0.22, 0.18) * entries
    return jnp.clip(entries, min=-limit, max=limit).astype(kind)


def setup_inputs(seed: int = 0) -> dict:
    streams_of = jax.random.split(jax.random.key(seed), 6)
    features = draw_features(jax.random.fold_in(streams_of[5], 71), 0)
    norm_gain_weight = jnp.clip(jnp.exp(jax.random.uniform(streams_of[1], (CH,), jnp.float32, math.log(0.5), math.log(2.0))), 0.5, 2.0)
    norm_bias = jnp.clip(jax.random.uniform(streams_of[2], (CH,), jnp.float32, -1.0, 1.0), -1.0, 1.0)
    kernel = noise(streams_of[3], (3, 3, 3, CH, CH), (27 * CH) ** -0.5, 0.109375)
    cotangent = noise(streams_of[4], (FRAMES, ROWS, COLS, CH), 1.0, 6.0, ((0, 16), (1, 32)))
    return {"features": features, "norm_gain_weight": norm_gain_weight, "norm_bias": norm_bias, "kernel": kernel, "cotangent": cotangent}


epsilon = 1e-06

def convolve(field, weights):
    padded = jnp.pad(field, ((2, 0), (1, 1), (1, 1), (0, 0)))
    result = lax.conv_general_dilated(padded[None], weights, (1, 1, 1), 'VALID', dimension_numbers=('NDHWC', 'DHWIO', 'NDHWC'), precision=lax.Precision.HIGHEST)
    return result[0]

def reference(features, norm_gain_weight, norm_bias, kernel, cotangent):
    per_group = CH // GROUPS
    cell_count = FRAMES * ROWS * COLS * per_group
    value_array = features.astype(jnp.float32)
    grouped = value_array.reshape(-1, GROUPS, per_group)
    average = lax.optimization_barrier(jnp.sum(grouped, axis=(0, 2))) / cell_count
    centered_values = grouped - average[None, :, None]
    spread = lax.optimization_barrier(jnp.sum(centered_values * centered_values, axis=(0, 2))) / cell_count
    inverse_deviation = lax.rsqrt(spread + epsilon)
    standardized_input = (centered_values * inverse_deviation[None, :, None]).reshape(value_array.shape)
    normed_output = standardized_input * norm_gain_weight + norm_bias
    sigmoid_output = jax.nn.sigmoid(normed_output)
    activated = (normed_output * sigmoid_output).astype(jnp.bfloat16)
    outputs, pullback = jax.vjp(convolve, activated.astype(jnp.float32), kernel.astype(jnp.float32))
    grad_act, grad_kernel = pullback(cotangent.astype(jnp.float32))
    normed_gradient = grad_act * sigmoid_output * (1.0 + normed_output * (1.0 - sigmoid_output))
    gain_gradient = lax.optimization_barrier(jnp.sum(normed_gradient * standardized_input, axis=(0, 1, 2)))
    grad_shift = lax.optimization_barrier(jnp.sum(normed_gradient, axis=(0, 1, 2)))
    grad_mean = lax.optimization_barrier(jnp.sum((norm_gain_weight * grad_shift).reshape(GROUPS, per_group), axis=1)) / cell_count
    grad_proj = lax.optimization_barrier(jnp.sum((norm_gain_weight * gain_gradient).reshape(GROUPS, per_group), axis=1)) / cell_count
    channel_mean = jnp.repeat(grad_mean, per_group)
    channel_projection = jnp.repeat(grad_proj, per_group)
    inverse_channel_count = jnp.repeat(inverse_deviation, per_group)
    feature_gradient = (inverse_channel_count * (normed_gradient * norm_gain_weight - channel_mean - standardized_input * channel_projection)).astype(jnp.bfloat16)
    return (feature_gradient, grad_kernel, gain_gradient, grad_shift)
```

```python
import jax
import jax.numpy as jnp
from jax import lax
from jax.experimental import pallas as pl
from jax.experimental.pallas import tpu as pltpu
from jax.sharding import PartitionSpec as P

MESH = pl.DeviceIdType.MESH
GROUPS = 32
EPS = 1e-06
NX = 4
NY = 4
NZ = 16
TAPS = 28
TY = TAPS // NY
NTILES = 2 * TY
F32 = jnp.float32
BF16 = jnp.bfloat16


def group_sum(v):
    lane = lax.broadcasted_iota(jnp.int32, v.shape, 1)
    v = v + jnp.where(lane % 2 == 0, pltpu.roll(v, 127, 1), pltpu.roll(v, 1, 1))
    return v + jnp.where(lane % 4 < 2, pltpu.roll(v, 126, 1), pltpu.roll(v, 2, 1))


def body(
    feat, gain, bias, w, cot,
    fg, gk, gs,
    ext, cotx, gact, xhat, act_t, s1, s2, g1, g2,
    part, rc, ra1, rb1, ra2, rb2, zsrc, rz, zg,
    halo_s, halo_r, s1_s, s1_r, s2_s, s2_r, g1_s, g1_r, g2_s, g2_r,
    core_s, core_r, st_s, st_r, z_s, z_r, zg_s, zg_r, ag_s, ag_r,
):
    f, t = lax.axis_index("frame"), lax.axis_index("tile")
    nf, nt = NX * NY, NZ * 2
    y, x = f // NX, f % NX
    z, core = t // 2, t % 2
    frames, rows, cols, ch = feat.shape
    cells = frames * rows * cols
    chunk = 128
    barrier = pltpu.get_barrier_semaphore()

    def at(df, dt):
        return ((f + df + nf) % nf, (t + dt + nt) % nt)

    def rcopy(src, dst, ss, rs, dev):
        return pltpu.make_async_remote_copy(
            src_ref=src, dst_ref=dst, send_sem=ss, recv_sem=rs,
            device_id=dev, device_id_type=MESH,
        )

    def hello(dev):
        pl.semaphore_signal(barrier, inc=1, device_id=dev, device_id_type=MESH)

    @pl.loop(1, nf)
    def _(i):
        hello(((f + i) % nf, t))

    @pl.loop(1, nt)
    def _(i):
        hello((f, (t + i) % nt))

    for df in (-1, 1):
        for dt in (-1, 1):
            hello(at(df, dt))

    def rows_of(ref, k):
        per = cols
        return ref

    flat = feat.reshape(cells, ch)
    flat_cot = cot.reshape(cells, ch)

    def add_up(k, acc):
        return acc + jnp.sum(flat[pl.ds(k * chunk, chunk), :].astype(F32), axis=0, keepdims=True)

    mean = lax.fori_loop(0, cells // chunk, add_up, jnp.zeros((1, ch), F32)) / cells

    def add_sq(k, acc):
        d = flat[pl.ds(k * chunk, chunk), :].astype(F32) - mean
        return acc + jnp.sum(d * d, axis=0, keepdims=True)

    m2 = lax.fori_loop(0, cells // chunk, add_sq, jnp.zeros((1, ch), F32))
    s1[f, 0:1, :] = mean
    s1[f, 1:2, :] = m2

    pl.semaphore_wait(barrier, (nf - 1) + (nt - 1) + 4)

    def send_frame(buf, ss, rs):
        @pl.loop(1, nf)
        def _(i):
            to = (f + i) % nf
            rcopy(buf.at[f], buf.at[f], ss.at[to], rs.at[f], (to, t)).start()

    def wait_frame(buf, ss, rs):
        @pl.loop(1, nf)
        def _(i):
            to = (f + i) % nf
            rcopy(buf.at[to], buf.at[to], ss.at[to], rs.at[to], (to, t)).wait()

    def send_tile(buf, ss, rs):
        @pl.loop(1, nt)
        def _(i):
            to = (t + i) % nt
            rcopy(buf.at[t], buf.at[t], ss.at[to], rs.at[t], (f, to)).start()

    def wait_tile(buf, ss, rs):
        @pl.loop(1, nt)
        def _(i):
            to = (t + i) % nt
            rcopy(buf.at[to], buf.at[to], ss.at[to], rs.at[to], (f, to)).wait()

    send_frame(s1, s1_s, s1_r)

    halo = [
        rcopy(cot, ext.at[2:4, 1:7], halo_s.at[0], halo_r.at[0], at(-1, 0)),
        rcopy(cot.at[:, 0], ext.at[0:2, 7], halo_s.at[1], halo_r.at[1], at(0, -1)),
        rcopy(cot.at[:, 5], ext.at[0:2, 0], halo_s.at[2], halo_r.at[2], at(0, 1)),
        rcopy(cot.at[:, 0], ext.at[2:4, 7], halo_s.at[3], halo_r.at[3], at(-1, -1)),
        rcopy(cot.at[:, 5], ext.at[2:4, 0], halo_s.at[4], halo_r.at[4], at(-1, 1)),
    ]
    for c in halo:
        c.start()
    ext[0:2, 1:7] = cot[...]

    def combine(buf, each):
        m = buf[:, 0, :]
        n = m.shape[0]
        avg = jnp.sum(m, axis=0, keepdims=True) / n
        d = m - avg
        return avg, jnp.sum(buf[:, 1, :], axis=0, keepdims=True) + each * jnp.sum(
            d * d, axis=0, keepdims=True
        )

    wait_frame(s1, s1_s, s1_r)
    avg, m2 = combine(s1, float(cells))
    s2[t, 0:1, :] = avg
    s2[t, 1:2, :] = m2
    send_tile(s2, s2_s, s2_r)

    for c in halo:
        c.wait()

    @pl.when(t == 0)
    def _():
        ext[:, 0] = jnp.zeros((4, cols, ch), BF16)

    @pl.when(t == nt - 1)
    def _():
        ext[:, 7] = jnp.zeros((4, cols, ch), BF16)

    @pl.when(f == nf - 1)
    def _():
        ext[2:4] = jnp.zeros((2, 8, cols, ch), BF16)

    @pl.loop(0, 4 * 8)
    def _(k):
        p, r = k // 8, k % 8
        v = ext[p, r].astype(F32)
        col = lax.broadcasted_iota(jnp.int32, v.shape, 0)
        up = jnp.where(col == cols - 1, 0.0, pltpu.roll(v, cols - 1, 0))
        down = jnp.where(col == 0, 0.0, pltpu.roll(v, 1, 0))
        cotx[p, r, :, 0:ch] = up.astype(BF16)
        cotx[p, r, :, ch : 2 * ch] = ext[p, r]
        cotx[p, r, :, 2 * ch : 3 * ch] = down.astype(BF16)

    def patch(k):
        a, b = k // 3, k % 3
        return cotx[pl.ds(2 - a, frames), pl.ds(2 - b, rows)].reshape(cells, 3 * ch)

    gact[...] = jnp.zeros_like(gact)

    @pl.loop(0, 9)
    def _(k):
        taps = jnp.concatenate([w[3 * k], w[3 * k + 1], w[3 * k + 2]], axis=1)
        gact[...] += lax.dot_general(
            patch(k), taps, (((1,), (1,)), ((), ())), preferred_element_type=F32
        )

    wait_tile(s2, s2_s, s2_r)
    avg, m2 = combine(s2, float(cells * nf))
    per_channel = float(cells * nf * nt)
    group = ch // GROUPS
    g_avg = group_sum(avg) / group
    d = avg - g_avg
    spread = group_sum(m2 + per_channel * (d * d)) / (per_channel * group)
    inv = lax.rsqrt(spread + EPS)

    gw, bw = gain[...], bias[...]

    def norm(k, acc):
        at_rows = pl.ds(k * chunk, chunk)
        xh = (flat[at_rows, :].astype(F32) - g_avg) * inv
        nrm = xh * gw + bw
        s = 1.0 / (1.0 + jnp.exp(-nrm))
        act = (nrm * s).astype(BF16).astype(F32)
        act_t[:, at_rows] = act.T.astype(BF16)
        gn = gact[at_rows, :] * s * (1.0 + nrm * (1.0 - s))
        gact[at_rows, :] = gn
        xhat[at_rows, :] = xh
        return (
            acc[0] + jnp.sum(gn * xh, axis=0, keepdims=True),
            acc[1] + jnp.sum(gn, axis=0, keepdims=True),
        )

    zero = jnp.zeros((1, ch), F32)
    sums = (zero, zero)
    for k in range(cells // chunk):
        sums = norm(k, sums)
    g1[f, 0:1, :] = sums[0]
    g1[f, 1:2, :] = sums[1]
    send_frame(g1, g1_s, g1_r)

    part[:, :, :, 27] = jnp.zeros((2, 2, NX, 8, ch), F32)

    @pl.loop(0, 9)
    def _(k):
        got = jnp.dot(act_t[...], patch(k), preferred_element_type=F32)
        for e in range(3):
            part[:, :, :, 3 * k + e] = got[:, e * ch : (e + 1) * ch].reshape(2, 2, NX, 8, ch)

    other = 1 - core
    swap = rcopy(part.at[other], rc, core_s.at[0], core_r.at[0], (f, z * 2 + other))
    swap.start()

    wait_frame(g1, g1_s, g1_r)
    g2[t, 0:1, :] = jnp.sum(g1[:, 0, :], axis=0, keepdims=True)
    g2[t, 1:2, :] = jnp.sum(g1[:, 1, :], axis=0, keepdims=True)
    send_tile(g2, g2_s, g2_r)

    swap.wait()
    mine = part.at[core]

    @pl.loop(0, 2)
    def _(h):
        @pl.loop(0, NX)
        def _(i):
            mine[h, i] += rc[h, i]

    first = []
    for i in range(1, 4):
        xo, yo = (x + i) % NX, (y + i) % NY
        first.append(rcopy(mine.at[0, xo], ra1.at[i - 1], st_s.at[0, i], st_r.at[0, i], (y * NX + xo, t)))
        first.append(
            rcopy(mine.at[1, :, pl.ds(yo * TY, TY)], rb1.at[i - 1], st_s.at[1, i], st_r.at[1, i], (yo * NX + x, t))
        )
    for c in first:
        c.start()
    for c in first:
        c.wait()
    mine[0, x] += ra1[0] + ra1[1] + ra1[2]
    own_y = pl.ds(y * TY, TY)
    mine[1, :, own_y] += rb1[0] + rb1[1] + rb1[2]

    second = []
    for i in range(1, 4):
        xo, yo = (x + i) % NX, (y + i) % NY
        second.append(
            rcopy(mine.at[0, x, pl.ds(yo * TY, TY)], ra2.at[i - 1], st_s.at[2, i], st_r.at[2, i], (yo * NX + x, t))
        )
        second.append(
            rcopy(mine.at[1, xo, own_y], rb2.at[i - 1], st_s.at[3, i], st_r.at[3, i], (y * NX + xo, t))
        )
    for c in second:
        c.start()
    for c in second:
        c.wait()
    zsrc[0:TY] = mine[0, x, own_y] + (ra2[0] + ra2[1] + ra2[2])
    zsrc[TY:NTILES] = mine[1, x, own_y] + (rb2[0] + rb2[1] + rb2[2])

    def zdev(j):
        return (f, j * 2 + core)

    @pl.loop(0, NTILES)
    def _(j):
        @pl.when(j != z)
        def _():
            rcopy(zsrc.at[j], rz.at[z], z_s.at[j], z_r.at[z], zdev(j)).start()

    wait_tile(g2, g2_s, g2_r)
    d_gain = jnp.sum(g2[:, 0, :], axis=0, keepdims=True)
    d_shift = jnp.sum(g2[:, 1, :], axis=0, keepdims=True)
    gs[0:1, :] = d_gain
    gs[1:2, :] = d_shift
    count = per_channel * group
    g_mean = group_sum(gw * d_shift) / count
    g_proj = group_sum(gw * d_gain) / count

    out = fg.reshape(cells, ch)

    @pl.loop(0, cells // chunk)
    def _(k):
        at_rows = pl.ds(pl.multiple_of(k * chunk, chunk), chunk)
        out[at_rows, :] = (
            inv * (gact[at_rows, :] * gw - g_mean - xhat[at_rows, :] * g_proj)
        ).astype(BF16)

    @pl.loop(0, NTILES)
    def _(j):
        @pl.when(j != z)
        def _():
            rcopy(zsrc.at[j], rz.at[z], z_s.at[j], z_r.at[z], zdev(j)).wait_send()

    @pl.when(z < NTILES)
    def _():
        rz[z] = zsrc[z]

        @pl.loop(1, NZ)
        def _(i):
            j = (z + i) % NZ
            rcopy(zsrc.at[0], rz.at[j], z_s.at[0], z_r.at[j], zdev(j)).wait_recv()

        zg[z] = jnp.sum(rz[...], axis=0)

        @pl.loop(1, NZ)
        def _(i):
            j = (z + i) % NZ
            rcopy(zg.at[z], zg.at[z], zg_s.at[j], zg_r.at[z], zdev(j)).start()

        @pl.loop(1, NZ)
        def _(i):
            j = (z + i) % NZ
            rcopy(zg.at[z], zg.at[z], zg_s.at[j], zg_r.at[z], zdev(j)).wait_send()

    @pl.loop(0, NTILES)
    def _(j):
        @pl.when(j != z)
        def _():
            rcopy(zg.at[j], zg.at[j], zg_s.at[0], zg_r.at[j], zdev(j)).wait_recv()

    full = gk.at[core]
    full[0, x, own_y] = zg[0:TY]
    full[1, x, own_y] = zg[TY:NTILES]

    def spread_out(half_x, stage):
        sends, arrivals = [], []
        for i in range(1, 4):
            xo, yo = (x + i) % NX, (y + i) % NY
            for half, axis_x in ((half_x, True), (1 - half_x, False)):
                dev = (y * NX + xo, t) if axis_x else (yo * NX + x, t)
                xa, ya = (xo, y) if axis_x else (x, yo)
                if stage == 0:
                    here = full.at[half, x, own_y]
                    there = full.at[half, xa, pl.ds(ya * TY, TY)]
                elif axis_x:
                    here = full.at[half, x]
                    there = full.at[half, xo]
                else:
                    here = full.at[half, :, own_y]
                    there = full.at[half, :, pl.ds(yo * TY, TY)]
                k = 2 * stage + half
                mine_at = x if axis_x else y
                from_at = xo if axis_x else yo
                sends.append(rcopy(here, here, ag_s.at[k, from_at], ag_r.at[k, mine_at], dev))
                arrivals.append(rcopy(there, there, ag_s.at[k, from_at], ag_r.at[k, from_at], dev))
        for c in sends:
            c.start()
        for c in sends:
            c.wait_send()
        for c in arrivals:
            c.wait_recv()

    spread_out(1, 0)
    spread_out(0, 1)

    last = rcopy(full, full, core_s.at[1], core_r.at[1], (f, z * 2 + other))
    last.start()
    last.wait_send()
    rcopy(gk.at[other], gk.at[other], core_s.at[1], core_r.at[1], (f, z * 2 + other)).wait_recv()


def on_device(features, norm_gain_weight, norm_bias, kernel, cotangent):
    frames, rows, cols, ch = features.shape
    cells = frames * rows * cols
    nf, nt = NX * NY, NZ * 2
    vm = pl.BlockSpec(memory_space=pltpu.VMEM)
    dma = pltpu.SemaphoreType.DMA
    fg, gk, gs = pl.pallas_call(
        body,
        out_shape=(
            jax.ShapeDtypeStruct(features.shape, BF16),
            jax.ShapeDtypeStruct((2, 2, NX, TAPS, 8, ch), F32),
            jax.ShapeDtypeStruct((2, ch), F32),
        ),
        in_specs=[vm] * 5,
        out_specs=(vm, vm, vm),
        scratch_shapes=[
            pltpu.VMEM((4, rows + 2, cols, ch), BF16),
            pltpu.VMEM((4, rows + 2, cols, 3 * ch), BF16),
            pltpu.VMEM((cells, ch), F32),
            pltpu.VMEM((cells, ch), F32),
            pltpu.VMEM((ch, cells), BF16),
            pltpu.VMEM((nf, 2, ch), F32),
            pltpu.VMEM((nt, 2, ch), F32),
            pltpu.VMEM((nf, 2, ch), F32),
            pltpu.VMEM((nt, 2, ch), F32),
            pltpu.VMEM((2, 2, NX, TAPS, 8, ch), F32),
            pltpu.VMEM((2, NX, TAPS, 8, ch), F32),
            pltpu.VMEM((3, TAPS, 8, ch), F32),
            pltpu.VMEM((3, NX, TY, 8, ch), F32),
            pltpu.VMEM((3, TY, 8, ch), F32),
            pltpu.VMEM((3, TY, 8, ch), F32),
            pltpu.VMEM((NTILES, 8, ch), F32),
            pltpu.VMEM((NZ, 8, ch), F32),
            pltpu.VMEM((NTILES, 8, ch), F32),
            dma((5,)), dma((5,)),
            dma((nf,)), dma((nf,)), dma((nt,)), dma((nt,)),
            dma((nf,)), dma((nf,)), dma((nt,)), dma((nt,)),
            dma((2,)), dma((2,)),
            dma((4, 4)), dma((4, 4)),
            dma((NZ,)), dma((NZ,)), dma((NZ,)), dma((NZ,)),
            dma((4, 4)), dma((4, 4)),
        ],
        compiler_params=pltpu.CompilerParams(
            collective_id=0, has_side_effects=True, vmem_limit_bytes=40 * 2**20
        ),
    )(
        features,
        norm_gain_weight.reshape(1, ch),
        norm_bias.reshape(1, ch),
        kernel.reshape(27, ch, ch),
        cotangent,
    )
    grad_kernel = jnp.transpose(gk, (3, 0, 1, 2, 4, 5))[:27].reshape(3, 3, 3, ch, ch)
    return fg, grad_kernel, gs[0], gs[1]


def solution(mesh):
    placed = (P("frame", "tile", None, None), P(), P(), P(), P("frame", "tile", None, None))
    return jax.shard_map(
        on_device,
        mesh=mesh,
        in_specs=placed,
        out_specs=(P("frame", "tile", None, None), P(), P(), P()),
        check_vma=False,
    )
```

```python
import functools

import jax
import jax.numpy as jnp
from jax import lax
from jax.experimental import pallas as pl
from jax.experimental.pallas import tpu as pltpu
from jax.sharding import PartitionSpec as P

MESH = pl.DeviceIdType.MESH
GROUPS = 32
EPS = 1e-06
NX = 4
NY = 4
NZ = 16
NF = NX * NY
LAST = 26
HALF = 7
F32 = jnp.float32
BF16 = jnp.bfloat16
CHUNK = 128


def group_sum(v):
    lane = lax.broadcasted_iota(jnp.int32, v.shape, 1)
    v = v + jnp.where(lane % 2 == 0, pltpu.roll(v, 127, 1), pltpu.roll(v, 1, 1))
    return v + jnp.where(lane % 4 < 2, pltpu.roll(v, 126, 1), pltpu.roll(v, 2, 1))


def rcopy(src, dst, ss, rs, dev):
    return pltpu.make_async_remote_copy(
        src_ref=src, dst_ref=dst, send_sem=ss, recv_sem=rs, device_id=dev, device_id_type=MESH
    )


def body(
    stop,
    feat_h, gain_h, bias_h, w_h, cot_h,
    fg, gk, gs,
    fx, gain, bias, w, ext, cotx, gact, xhat, act_t,
    s0, s1, s2, g0, g1, g2,
    part, ra1, rb1, ra2, rb2, zsrc, rz,
    load_s, halo_s, halo_r, sm_s, sm_r, st_s, st_r, z_s, z_r, ag_s, ag_r, fw_s, fw_r,
):
    f, t = lax.axis_index("frame"), lax.axis_index("tile")
    y, x = f // NX, lax.rem(f, NX)
    z, core = t // 2, lax.rem(t, 2)
    other = 1 - core
    _, frames, rows, cols, ch = fx.shape
    cells = frames * rows * cols
    mate = (f, z * 2 + other)
    zn = lax.rem(z - 1 + 2 * core + NZ, NZ)
    fdevs = [(lax.rem(f + i, NF), t) for i in range(1, NF)]
    far = sorted(range(1, NZ), key=lambda i: -min(i, NZ - i))
    zs = [lax.rem(z + i, NZ) for i in far]
    zdevs = [(f, j * 2 + core) for j in zs]
    xs = [lax.rem(x + i, NX) for i in range(1, NX)]
    ys = [lax.rem(y + i, NY) for i in range(1, NY)]
    xdevs = [(y * NX + i, t) for i in xs]
    ydevs = [(i * NX + x, t) for i in ys]
    own_rows = pl.ds(1 + rows * core, rows)
    mate_rows = pl.ds(1 + rows * other, rows)

    loads = [
        pltpu.make_async_copy(feat_h, fx.at[core], load_s.at[0]),
        pltpu.make_async_copy(cot_h, ext.at[0:2, own_rows], load_s.at[1]),
        pltpu.make_async_copy(w_h, w, load_s.at[2]),
        pltpu.make_async_copy(gain_h, gain, load_s.at[3]),
        pltpu.make_async_copy(bias_h, bias, load_s.at[4]),
    ]
    for c in loads:
        c.start()

    barrier = pltpu.get_barrier_semaphore()
    greet = zdevs + fdevs + [mate, (f, zn * 2 + other)]
    for dev in greet:
        pl.semaphore_signal(barrier, inc=1, device_id=dev, device_id_type=MESH)

    loads[0].wait()
    flat = fx.reshape(2, cells, ch)
    chunks = cells // CHUNK

    def add_up(k, acc):
        return acc + jnp.sum(flat[core, pl.ds(k * CHUNK, CHUNK), :].astype(F32), axis=0, keepdims=True)

    mean = lax.fori_loop(0, chunks, add_up, jnp.zeros((1, ch), F32)) / cells

    def add_sq(k, acc):
        d = flat[core, pl.ds(k * CHUNK, CHUNK), :].astype(F32) - mean
        return acc + jnp.sum(d * d, axis=0, keepdims=True)

    m2 = lax.fori_loop(0, chunks, add_sq, jnp.zeros((1, ch), F32))
    s0[core, 0:1, :] = mean
    s0[core, 1:2, :] = m2
    loads[1].wait()

    pl.semaphore_wait(barrier, len(greet))
    if stop == 1:
        for c in loads[2:]:
            c.wait()
        return

    def fan(buf, me, devs, k):
        for dev in devs:
            rcopy(buf.at[me], buf.at[me], sm_s.at[k], sm_r.at[k], dev).start()

    def fan_recv(buf, k, n):
        many = buf.at[pl.ds(0, n)]
        rcopy(many, many, sm_s.at[k], sm_r.at[k], mate).wait_recv()

    def fan_sent(buf, k, n):
        many = buf.at[pl.ds(0, n)]
        rcopy(many, many, sm_s.at[k], sm_r.at[k], mate).wait_send()

    fan(s0, core, [mate], 0)
    block = ext.at[0:2, own_rows]
    to_mate = rcopy(block, block, halo_s.at[0], halo_r.at[0], mate)
    feats = rcopy(fx.at[core], fx.at[core], halo_s.at[1], halo_r.at[1], mate)
    edge_src, edge_dst = ext.at[0:2, 1 + (2 * rows - 1) * core], ext.at[0:2, (2 * rows + 1) * other]
    edges = [
        rcopy(edge_src, edge_dst, halo_s.at[2 + c], halo_r.at[2 + core], (f, zn * 2 + c)) for c in range(2)
    ]
    edge_in = [
        rcopy(ext.at[0:2, 2 * rows + 1], ext.at[0:2, 2 * rows + 1], halo_s.at[2], halo_r.at[2], mate),
        rcopy(ext.at[0:2, 0], ext.at[0:2, 0], halo_s.at[3], halo_r.at[3], mate),
    ]
    for c in [feats, to_mate] + edges:
        c.start()

    def combine(buf, each):
        m = buf[:, 0, :]
        n = m.shape[0]
        avg = jnp.sum(m, axis=0, keepdims=True) / n
        d = m - avg
        return avg, jnp.sum(buf[:, 1, :], axis=0, keepdims=True) + each * jnp.sum(
            d * d, axis=0, keepdims=True
        )

    fan_recv(s0, 0, 1)
    avg, m2 = combine(s0, float(cells))
    s1[f, 0:1, :] = avg
    s1[f, 1:2, :] = m2
    fan(s1, f, fdevs, 1)

    before = (lax.rem(f - 1 + NF, NF), t)
    later = ext.at[2:4, own_rows]
    to_before = rcopy(block, later, halo_s.at[4], halo_r.at[4], before)
    to_before.start()

    for c in edge_in:
        c.wait_recv()

    @pl.when(z == 0)
    def _():
        ext[0:2, 0] = jnp.zeros((2, cols, ch), BF16)

    @pl.when(z == NZ - 1)
    def _():
        ext[0:2, 2 * rows + 1] = jnp.zeros((2, cols, ch), BF16)

    rims = [
        rcopy(ext.at[0:2, r], ext.at[2:4, r], halo_s.at[k], halo_r.at[k], before)
        for k, r in ((5, 0), (6, 2 * rows + 1))
    ]
    for c in rims:
        c.start()

    fan_recv(s1, 1, NF - 1)
    avg, m2 = combine(s1, float(cells * 2))
    s2[z, 0:1, :] = avg
    s2[z, 1:2, :] = m2
    fan(s2, z, zdevs, 2)

    to_before.wait_recv()
    relay = rcopy(later, later, halo_s.at[7], halo_r.at[7], mate)
    relay.start()
    to_mate.wait()
    feats.wait()
    for c in edges:
        c.wait_send()
    to_before.wait_send()
    for c in rims:
        c.wait()
    relay.wait()
    fan_sent(s0, 0, 1)
    fan_sent(s1, 1, NF - 1)

    @pl.when(f == NF - 1)
    def _():
        ext[2:4] = jnp.zeros((2, 2 * rows + 2, cols, ch), BF16)

    @pl.loop(0, 4 * (2 * rows + 2))
    def _(k):
        p, r = k // (2 * rows + 2), lax.rem(k, 2 * rows + 2)
        v = ext[p, r].astype(F32)
        col = lax.broadcasted_iota(jnp.int32, v.shape, 0)
        up = jnp.where(col == cols - 1, 0.0, pltpu.roll(v, cols - 1, 0))
        down = jnp.where(col == 0, 0.0, pltpu.roll(v, 1, 0))
        cotx[0, p, r] = up.astype(BF16)
        cotx[1, p, r] = ext[p, r]
        cotx[2, p, r] = down.astype(BF16)

    for c in loads[2:]:
        c.wait()
    gact[...] = jnp.zeros_like(gact)

    @pl.loop(0, 9)
    def _(k):
        a, b = k // 3, lax.rem(k, 3)
        p, r = pl.ds(2 - a, frames), pl.ds(2 - b + rows * core, rows)
        taps = jnp.concatenate([w[3 * k], w[3 * k + 1], w[3 * k + 2]], axis=1)
        patch = jnp.concatenate([cotx[e, p, r].reshape(cells, ch) for e in range(3)], axis=1)
        gact[...] += lax.dot_general(patch, taps, (((1,), (1,)), ((), ())), preferred_element_type=F32)

    fan_recv(s2, 2, NZ - 1)
    fan_sent(s2, 2, NZ - 1)
    if stop == 2:
        return
    avg, m2 = combine(s2, float(cells * 2 * NF))
    per_channel = float(cells * 2 * NF * NZ)
    group = ch // GROUPS
    g_avg = group_sum(avg) / group
    d = avg - g_avg
    spread = group_sum(m2 + per_channel * (d * d)) / (per_channel * group)
    inv = lax.rsqrt(spread + EPS)
    gw, bw = gain[...], bias[...]

    def normed(c, k):
        xh = (flat[c, pl.ds(k * CHUNK, CHUNK), :].astype(F32) - g_avg) * inv
        nrm = xh * gw + bw
        return xh, nrm, 1.0 / (1.0 + jnp.exp(-nrm))

    @pl.loop(0, 2 * chunks)
    def _(k):
        c, kk = k // chunks, lax.rem(k, chunks)
        _, nrm, s = normed(c, kk)
        act = (nrm * s).astype(BF16)
        per = chunks // frames
        to = (kk // per) * (2 * per) + c * per + lax.rem(kk, per)
        act_t[to] = act.T

    def pair(q):
        got = []
        for n in range(2):
            tap = jnp.minimum(core * (2 * HALF) + 2 * q + n, LAST)
            a, b, e = tap // 9, lax.rem(tap // 3, 3), lax.rem(tap, 3)
            got.append(
                cotx[e, pl.ds(2 - a, frames), pl.ds(2 - b, 2 * rows)].reshape(2 * cells, ch)
            )
        acts = jnp.concatenate([act_t[i] for i in range(2 * chunks)], axis=1)
        out = jnp.dot(acts, jnp.concatenate(got, axis=1), preferred_element_type=F32)
        for n in range(2):
            j = 2 * q + n
            part[j // HALF, :, :, lax.rem(j, HALF)] = out[:, n * ch : (n + 1) * ch].reshape(NX, NY, 8, ch)

    pl.loop(0, 4)(pair)
    a1 = [
        rcopy(part.at[0, xo], ra1.at[i], st_s.at[0, i], st_r.at[0, i], dev)
        for i, (xo, dev) in enumerate(zip(xs, xdevs))
    ]
    for c in a1:
        c.start()
    pl.loop(4, HALF)(pair)
    b1 = [
        rcopy(part.at[1, :, yo], rb1.at[i], st_s.at[1, i], st_r.at[1, i], dev)
        for i, (yo, dev) in enumerate(zip(ys, ydevs))
    ]
    for c in b1:
        c.start()

    def norm_grad(k, acc):
        at_rows = pl.ds(k * CHUNK, CHUNK)
        xh, nrm, s = normed(core, k)
        gn = gact[at_rows, :] * s * (1.0 + nrm * (1.0 - s))
        gact[at_rows, :] = gn
        xhat[at_rows, :] = xh
        return (
            acc[0] + jnp.sum(gn * xh, axis=0, keepdims=True),
            acc[1] + jnp.sum(gn, axis=0, keepdims=True),
        )

    zero = jnp.zeros((1, ch), F32)
    d_gain, d_shift = lax.fori_loop(0, chunks, norm_grad, (zero, zero))
    g0[core, 0:1, :] = d_gain
    g0[core, 1:2, :] = d_shift
    fan(g0, core, [mate], 3)

    def pass_on(buf, k, n, to, me, devs):
        fan_recv(buf, k, n)
        to[me, 0:1, :] = jnp.sum(buf[:, 0, :], axis=0, keepdims=True)
        to[me, 1:2, :] = jnp.sum(buf[:, 1, :], axis=0, keepdims=True)
        fan(to, me, devs, k + 1)
        fan_sent(buf, k, n)

    pass_on(g0, 3, 1, g1, f, fdevs)

    for c in a1:
        c.wait_recv()
    part[0, x] += ra1[0] + ra1[1] + ra1[2]
    a2 = [
        rcopy(part.at[0, x, yo], ra2.at[i], st_s.at[2, i], st_r.at[2, i], dev)
        for i, (yo, dev) in enumerate(zip(ys, ydevs))
    ]
    for c in a2:
        c.start()
    for c in b1:
        c.wait_recv()
    part[1, :, y] += rb1[0] + rb1[1] + rb1[2]
    b2 = [
        rcopy(part.at[1, xo, y], rb2.at[i], st_s.at[3, i], st_r.at[3, i], dev)
        for i, (xo, dev) in enumerate(zip(xs, xdevs))
    ]
    for c in b2:
        c.start()

    pass_on(g1, 4, NF - 1, g2, z, zdevs)

    def z_send(h):
        for j in range(HALF):
            q = 2 * j + h

            @pl.when(z != q)
            def _():
                rcopy(zsrc.at[h, j], rz.at[z], z_s.at[0, q], z_r.at[0], (f, q * 2 + core)).start()

    for c in a2:
        c.wait_recv()
    zsrc[0] = part[0, x, y] + (ra2[0] + ra2[1] + ra2[2])
    z_send(0)
    for c in b2:
        c.wait_recv()
    zsrc[1] = part[1, x, y] + (rb2[0] + rb2[1] + rb2[2])
    z_send(1)
    for c in a1 + b1 + a2 + b2:
        c.wait_send()

    full = gk.at[core]
    mine = full.at[:, x, y]

    @pl.when(z < 2 * HALF)
    def _():
        h, j = lax.rem(z, 2), z // 2
        rz[z] = zsrc[h, j]
        many = rz.at[pl.ds(0, NZ - 1)]
        rcopy(many, many, z_s.at[0, 0], z_r.at[0], mate).wait_recv()
        mine[h, j] = jnp.sum(rz[...], axis=0)
        for jz, dev in zip(zs, zdevs):
            rcopy(mine.at[h, j], mine.at[h, j], z_s.at[1, jz], z_r.at[1 + z], dev).start()

    fan_recv(g2, 5, NZ - 1)
    fan_sent(g2, 5, NZ - 1)
    d_gain = jnp.sum(g2[:, 0, :], axis=0, keepdims=True)
    d_shift = jnp.sum(g2[:, 1, :], axis=0, keepdims=True)
    gs[0:1, :] = d_gain
    gs[1:2, :] = d_shift
    count = per_channel * group
    g_mean = group_sum(gw * d_shift) / count
    g_proj = group_sum(gw * d_gain) / count
    out = fg.reshape(cells, ch)

    @pl.loop(0, chunks)
    def _(k):
        at_rows = pl.ds(pl.multiple_of(k * CHUNK, CHUNK), CHUNK)
        out[at_rows, :] = (
            inv * (gact[at_rows, :] * gw - g_mean - xhat[at_rows, :] * g_proj)
        ).astype(BF16)

    for h in range(2):
        for j in range(HALF):
            q = 2 * j + h

            @pl.when(z != q)
            def _():
                rcopy(zsrc.at[h, j], rz.at[z], z_s.at[0, q], z_r.at[0], (f, q * 2 + core)).wait_send()

    def z_recv(h):
        for j in range(HALF):
            q = 2 * j + h

            @pl.when(z != q)
            def _():
                rcopy(mine.at[h, j], mine.at[h, j], z_s.at[1, 0], z_r.at[1 + q], mate).wait_recv()

    def gather(here, there, k, devs):
        sends = [rcopy(here, here, ag_s.at[k, i], ag_r.at[k, i], dev) for i, dev in enumerate(devs)]
        come = [rcopy(p, p, ag_s.at[k, i], ag_r.at[k, i], mate) for i, p in enumerate(there)]
        for c in sends:
            c.start()
        return sends, come

    def behind(v, n):
        return [lax.rem(v - i + n, n) for i in range(1, n)]

    xb, yb = behind(x, NX), behind(y, NY)

    def forward(piece, h, i):
        c = rcopy(piece, piece, fw_s.at[h, i], fw_r.at[h, i], mate)
        c.start()
        return c

    z_recv(0)
    a_out, a_in = gather(full.at[0, x, y], [full.at[0, x, i] for i in yb], 0, ydevs)
    z_recv(1)
    b_out, b_in = gather(full.at[1, x, y], [full.at[1, i, y] for i in xb], 1, xdevs)
    for c in a_in:
        c.wait_recv()
    a_out2, a_in2 = gather(full.at[0, x], [full.at[0, i] for i in xb], 2, xdevs)
    fw = [forward(full.at[0, x], 0, 0)]
    for c in b_in:
        c.wait_recv()
    b_out2, b_in2 = gather(full.at[1, :, y], [full.at[1, :, i] for i in yb], 3, ydevs)
    fw.append(forward(full.at[1, :, y], 1, 0))
    for i in range(NX - 1):
        a_in2[i].wait_recv()
        fw.append(forward(full.at[0, xb[i]], 0, i + 1))
        b_in2[i].wait_recv()
        fw.append(forward(full.at[1, :, yb[i]], 1, i + 1))

    @pl.when(z < 2 * HALF)
    def _():
        h, j = lax.rem(z, 2), z // 2
        for jz, dev in zip(zs, zdevs):
            rcopy(mine.at[h, j], mine.at[h, j], z_s.at[1, jz], z_r.at[1 + z], dev).wait_send()

    for c in a_out + b_out + a_out2 + b_out2:
        c.wait_send()
    for c in fw:
        c.wait()


def call(stop, cid, features, norm_gain_weight, norm_bias, kernel, cotangent):
    frames, rows, cols, ch = features.shape
    cells = frames * rows * cols
    vm = pl.BlockSpec(memory_space=pltpu.VMEM)
    hbm = pl.BlockSpec(memory_space=pltpu.HBM)
    dma = pltpu.SemaphoreType.DMA
    tile = (8, ch)
    return pl.pallas_call(
        functools.partial(body, stop),
        out_shape=(
            jax.ShapeDtypeStruct(features.shape, BF16),
            jax.ShapeDtypeStruct((2, 2, NX, NY, HALF) + tile, F32),
            jax.ShapeDtypeStruct((2, ch), F32),
        ),
        in_specs=[hbm] * 5,
        out_specs=(vm, vm, vm),
        scratch_shapes=[
            pltpu.VMEM((2,) + features.shape, BF16),
            pltpu.VMEM((1, ch), F32),
            pltpu.VMEM((1, ch), F32),
            pltpu.VMEM((27, ch, ch), BF16),
            pltpu.VMEM((4, 2 * rows + 2, cols, ch), BF16),
            pltpu.VMEM((3, 4, 2 * rows + 2, cols, ch), BF16),
            pltpu.VMEM((cells, ch), F32),
            pltpu.VMEM((cells, ch), F32),
            pltpu.VMEM((2 * cells // CHUNK, ch, CHUNK), BF16),
            pltpu.VMEM((2, 2, ch), F32),
            pltpu.VMEM((NF, 2, ch), F32),
            pltpu.VMEM((NZ, 2, ch), F32),
            pltpu.VMEM((2, 2, ch), F32),
            pltpu.VMEM((NF, 2, ch), F32),
            pltpu.VMEM((NZ, 2, ch), F32),
            pltpu.VMEM((2, NX, NY, HALF) + tile, F32),
            pltpu.VMEM((3, NY, HALF) + tile, F32),
            pltpu.VMEM((3, NX, HALF) + tile, F32),
            pltpu.VMEM((3, HALF) + tile, F32),
            pltpu.VMEM((3, HALF) + tile, F32),
            pltpu.VMEM((2, HALF) + tile, F32),
            pltpu.VMEM((NZ,) + tile, F32),
            dma((5,)), dma((8,)), dma((8,)),
            dma((6,)), dma((6,)),
            dma((4, 3)), dma((4, 3)),
            dma((2, NZ)), dma((1 + NZ,)),
            dma((4, 3)), dma((4, 3)),
            dma((2, 4)), dma((2, 4)),
        ],
        compiler_params=pltpu.CompilerParams(
            collective_id=cid, has_side_effects=True, vmem_limit_bytes=56 * 2**20
        ),
    )(
        features,
        norm_gain_weight.reshape(1, ch),
        norm_bias.reshape(1, ch),
        kernel.reshape(27, ch, ch),
        cotangent,
    )


def on_device(features, norm_gain_weight, norm_bias, kernel, cotangent):
    ch = features.shape[-1]
    fg, gk, gs = call(0, 0, features, norm_gain_weight, norm_bias, kernel, cotangent)
    taps = jnp.transpose(gk, (0, 1, 4, 2, 3, 5, 6)).reshape(4 * HALF, ch, ch)[: LAST + 1]
    return fg, taps.reshape(3, 3, 3, ch, ch), gs[0], gs[1]


def solution(mesh):
    placed = (P("frame", "tile", None, None), P(), P(), P(), P("frame", "tile", None, None))
    return jax.shard_map(
        on_device,
        mesh=mesh,
        in_specs=placed,
        out_specs=(P("frame", "tile", None, None), P(), P(), P()),
        check_vma=False,
    )
```

```python
import functools

import jax
import jax.numpy as jnp
from jax import lax
from jax.experimental import pallas as pl
from jax.experimental.pallas import tpu as pltpu
from jax.sharding import PartitionSpec as P

MESH = pl.DeviceIdType.MESH
GROUPS = 32
EPS = 1e-06
NX = 4
NY = 4
NZ = 16
NF = NX * NY
LAST = 26
HALF = 7
F32 = jnp.float32
BF16 = jnp.bfloat16
CHUNK = 128


def group_sum(v):
    lane = lax.broadcasted_iota(jnp.int32, v.shape, 1)
    v = v + jnp.where(lane % 2 == 0, pltpu.roll(v, 127, 1), pltpu.roll(v, 1, 1))
    return v + jnp.where(lane % 4 < 2, pltpu.roll(v, 126, 1), pltpu.roll(v, 2, 1))


def rcopy(src, dst, ss, rs, dev):
    return pltpu.make_async_remote_copy(
        src_ref=src, dst_ref=dst, send_sem=ss, recv_sem=rs, device_id=dev, device_id_type=MESH
    )


def body(
    stop,
    feat_h, gain_h, bias_h, w_h, cot_h,
    fg, gk, gs,
    fx, gain, bias, w, ext, cotx, gact, xhat, feat_t, act_t,
    s0, s1, s2, g0, g1, g2,
    part, ra1, rb1, ra2, rb2, zsrc, rz,
    load_s, halo_s, halo_r, sm_s, sm_r, rs_s, rs_r1, rs_r2, z_s, z_r, ag_s, ag_r1, ag_r2, fw_s, fw_r,
):
    f, t = lax.axis_index("frame"), lax.axis_index("tile")
    y, x = f // NX, lax.rem(f, NX)
    z, core = t // 2, lax.rem(t, 2)
    other = 1 - core
    _, frames, rows, cols, ch = fx.shape
    cells = frames * rows * cols
    mate = (f, z * 2 + other)
    zn = lax.rem(z - 1 + 2 * core + NZ, NZ)
    fdevs = [(lax.rem(f + i, NF), t) for i in range(1, NF)]
    far = sorted(range(1, NZ), key=lambda i: -min(i, NZ - i))
    zs = [lax.rem(z + i, NZ) for i in far]
    zdevs = [(f, j * 2 + core) for j in zs]
    xs = [lax.rem(x + i, NX) for i in range(1, NX)]
    ys = [lax.rem(y + i, NY) for i in range(1, NY)]
    xdevs = [(y * NX + i, t) for i in xs]
    ydevs = [(i * NX + x, t) for i in ys]
    own_rows = pl.ds(1 + rows * core, rows)
    mate_rows = pl.ds(1 + rows * other, rows)

    loads = [
        pltpu.make_async_copy(feat_h, fx.at[core], load_s.at[0]),
        pltpu.make_async_copy(cot_h, ext.at[0:2, own_rows], load_s.at[1]),
        pltpu.make_async_copy(w_h, w, load_s.at[2]),
        pltpu.make_async_copy(gain_h, gain, load_s.at[3]),
        pltpu.make_async_copy(bias_h, bias, load_s.at[4]),
    ]
    for c in loads:
        c.start()

    barrier = pltpu.get_barrier_semaphore()
    greet = zdevs + fdevs + [mate, (f, zn * 2 + other)]
    for dev in greet:
        pl.semaphore_signal(barrier, inc=1, device_id=dev, device_id_type=MESH)

    loads[0].wait()
    flat = fx.reshape(2, cells, ch)
    chunks = cells // CHUNK

    def add_up(k, acc):
        return acc + jnp.sum(flat[core, pl.ds(k * CHUNK, CHUNK), :].astype(F32), axis=0, keepdims=True)

    mean = lax.fori_loop(0, chunks, add_up, jnp.zeros((1, ch), F32)) / cells

    def add_sq(k, acc):
        d = flat[core, pl.ds(k * CHUNK, CHUNK), :].astype(F32) - mean
        return acc + jnp.sum(d * d, axis=0, keepdims=True)

    m2 = lax.fori_loop(0, chunks, add_sq, jnp.zeros((1, ch), F32))
    s0[core, 0:1, :] = mean
    s0[core, 1:2, :] = m2
    loads[1].wait()

    pl.semaphore_wait(barrier, len(greet))
    if stop == 1:
        for c in loads[2:]:
            c.wait()
        return

    def fan(buf, me, devs, k):
        for dev in devs:
            rcopy(buf.at[me], buf.at[me], sm_s.at[k], sm_r.at[k], dev).start()

    def fan_recv(buf, k, n):
        many = buf.at[pl.ds(0, n)]
        rcopy(many, many, sm_s.at[k], sm_r.at[k], mate).wait_recv()

    def fan_sent(buf, k, n):
        many = buf.at[pl.ds(0, n)]
        rcopy(many, many, sm_s.at[k], sm_r.at[k], mate).wait_send()

    fan(s0, core, [mate], 0)
    block = ext.at[0:2, own_rows]
    to_mate = rcopy(block, block, halo_s.at[0], halo_r.at[0], mate)
    feats = rcopy(fx.at[core], fx.at[core], halo_s.at[1], halo_r.at[1], mate)
    edge_src, edge_dst = ext.at[0:2, 1 + (2 * rows - 1) * core], ext.at[0:2, (2 * rows + 1) * other]
    edges = [
        rcopy(edge_src, edge_dst, halo_s.at[2 + c], halo_r.at[2 + core], (f, zn * 2 + c)) for c in range(2)
    ]
    edge_in = [
        rcopy(ext.at[0:2, 2 * rows + 1], ext.at[0:2, 2 * rows + 1], halo_s.at[2], halo_r.at[2], mate),
        rcopy(ext.at[0:2, 0], ext.at[0:2, 0], halo_s.at[3], halo_r.at[3], mate),
    ]
    for c in [feats, to_mate] + edges:
        c.start()

    def combine(buf, each):
        m = buf[:, 0, :]
        n = m.shape[0]
        avg = jnp.sum(m, axis=0, keepdims=True) / n
        d = m - avg
        return avg, jnp.sum(buf[:, 1, :], axis=0, keepdims=True) + each * jnp.sum(
            d * d, axis=0, keepdims=True
        )

    fan_recv(s0, 0, 1)
    avg, m2 = combine(s0, float(cells))
    s1[f, 0:1, :] = avg
    s1[f, 1:2, :] = m2
    fan(s1, f, fdevs, 1)

    before = (lax.rem(f - 1 + NF, NF), t)
    later = ext.at[2:4, own_rows]
    to_before = rcopy(block, later, halo_s.at[4], halo_r.at[4], before)
    to_before.start()

    for c in edge_in:
        c.wait_recv()

    @pl.when(z == 0)
    def _():
        ext[0:2, 0] = jnp.zeros((2, cols, ch), BF16)

    @pl.when(z == NZ - 1)
    def _():
        ext[0:2, 2 * rows + 1] = jnp.zeros((2, cols, ch), BF16)

    rims = [
        rcopy(ext.at[0:2, r], ext.at[2:4, r], halo_s.at[k], halo_r.at[k], before)
        for k, r in ((5, 0), (6, 2 * rows + 1))
    ]
    for c in rims:
        c.start()

    fan_recv(s1, 1, NF - 1)
    avg, m2 = combine(s1, float(cells * 2))
    s2[z, 0:1, :] = avg
    s2[z, 1:2, :] = m2
    fan(s2, z, zdevs, 2)

    to_before.wait_recv()
    relay = rcopy(later, later, halo_s.at[7], halo_r.at[7], mate)
    relay.start()
    to_mate.wait()
    feats.wait()
    for c in edges:
        c.wait_send()
    to_before.wait_send()
    for c in rims:
        c.wait()
    relay.wait()
    fan_sent(s0, 0, 1)
    fan_sent(s1, 1, NF - 1)

    @pl.when(f == NF - 1)
    def _():
        ext[2:4] = jnp.zeros((2, 2 * rows + 2, cols, ch), BF16)

    @pl.loop(0, 4 * (2 * rows + 2))
    def _(k):
        p, r = k // (2 * rows + 2), lax.rem(k, 2 * rows + 2)
        v = ext[p, r].astype(F32)
        col = lax.broadcasted_iota(jnp.int32, v.shape, 0)
        up = jnp.where(col == cols - 1, 0.0, pltpu.roll(v, cols - 1, 0))
        down = jnp.where(col == 0, 0.0, pltpu.roll(v, 1, 0))
        cotx[0, p, r] = up.astype(BF16)
        cotx[1, p, r] = ext[p, r]
        cotx[2, p, r] = down.astype(BF16)

    @pl.loop(0, 2 * chunks)
    def _(k):
        c, kk = k // chunks, lax.rem(k, chunks)
        per = chunks // frames
        to = (kk // per) * (2 * per) + c * per + lax.rem(kk, per)
        feat_t[to] = flat[c, pl.ds(kk * CHUNK, CHUNK), :].T

    for c in loads[2:]:
        c.wait()
    gact[...] = jnp.zeros_like(gact)

    @pl.loop(0, 9)
    def _(k):
        a, b = k // 3, lax.rem(k, 3)
        p, r = pl.ds(2 - a, frames), pl.ds(2 - b + rows * core, rows)
        taps = jnp.concatenate([w[3 * k], w[3 * k + 1], w[3 * k + 2]], axis=1)
        patch = jnp.concatenate([cotx[e, p, r].reshape(cells, ch) for e in range(3)], axis=1)
        gact[...] += lax.dot_general(patch, taps, (((1,), (1,)), ((), ())), preferred_element_type=F32)

    fan_recv(s2, 2, NZ - 1)
    fan_sent(s2, 2, NZ - 1)
    if stop == 2:
        return
    avg, m2 = combine(s2, float(cells * 2 * NF))
    per_channel = float(cells * 2 * NF * NZ)
    group = ch // GROUPS
    g_avg = group_sum(avg) / group
    d = avg - g_avg
    spread = group_sum(m2 + per_channel * (d * d)) / (per_channel * group)
    inv = lax.rsqrt(spread + EPS)
    gw, bw = gain[...], bias[...]

    def normed(c, k):
        xh = (flat[c, pl.ds(k * CHUNK, CHUNK), :].astype(F32) - g_avg) * inv
        nrm = xh * gw + bw
        return xh, nrm, 1.0 / (1.0 + jnp.exp(-nrm))

    def down(v):
        return jnp.broadcast_to(v, (CHUNK, ch)).T

    avg_t, scale_t, bias_t = down(g_avg), down(inv * gw), down(bw)

    @pl.loop(0, 2 * chunks)
    def _(k):
        nrm = (feat_t[k].astype(F32) - avg_t) * scale_t + bias_t
        act_t[k] = (nrm * (1.0 / (1.0 + jnp.exp(-nrm)))).astype(BF16)

    def pair(q):
        got = []
        for n in range(2):
            tap = jnp.minimum(core * (2 * HALF) + 2 * q + n, LAST)
            a, b, e = tap // 9, lax.rem(tap // 3, 3), lax.rem(tap, 3)
            got.append(
                cotx[e, pl.ds(2 - a, frames), pl.ds(2 - b, 2 * rows)].reshape(2 * cells, ch)
            )
        acts = jnp.concatenate([act_t[i] for i in range(2 * chunks)], axis=1)
        out = jnp.dot(acts, jnp.concatenate(got, axis=1), preferred_element_type=F32)
        for n in range(2):
            j = 2 * q + n
            part[j // HALF, :, :, lax.rem(j, HALF)] = out[:, n * ch : (n + 1) * ch].reshape(NX, NY, 8, ch)

    pl.loop(0, 4)(pair)
    def pieces_out(h, order, take, devs, into):
        for p, o in enumerate(order):
            for i, (to, dev) in enumerate(devs):
                rcopy(take(to, o), into.at[p, i], rs_s.at[0], rs_r1.at[h, p], dev).start()

    pieces_out(0, ys + [y], lambda to, o: part.at[0, to, o], list(zip(xs, xdevs)), ra1)
    pl.loop(4, HALF)(pair)
    pieces_out(1, xs + [x], lambda to, o: part.at[1, o, to], list(zip(ys, ydevs)), rb1)

    def norm_grad(k, acc):
        at_rows = pl.ds(k * CHUNK, CHUNK)
        xh, nrm, s = normed(core, k)
        gn = gact[at_rows, :] * s * (1.0 + nrm * (1.0 - s))
        gact[at_rows, :] = gn
        xhat[at_rows, :] = xh
        return (
            acc[0] + jnp.sum(gn * xh, axis=0, keepdims=True),
            acc[1] + jnp.sum(gn, axis=0, keepdims=True),
        )

    zero = jnp.zeros((1, ch), F32)
    d_gain, d_shift = lax.fori_loop(0, chunks, norm_grad, (zero, zero))
    g0[core, 0:1, :] = d_gain
    g0[core, 1:2, :] = d_shift
    fan(g0, core, [mate], 3)

    def pass_on(buf, k, n, to, me, devs):
        fan_recv(buf, k, n)
        to[me, 0:1, :] = jnp.sum(buf[:, 0, :], axis=0, keepdims=True)
        to[me, 1:2, :] = jnp.sum(buf[:, 1, :], axis=0, keepdims=True)
        fan(to, me, devs, k + 1)
        fan_sent(buf, k, n)

    pass_on(g0, 3, 1, g1, f, fdevs)

    for p in range(NX):
        yo, xo = (ys + [y])[p], (xs + [x])[p]
        rcopy(ra1.at[p], ra1.at[p], rs_s.at[0], rs_r1.at[0, p], mate).wait_recv()
        part[0, x, yo] += ra1[p, 0] + ra1[p, 1] + ra1[p, 2]
        if p < NX - 1:
            rcopy(part.at[0, x, yo], ra2.at[p], rs_s.at[0], rs_r2.at[0], ydevs[p]).start()
        rcopy(rb1.at[p], rb1.at[p], rs_s.at[0], rs_r1.at[1, p], mate).wait_recv()
        part[1, xo, y] += rb1[p, 0] + rb1[p, 1] + rb1[p, 2]
        if p < NX - 1:
            rcopy(part.at[1, xo, y], rb2.at[p], rs_s.at[0], rs_r2.at[1], xdevs[p]).start()

    def z_send(h):
        for j in range(HALF):
            q = 2 * j + h

            @pl.when(z != q)
            def _():
                rcopy(zsrc.at[h, j], rz.at[z], z_s.at[0], z_r.at[0], (f, q * 2 + core)).start()

    rcopy(ra2, ra2, rs_s.at[0], rs_r2.at[0], mate).wait_recv()
    zsrc[0] = part[0, x, y] + (ra2[0] + ra2[1] + ra2[2])
    z_send(0)
    rcopy(rb2, rb2, rs_s.at[0], rs_r2.at[1], mate).wait_recv()
    zsrc[1] = part[1, x, y] + (rb2[0] + rb2[1] + rb2[2])
    z_send(1)

    pass_on(g1, 4, NF - 1, g2, z, zdevs)
    sent = part.reshape(2 * NX * NY, HALF, 8, ch).at[pl.ds(0, 30)]
    rcopy(sent, sent, rs_s.at[0], rs_r2.at[0], mate).wait_send()

    full = gk.at[core]
    mine = full.at[:, x, y]

    def tiles(n):
        return rz.at[pl.ds(0, n)]

    @pl.when(z < 2 * HALF)
    def _():
        h, j = lax.rem(z, 2), z // 2
        rz[z] = zsrc[h, j]
        rcopy(tiles(NZ - 1), tiles(NZ - 1), z_s.at[0], z_r.at[0], mate).wait_recv()
        mine[h, j] = jnp.sum(rz[...], axis=0)
        for dev in zdevs:
            rcopy(mine.at[h, j], mine.at[h, j], z_s.at[1], z_r.at[1 + h], dev).start()

    fan_recv(g2, 5, NZ - 1)
    fan_sent(g2, 5, NZ - 1)
    d_gain = jnp.sum(g2[:, 0, :], axis=0, keepdims=True)
    d_shift = jnp.sum(g2[:, 1, :], axis=0, keepdims=True)
    gs[0:1, :] = d_gain
    gs[1:2, :] = d_shift
    count = per_channel * group
    g_mean = group_sum(gw * d_shift) / count
    g_proj = group_sum(gw * d_gain) / count
    out = fg.reshape(cells, ch)

    @pl.loop(0, chunks)
    def _(k):
        at_rows = pl.ds(pl.multiple_of(k * CHUNK, CHUNK), CHUNK)
        out[at_rows, :] = (
            inv * (gact[at_rows, :] * gw - g_mean - xhat[at_rows, :] * g_proj)
        ).astype(BF16)

    def z_recv(h):
        own = jnp.logical_and(z < 2 * HALF, lax.rem(z, 2) == h)

        @pl.when(own)
        def _():
            rcopy(tiles(HALF - 1), tiles(HALF - 1), z_s.at[1], z_r.at[1 + h], mate).wait_recv()

        @pl.when(jnp.logical_not(own))
        def _():
            rcopy(tiles(HALF), tiles(HALF), z_s.at[1], z_r.at[1 + h], mate).wait_recv()

    def behind(v, n):
        return [lax.rem(v - i + n, n) for i in range(1, n)]

    xb, yb = behind(x, NX), behind(y, NY)

    def put(piece, sem, dev):
        rcopy(piece, piece, ag_s.at[0], sem, dev).start()

    def come(piece, sem):
        rcopy(piece, piece, ag_s.at[0], sem, mate).wait_recv()

    def forward(piece):
        rcopy(piece, piece, fw_s.at[0], fw_r.at[0], mate).start()

    places = [[(x, yy) for yy in [y] + yb], [(xx, y) for xx in [x] + xb]]
    first_devs, second_devs = [ydevs, xdevs], [xdevs, ydevs]
    for p in range(NX):
        for h in range(2):
            piece = full.at[h, places[h][p][0], places[h][p][1]]
            if p == 0:
                z_recv(h)
                for i, dev in enumerate(first_devs[h]):
                    put(piece, ag_r1.at[h, i], dev)
            else:
                come(piece, ag_r1.at[h, p - 1])
            for i, dev in enumerate(second_devs[h]):
                put(piece, ag_r2.at[h, p, i], dev)
            forward(piece)
    for p in range(NX):
        for i in range(NX - 1):
            for h in range(2):
                px, py = places[h][p]
                piece = full.at[0, xb[i], py] if h == 0 else full.at[1, px, yb[i]]
                come(piece, ag_r2.at[h, p, i])
                forward(piece)

    @pl.when(z < 2 * HALF)
    def _():
        rcopy(tiles(NZ - 1), tiles(NZ - 1), z_s.at[1], z_r.at[0], mate).wait_send()
        rcopy(tiles(2 * HALF - 1), tiles(2 * HALF - 1), z_s.at[0], z_r.at[0], mate).wait_send()

    @pl.when(z >= 2 * HALF)
    def _():
        rcopy(tiles(2 * HALF), tiles(2 * HALF), z_s.at[0], z_r.at[0], mate).wait_send()

    rcopy(sent, sent, ag_s.at[0], ag_r1.at[0, 0], mate).wait_send()
    rcopy(full, full, fw_s.at[0], fw_r.at[0], mate).wait_send()
    rcopy(gk.at[other], gk.at[other], fw_s.at[0], fw_r.at[0], mate).wait_recv()


def place(fg, gk, gs, fg_o, gk_o, gain_o, shift_o, sem):
    copies = [
        pltpu.make_async_copy(fg, fg_o, sem.at[0]),
        pltpu.make_async_copy(gs.at[0:1], gain_o, sem.at[1]),
        pltpu.make_async_copy(gs.at[1:2], shift_o, sem.at[2]),
    ]
    for tap in range(LAST + 1):
        core, h, j = tap // (2 * HALF), tap // HALF % 2, tap % HALF
        pltpu.make_async_copy(gk.at[core, h, :, :, j], gk_o.at[tap], sem.at[3]).start()
    for c in copies:
        c.start()
    for c in copies:
        c.wait()
    pltpu.make_async_copy(gk_o, gk_o, sem.at[3]).wait()


def call(stop, cid, features, norm_gain_weight, norm_bias, kernel, cotangent):
    frames, rows, cols, ch = features.shape
    cells = frames * rows * cols
    vm = pl.BlockSpec(memory_space=pltpu.VMEM)
    hbm = pl.BlockSpec(memory_space=pltpu.HBM)
    dma = pltpu.SemaphoreType.DMA
    tile = (8, ch)
    return pl.pallas_call(
        functools.partial(body, stop),
        out_shape=(
            jax.ShapeDtypeStruct(features.shape, BF16),
            jax.ShapeDtypeStruct((2, 2, NX, NY, HALF) + tile, F32),
            jax.ShapeDtypeStruct((2, ch), F32),
        ),
        in_specs=[hbm] * 5,
        out_specs=(vm, vm, vm),
        scratch_shapes=[
            pltpu.VMEM((2,) + features.shape, BF16),
            pltpu.VMEM((1, ch), F32),
            pltpu.VMEM((1, ch), F32),
            pltpu.VMEM((27, ch, ch), BF16),
            pltpu.VMEM((4, 2 * rows + 2, cols, ch), BF16),
            pltpu.VMEM((3, 4, 2 * rows + 2, cols, ch), BF16),
            pltpu.VMEM((cells, ch), F32),
            pltpu.VMEM((cells, ch), F32),
            pltpu.VMEM((2 * cells // CHUNK, ch, CHUNK), BF16),
            pltpu.VMEM((2 * cells // CHUNK, ch, CHUNK), BF16),
            pltpu.VMEM((2, 2, ch), F32),
            pltpu.VMEM((NF, 2, ch), F32),
            pltpu.VMEM((NZ, 2, ch), F32),
            pltpu.VMEM((2, 2, ch), F32),
            pltpu.VMEM((NF, 2, ch), F32),
            pltpu.VMEM((NZ, 2, ch), F32),
            pltpu.VMEM((2, NX, NY, HALF) + tile, F32),
            pltpu.VMEM((NY, 3, HALF) + tile, F32),
            pltpu.VMEM((NX, 3, HALF) + tile, F32),
            pltpu.VMEM((3, HALF) + tile, F32),
            pltpu.VMEM((3, HALF) + tile, F32),
            pltpu.VMEM((2, HALF) + tile, F32),
            pltpu.VMEM((NZ,) + tile, F32),
            dma((5,)), dma((8,)), dma((8,)),
            dma((6,)), dma((6,)),
            dma((1,)), dma((2, NX)), dma((2,)),
            dma((2,)), dma((3,)),
            dma((1,)), dma((2, 3)), dma((2, NX, 3)),
            dma((1,)), dma((1,)),
        ],
        compiler_params=pltpu.CompilerParams(
            collective_id=cid, has_side_effects=True, vmem_limit_bytes=24 * 2**20
        ),
    )(
        *(
            pltpu.with_memory_space_constraint(v, pltpu.HBM)
            for v in (
                features,
                norm_gain_weight.reshape(1, ch),
                norm_bias.reshape(1, ch),
                kernel.reshape(27, ch, ch),
                cotangent,
            )
        )
    )


def on_device(features, norm_gain_weight, norm_bias, kernel, cotangent):
    ch = features.shape[-1]
    made = call(0, 0, features, norm_gain_weight, norm_bias, kernel, cotangent)
    vm = pl.BlockSpec(memory_space=pltpu.VMEM)
    hbm = pl.BlockSpec(memory_space=pltpu.HBM)
    fg, taps, gain, shift = pl.pallas_call(
        place,
        out_shape=(
            jax.ShapeDtypeStruct(features.shape, BF16),
            jax.ShapeDtypeStruct((LAST + 1, NX, NY, 8, ch), F32),
            jax.ShapeDtypeStruct((1, ch), F32),
            jax.ShapeDtypeStruct((1, ch), F32),
        ),
        in_specs=[vm] * 3,
        out_specs=(hbm,) * 4,
        scratch_shapes=[pltpu.SemaphoreType.DMA((4,))],
    )(*made)
    return fg, taps.reshape(3, 3, 3, ch, ch), gain.reshape(ch), shift.reshape(ch)


def solution(mesh):
    placed = (P("frame", "tile", None, None), P(), P(), P(), P("frame", "tile", None, None))
    return jax.shard_map(
        on_device,
        mesh=mesh,
        in_specs=placed,
        out_specs=(P("frame", "tile", None, None), P(), P(), P()),
        check_vma=False,
    )
```

```python
import functools

import jax
import jax.numpy as jnp
from jax import lax
from jax.experimental import pallas as pl
from jax.experimental.pallas import tpu as pltpu
from jax.sharding import PartitionSpec as P

MESH = pl.DeviceIdType.MESH
GROUPS = 32
EPS = 1e-06
NX = 4
NY = 4
NZ = 16
NF = NX * NY
LAST = 26
HALF = 7
F32 = jnp.float32
BF16 = jnp.bfloat16
CHUNK = 128


def group_sum(v):
    lane = lax.broadcasted_iota(jnp.int32, v.shape, 1)
    v = v + jnp.where(lane % 2 == 0, pltpu.roll(v, 127, 1), pltpu.roll(v, 1, 1))
    return v + jnp.where(lane % 4 < 2, pltpu.roll(v, 126, 1), pltpu.roll(v, 2, 1))


def rcopy(src, dst, ss, rs, dev):
    return pltpu.make_async_remote_copy(
        src_ref=src, dst_ref=dst, send_sem=ss, recv_sem=rs, device_id=dev, device_id_type=MESH
    )


def body(
    stop,
    feat_h, gain_h, bias_h, w_h, cot_h,
    fg, gk, gs,
    fx, gain, bias, w, ext, cotx, gact, xhat, feat_t, act_t,
    s0, s1, s2, g0, g1, g2,
    part, ra1, rb1, ra2, rb2, zsrc, rz,
    load_s, halo_s, halo_r, sm_s, sm_r, rs_s, rs_r1, rs_r2, z_s, z_r, ag_s, ag_r1, ag_r2, fw_s, fw_r,
):
    f, t = lax.axis_index("frame"), lax.axis_index("tile")
    y, x = f // NX, lax.rem(f, NX)
    z, core = t // 2, lax.rem(t, 2)
    other = 1 - core
    _, frames, rows, cols, ch = fx.shape
    cells = frames * rows * cols
    mate = (f, z * 2 + other)
    zn = lax.rem(z - 1 + 2 * core + NZ, NZ)
    fdevs = [(lax.rem(f + i, NF), t) for i in range(1, NF)]
    far = sorted(range(1, NZ), key=lambda i: -min(i, NZ - i))
    zs = [lax.rem(z + i, NZ) for i in far]
    zdevs = [(f, j * 2 + core) for j in zs]
    xs = [lax.rem(x + i, NX) for i in range(1, NX)]
    ys = [lax.rem(y + i, NY) for i in range(1, NY)]
    xdevs = [(y * NX + i, t) for i in xs]
    ydevs = [(i * NX + x, t) for i in ys]
    own_rows = pl.ds(1 + rows * core, rows)
    mate_rows = pl.ds(1 + rows * other, rows)

    loads = [
        pltpu.make_async_copy(feat_h, fx.at[core], load_s.at[0]),
        pltpu.make_async_copy(cot_h, ext.at[0:2, own_rows], load_s.at[1]),
        pltpu.make_async_copy(w_h, w, load_s.at[2]),
        pltpu.make_async_copy(gain_h, gain, load_s.at[3]),
        pltpu.make_async_copy(bias_h, bias, load_s.at[4]),
    ]
    for c in loads:
        c.start()

    barrier = pltpu.get_barrier_semaphore()
    greet = zdevs + fdevs + [mate, (f, zn * 2 + other)]
    for dev in greet:
        pl.semaphore_signal(barrier, inc=1, device_id=dev, device_id_type=MESH)

    loads[0].wait()
    flat = fx.reshape(2, cells, ch)
    chunks = cells // CHUNK

    def add_up(k, acc):
        return acc + jnp.sum(flat[core, pl.ds(k * CHUNK, CHUNK), :].astype(F32), axis=0, keepdims=True)

    mean = lax.fori_loop(0, chunks, add_up, jnp.zeros((1, ch), F32)) / cells

    def add_sq(k, acc):
        d = flat[core, pl.ds(k * CHUNK, CHUNK), :].astype(F32) - mean
        return acc + jnp.sum(d * d, axis=0, keepdims=True)

    m2 = lax.fori_loop(0, chunks, add_sq, jnp.zeros((1, ch), F32))
    s0[core, 0:1, :] = mean
    s0[core, 1:2, :] = m2
    loads[1].wait()

    pl.semaphore_wait(barrier, len(greet))
    if stop == 1:
        for c in loads[2:]:
            c.wait()
        return

    def fan(buf, me, devs, k):
        for dev in devs:
            rcopy(buf.at[me], buf.at[me], sm_s.at[k], sm_r.at[k], dev).start()

    def fan_recv(buf, k, n):
        many = buf.at[pl.ds(0, n)]
        rcopy(many, many, sm_s.at[k], sm_r.at[k], mate).wait_recv()

    def fan_sent(buf, k, n):
        many = buf.at[pl.ds(0, n)]
        rcopy(many, many, sm_s.at[k], sm_r.at[k], mate).wait_send()

    fan(s0, core, [mate], 0)
    block = ext.at[0:2, own_rows]
    to_mate = rcopy(block, block, halo_s.at[0], halo_r.at[0], mate)
    feats = rcopy(fx.at[core], fx.at[core], halo_s.at[1], halo_r.at[1], mate)
    edge_src, edge_dst = ext.at[0:2, 1 + (2 * rows - 1) * core], ext.at[0:2, (2 * rows + 1) * other]
    edges = [
        rcopy(edge_src, edge_dst, halo_s.at[2 + c], halo_r.at[2 + core], (f, zn * 2 + c)) for c in range(2)
    ]
    edge_in = [
        rcopy(ext.at[0:2, 2 * rows + 1], ext.at[0:2, 2 * rows + 1], halo_s.at[2], halo_r.at[2], mate),
        rcopy(ext.at[0:2, 0], ext.at[0:2, 0], halo_s.at[3], halo_r.at[3], mate),
    ]
    for c in [feats, to_mate] + edges:
        c.start()

    def combine(buf, each):
        m = buf[:, 0, :]
        n = m.shape[0]
        avg = jnp.sum(m, axis=0, keepdims=True) / n
        d = m - avg
        return avg, jnp.sum(buf[:, 1, :], axis=0, keepdims=True) + each * jnp.sum(
            d * d, axis=0, keepdims=True
        )

    fan_recv(s0, 0, 1)
    avg, m2 = combine(s0, float(cells))
    s1[f, 0:1, :] = avg
    s1[f, 1:2, :] = m2
    fan(s1, f, fdevs, 1)

    before = (lax.rem(f - 1 + NF, NF), t)
    later = ext.at[2:4, own_rows]
    to_before = rcopy(block, later, halo_s.at[4], halo_r.at[4], before)
    to_before.start()

    for c in edge_in:
        c.wait_recv()

    @pl.when(z == 0)
    def _():
        ext[0:2, 0] = jnp.zeros((2, cols, ch), BF16)

    @pl.when(z == NZ - 1)
    def _():
        ext[0:2, 2 * rows + 1] = jnp.zeros((2, cols, ch), BF16)

    rims = [
        rcopy(ext.at[0:2, r], ext.at[2:4, r], halo_s.at[k], halo_r.at[k], before)
        for k, r in ((5, 0), (6, 2 * rows + 1))
    ]
    for c in rims:
        c.start()

    fan_recv(s1, 1, NF - 1)
    avg, m2 = combine(s1, float(cells * 2))
    s2[z, 0:1, :] = avg
    s2[z, 1:2, :] = m2
    fan(s2, z, zdevs, 2)

    to_before.wait_recv()
    relay = rcopy(later, later, halo_s.at[7], halo_r.at[7], mate)
    relay.start()
    to_mate.wait()
    feats.wait()
    for c in edges:
        c.wait_send()
    to_before.wait_send()
    for c in rims:
        c.wait()
    relay.wait()
    fan_sent(s0, 0, 1)
    fan_sent(s1, 1, NF - 1)

    @pl.when(f == NF - 1)
    def _():
        ext[2:4] = jnp.zeros((2, 2 * rows + 2, cols, ch), BF16)

    @pl.loop(0, 4 * (2 * rows + 2))
    def _(k):
        p, r = k // (2 * rows + 2), lax.rem(k, 2 * rows + 2)
        v = ext[p, r].astype(F32)
        col = lax.broadcasted_iota(jnp.int32, v.shape, 0)
        up = jnp.where(col == cols - 1, 0.0, pltpu.roll(v, cols - 1, 0))
        down = jnp.where(col == 0, 0.0, pltpu.roll(v, 1, 0))
        cotx[0, p, r] = up.astype(BF16)
        cotx[1, p, r] = ext[p, r]
        cotx[2, p, r] = down.astype(BF16)

    @pl.loop(0, 2 * chunks)
    def _(k):
        c, kk = k // chunks, lax.rem(k, chunks)
        per = chunks // frames
        to = (kk // per) * (2 * per) + c * per + lax.rem(kk, per)
        feat_t[to] = flat[c, pl.ds(kk * CHUNK, CHUNK), :].T

    for c in loads[2:]:
        c.wait()
    gact[...] = jnp.zeros_like(gact)

    @pl.loop(0, 9)
    def _(k):
        a, b = k // 3, lax.rem(k, 3)
        p, r = pl.ds(2 - a, frames), pl.ds(2 - b + rows * core, rows)
        taps = jnp.concatenate([w[3 * k], w[3 * k + 1], w[3 * k + 2]], axis=1)
        patch = jnp.concatenate([cotx[e, p, r].reshape(cells, ch) for e in range(3)], axis=1)
        gact[...] += lax.dot_general(patch, taps, (((1,), (1,)), ((), ())), preferred_element_type=F32)

    fan_recv(s2, 2, NZ - 1)
    fan_sent(s2, 2, NZ - 1)
    if stop == 2:
        return
    avg, m2 = combine(s2, float(cells * 2 * NF))
    per_channel = float(cells * 2 * NF * NZ)
    group = ch // GROUPS
    g_avg = group_sum(avg) / group
    d = avg - g_avg
    spread = group_sum(m2 + per_channel * (d * d)) / (per_channel * group)
    inv = lax.rsqrt(spread + EPS)
    gw, bw = gain[...], bias[...]

    def normed(c, k):
        xh = (flat[c, pl.ds(k * CHUNK, CHUNK), :].astype(F32) - g_avg) * inv
        nrm = xh * gw + bw
        return xh, nrm, 1.0 / (1.0 + jnp.exp(-nrm))

    def down(v):
        return jnp.broadcast_to(v, (CHUNK, ch)).T

    avg_t, scale_t, bias_t = down(g_avg), down(inv * gw), down(bw)

    @pl.loop(0, 2 * chunks)
    def _(k):
        nrm = (feat_t[k].astype(F32) - avg_t) * scale_t + bias_t
        act_t[k] = (nrm * (1.0 / (1.0 + jnp.exp(-nrm)))).astype(BF16)

    def pair(q):
        got = []
        for n in range(2):
            tap = jnp.minimum(core * (2 * HALF) + 2 * q + n, LAST)
            a, b, e = tap // 9, lax.rem(tap // 3, 3), lax.rem(tap, 3)
            got.append(
                cotx[e, pl.ds(2 - a, frames), pl.ds(2 - b, 2 * rows)].reshape(2 * cells, ch)
            )
        acts = jnp.concatenate([act_t[i] for i in range(2 * chunks)], axis=1)
        out = jnp.dot(acts, jnp.concatenate(got, axis=1), preferred_element_type=F32)
        for n in range(2):
            j = 2 * q + n
            part[j // HALF, :, :, lax.rem(j, HALF)] = out[:, n * ch : (n + 1) * ch].reshape(NX, NY, 8, ch)

    pl.loop(0, 4)(pair)
    def pieces_out(h, order, take, devs, into):
        for p, o in enumerate(order):
            for i, (to, dev) in enumerate(devs):
                rcopy(take(to, o), into.at[p, i], rs_s.at[0], rs_r1.at[h, p], dev).start()

    pieces_out(0, ys + [y], lambda to, o: part.at[0, to, o], list(zip(xs, xdevs)), ra1)
    pl.loop(4, HALF)(pair)
    pieces_out(1, xs + [x], lambda to, o: part.at[1, o, to], list(zip(ys, ydevs)), rb1)

    def norm_grad(k, acc):
        at_rows = pl.ds(k * CHUNK, CHUNK)
        xh, nrm, s = normed(core, k)
        gn = gact[at_rows, :] * s * (1.0 + nrm * (1.0 - s))
        gact[at_rows, :] = gn
        xhat[at_rows, :] = xh
        return (
            acc[0] + jnp.sum(gn * xh, axis=0, keepdims=True),
            acc[1] + jnp.sum(gn, axis=0, keepdims=True),
        )

    zero = jnp.zeros((1, ch), F32)
    d_gain, d_shift = lax.fori_loop(0, chunks, norm_grad, (zero, zero))
    g0[core, 0:1, :] = d_gain
    g0[core, 1:2, :] = d_shift
    fan(g0, core, [mate], 3)

    def pass_on(buf, k, n, to, me, devs):
        fan_recv(buf, k, n)
        to[me, 0:1, :] = jnp.sum(buf[:, 0, :], axis=0, keepdims=True)
        to[me, 1:2, :] = jnp.sum(buf[:, 1, :], axis=0, keepdims=True)
        fan(to, me, devs, k + 1)
        fan_sent(buf, k, n)

    pass_on(g0, 3, 1, g1, f, fdevs)

    for p in range(NX):
        yo, xo = (ys + [y])[p], (xs + [x])[p]
        rcopy(ra1.at[p], ra1.at[p], rs_s.at[0], rs_r1.at[0, p], mate).wait_recv()
        part[0, x, yo] += ra1[p, 0] + ra1[p, 1] + ra1[p, 2]
        if p < NX - 1:
            rcopy(part.at[0, x, yo], ra2.at[p], rs_s.at[0], rs_r2.at[0], ydevs[p]).start()
        rcopy(rb1.at[p], rb1.at[p], rs_s.at[0], rs_r1.at[1, p], mate).wait_recv()
        part[1, xo, y] += rb1[p, 0] + rb1[p, 1] + rb1[p, 2]
        if p < NX - 1:
            rcopy(part.at[1, xo, y], rb2.at[p], rs_s.at[0], rs_r2.at[1], xdevs[p]).start()

    def z_send(h):
        for j in range(HALF):
            q = 2 * j + h

            @pl.when(z != q)
            def _():
                rcopy(zsrc.at[h, j], rz.at[z], z_s.at[0], z_r.at[0], (f, q * 2 + core)).start()

    rcopy(ra2, ra2, rs_s.at[0], rs_r2.at[0], mate).wait_recv()
    zsrc[0] = part[0, x, y] + (ra2[0] + ra2[1] + ra2[2])
    z_send(0)
    rcopy(rb2, rb2, rs_s.at[0], rs_r2.at[1], mate).wait_recv()
    zsrc[1] = part[1, x, y] + (rb2[0] + rb2[1] + rb2[2])
    z_send(1)

    pass_on(g1, 4, NF - 1, g2, z, zdevs)
    sent = part.reshape(2 * NX * NY, HALF, 8, ch).at[pl.ds(0, 30)]
    rcopy(sent, sent, rs_s.at[0], rs_r2.at[0], mate).wait_send()

    share = 2 * HALF * core

    def out_piece(h, px, py):
        return gk.at[pl.ds(share + h * HALF, HALF), px, py]

    def tiles(n):
        return rz.at[pl.ds(0, n)]

    @pl.when(z < 2 * HALF)
    def _():
        h, j = lax.rem(z, 2), z // 2
        rz[z] = zsrc[h, j]
        rcopy(tiles(NZ - 1), tiles(NZ - 1), z_s.at[0], z_r.at[0], mate).wait_recv()
        tile = gk.at[share + h * HALF + j, x, y]
        tile[...] = jnp.sum(rz[...], axis=0)
        for dev in zdevs:
            rcopy(tile, tile, z_s.at[1], z_r.at[1 + h], dev).start()

    fan_recv(g2, 5, NZ - 1)
    fan_sent(g2, 5, NZ - 1)
    d_gain = jnp.sum(g2[:, 0, :], axis=0, keepdims=True)
    d_shift = jnp.sum(g2[:, 1, :], axis=0, keepdims=True)
    gs[0:1, :] = d_gain
    gs[1:2, :] = d_shift
    count = per_channel * group
    g_mean = group_sum(gw * d_shift) / count
    g_proj = group_sum(gw * d_gain) / count
    out = fg.reshape(cells, ch)

    @pl.loop(0, chunks)
    def _(k):
        at_rows = pl.ds(pl.multiple_of(k * CHUNK, CHUNK), CHUNK)
        out[at_rows, :] = (
            inv * (gact[at_rows, :] * gw - g_mean - xhat[at_rows, :] * g_proj)
        ).astype(BF16)

    def z_recv(h):
        own = jnp.logical_and(z < 2 * HALF, lax.rem(z, 2) == h)

        @pl.when(own)
        def _():
            rcopy(tiles(HALF - 1), tiles(HALF - 1), z_s.at[1], z_r.at[1 + h], mate).wait_recv()

        @pl.when(jnp.logical_not(own))
        def _():
            rcopy(tiles(HALF), tiles(HALF), z_s.at[1], z_r.at[1 + h], mate).wait_recv()

    def behind(v, n):
        return [lax.rem(v - i + n, n) for i in range(1, n)]

    xb, yb = behind(x, NX), behind(y, NY)

    def put(piece, sem, dev):
        rcopy(piece, piece, ag_s.at[0], sem, dev).start()

    def come(piece, sem):
        rcopy(piece, piece, ag_s.at[0], sem, mate).wait_recv()

    def forward(piece):
        rcopy(piece, piece, fw_s.at[0], fw_r.at[0], mate).start()

    places = [[(x, yy) for yy in [y] + yb], [(xx, y) for xx in [x] + xb]]
    first_devs, second_devs = [ydevs, xdevs], [xdevs, ydevs]
    for p in range(NX):
        for h in range(2):
            piece = out_piece(h, *places[h][p])
            if p == 0:
                z_recv(h)
                for i, dev in enumerate(first_devs[h]):
                    put(piece, ag_r1.at[h, i], dev)
            else:
                come(piece, ag_r1.at[h, p - 1])
            for i, dev in enumerate(second_devs[h]):
                put(piece, ag_r2.at[h, p, i], dev)
            forward(piece)
    for p in range(NX):
        for i in range(NX - 1):
            for h in range(2):
                px, py = places[h][p]
                piece = out_piece(0, xb[i], py) if h == 0 else out_piece(1, px, yb[i])
                come(piece, ag_r2.at[h, p, i])
                forward(piece)

    @pl.when(z < 2 * HALF)
    def _():
        rcopy(tiles(NZ - 1), tiles(NZ - 1), z_s.at[1], z_r.at[0], mate).wait_send()
        rcopy(tiles(2 * HALF - 1), tiles(2 * HALF - 1), z_s.at[0], z_r.at[0], mate).wait_send()

    @pl.when(z >= 2 * HALF)
    def _():
        rcopy(tiles(2 * HALF), tiles(2 * HALF), z_s.at[0], z_r.at[0], mate).wait_send()

    rcopy(sent, sent, ag_s.at[0], ag_r1.at[0, 0], mate).wait_send()
    full = gk.at[pl.ds(share, 2 * HALF)]
    rcopy(full, full, fw_s.at[0], fw_r.at[0], mate).wait()


def place(fg, gk, gs, fg_o, gk_o, gain_o, shift_o, sem):
    copies = [
        pltpu.make_async_copy(gk.at[pl.ds(0, LAST + 1)], gk_o, sem.at[0]),
        pltpu.make_async_copy(fg, fg_o, sem.at[1]),
        pltpu.make_async_copy(gs.at[0:1], gain_o, sem.at[2]),
        pltpu.make_async_copy(gs.at[1:2], shift_o, sem.at[3]),
    ]
    for c in copies:
        c.start()
    for c in copies:
        c.wait()


def call(stop, cid, features, norm_gain_weight, norm_bias, kernel, cotangent):
    frames, rows, cols, ch = features.shape
    cells = frames * rows * cols
    vm = pl.BlockSpec(memory_space=pltpu.VMEM)
    hbm = pl.BlockSpec(memory_space=pltpu.HBM)
    dma = pltpu.SemaphoreType.DMA
    tile = (8, ch)
    return pl.pallas_call(
        functools.partial(body, stop),
        out_shape=(
            pltpu.VMEM(features.shape, BF16),
            pltpu.VMEM((4 * HALF, NX, NY) + tile, F32),
            pltpu.VMEM((2, ch), F32),
        ),
        in_specs=[hbm] * 5,
        out_specs=(vm, vm, vm),
        scratch_shapes=[
            pltpu.VMEM((2,) + features.shape, BF16),
            pltpu.VMEM((1, ch), F32),
            pltpu.VMEM((1, ch), F32),
            pltpu.VMEM((27, ch, ch), BF16),
            pltpu.VMEM((4, 2 * rows + 2, cols, ch), BF16),
            pltpu.VMEM((3, 4, 2 * rows + 2, cols, ch), BF16),
            pltpu.VMEM((cells, ch), F32),
            pltpu.VMEM((cells, ch), F32),
            pltpu.VMEM((2 * cells // CHUNK, ch, CHUNK), BF16),
            pltpu.VMEM((2 * cells // CHUNK, ch, CHUNK), BF16),
            pltpu.VMEM((2, 2, ch), F32),
            pltpu.VMEM((NF, 2, ch), F32),
            pltpu.VMEM((NZ, 2, ch), F32),
            pltpu.VMEM((2, 2, ch), F32),
            pltpu.VMEM((NF, 2, ch), F32),
            pltpu.VMEM((NZ, 2, ch), F32),
            pltpu.VMEM((2, NX, NY, HALF) + tile, F32),
            pltpu.VMEM((NY, 3, HALF) + tile, F32),
            pltpu.VMEM((NX, 3, HALF) + tile, F32),
            pltpu.VMEM((3, HALF) + tile, F32),
            pltpu.VMEM((3, HALF) + tile, F32),
            pltpu.VMEM((2, HALF) + tile, F32),
            pltpu.VMEM((NZ,) + tile, F32),
            dma((5,)), dma((8,)), dma((8,)),
            dma((6,)), dma((6,)),
            dma((1,)), dma((2, NX)), dma((2,)),
            dma((2,)), dma((3,)),
            dma((1,)), dma((2, 3)), dma((2, NX, 3)),
            dma((1,)), dma((1,)),
        ],
        compiler_params=pltpu.CompilerParams(
            collective_id=cid, has_side_effects=True, vmem_limit_bytes=24 * 2**20
        ),
    )(
        *(
            pltpu.with_memory_space_constraint(v, pltpu.HBM)
            for v in (
                features,
                norm_gain_weight.reshape(1, ch),
                norm_bias.reshape(1, ch),
                kernel.reshape(27, ch, ch),
                cotangent,
            )
        )
    )


def on_device(features, norm_gain_weight, norm_bias, kernel, cotangent):
    ch = features.shape[-1]
    made = call(0, 0, features, norm_gain_weight, norm_bias, kernel, cotangent)
    vm = pl.BlockSpec(memory_space=pltpu.VMEM)
    hbm = pl.BlockSpec(memory_space=pltpu.HBM)
    fg, taps, gain, shift = pl.pallas_call(
        place,
        out_shape=(
            jax.ShapeDtypeStruct(features.shape, BF16),
            jax.ShapeDtypeStruct((LAST + 1, NX, NY, 8, ch), F32),
            jax.ShapeDtypeStruct((1, ch), F32),
            jax.ShapeDtypeStruct((1, ch), F32),
        ),
        in_specs=[vm] * 3,
        out_specs=(hbm,) * 4,
        scratch_shapes=[pltpu.SemaphoreType.DMA((4,))],
        compiler_params=pltpu.CompilerParams(vmem_limit_bytes=4 * 2**20),
    )(*(pltpu.with_memory_space_constraint(v, pltpu.VMEM) for v in made))
    return fg, taps.reshape(3, 3, 3, ch, ch), gain.reshape(ch), shift.reshape(ch)


def solution(mesh):
    placed = (P("frame", "tile", None, None), P(), P(), P(), P("frame", "tile", None, None))
    return jax.shard_map(
        on_device,
        mesh=mesh,
        in_specs=placed,
        out_specs=(P("frame", "tile", None, None), P(), P(), P()),
        check_vma=False,
    )
```

```python
import functools

import jax
import jax.numpy as jnp
from jax import lax
from jax.experimental import pallas as pl
from jax.experimental.pallas import tpu as pltpu
from jax.sharding import PartitionSpec as P

MESH = pl.DeviceIdType.MESH
GROUPS = 32
EPS = 1e-06
NX = 4
NY = 4
NZ = 16
NF = NX * NY
LAST = 26
HALF = 7
F32 = jnp.float32
BF16 = jnp.bfloat16
CHUNK = 128
REACH = NZ // 4


def group_sum(v):
    lane = lax.broadcasted_iota(jnp.int32, v.shape, 1)
    v = v + jnp.where(lane % 2 == 0, pltpu.roll(v, 127, 1), pltpu.roll(v, 1, 1))
    return v + jnp.where(lane % 4 < 2, pltpu.roll(v, 126, 1), pltpu.roll(v, 2, 1))


def rcopy(src, dst, ss, rs, dev):
    return pltpu.make_async_remote_copy(
        src_ref=src, dst_ref=dst, send_sem=ss, recv_sem=rs, device_id=dev, device_id_type=MESH
    )


def body(
    stop,
    feat_h, gain_h, bias_h, w_h, cot_h,
    fg, gk, gs,
    fx, gain, bias, w, ext, cotx, gact, xhat, feat_t, act_t,
    s1, s2, g0, g1, g2,
    part, ra1, rb1, ra2, rb2, zsrc, rz,
    load_s, halo_s, halo_r, sm_s, sm_r, rs_s, rs_r1, rs_r2, z_s, z_r, ag_s, ag_r1, ag_r2, fw_s, fw_r, known,
):
    f, t = lax.axis_index("frame"), lax.axis_index("tile")
    y, x = f // NX, lax.rem(f, NX)
    z, core = t // 2, lax.rem(t, 2)
    other = 1 - core
    _, frames, rows, cols, ch = fx.shape
    cells = frames * rows * cols
    mate = (f, z * 2 + other)
    zn = lax.rem(z - 1 + 2 * core + NZ, NZ)
    fdevs = [(lax.rem(f + i, NF), t) for i in range(1, NF)]
    fboth = [mate] + [(dev[0], z * 2 + c) for dev in fdevs for c in (core, other)]
    far = sorted(range(1, NZ), key=lambda i: -min(i, NZ - i))
    zs = [lax.rem(z + i, NZ) for i in far]
    zdevs = [(f, j * 2 + core) for j in zs]
    xs = [lax.rem(x + i, NX) for i in range(1, NX)]
    ys = [lax.rem(y + i, NY) for i in range(1, NY)]
    xdevs = [(y * NX + i, t) for i in xs]
    ydevs = [(i * NX + x, t) for i in ys]
    own_rows = pl.ds(1 + rows * core, rows)
    mate_rows = pl.ds(1 + rows * other, rows)

    loads = [
        pltpu.make_async_copy(feat_h, fx.at[core], load_s.at[0]),
        pltpu.make_async_copy(cot_h, ext.at[0:2, own_rows], load_s.at[1]),
        pltpu.make_async_copy(w_h, w, load_s.at[2]),
        pltpu.make_async_copy(gain_h, gain, load_s.at[3]),
        pltpu.make_async_copy(bias_h, bias, load_s.at[4]),
    ]
    for c in loads:
        c.start()

    barrier = pltpu.get_barrier_semaphore()
    near = [dev for i, dev in zip(far, zdevs) if min(i, NZ - i) <= REACH]
    edge = [dev for i, dev in zip(far, zdevs) if min(i, NZ - i) == REACH]
    greet = near + fboth + [(f, zn * 2 + other)]
    for dev in greet:
        pl.semaphore_signal(barrier, inc=1, device_id=dev, device_id_type=MESH)

    loads[0].wait()
    flat = fx.reshape(2, cells, ch)
    chunks = cells // CHUNK

    def add_up(k, acc):
        return acc + jnp.sum(flat[core, pl.ds(k * CHUNK, CHUNK), :].astype(F32), axis=0, keepdims=True)

    mean = lax.fori_loop(0, chunks, add_up, jnp.zeros((1, ch), F32)) / cells

    def add_sq(k, acc):
        d = flat[core, pl.ds(k * CHUNK, CHUNK), :].astype(F32) - mean
        return acc + jnp.sum(d * d, axis=0, keepdims=True)

    m2 = lax.fori_loop(0, chunks, add_sq, jnp.zeros((1, ch), F32))
    s1[core, f, 0:1, :] = mean
    s1[core, f, 1:2, :] = m2
    loads[1].wait()

    pl.semaphore_wait(barrier, len(greet))
    if stop == 1:
        for c in loads[2:]:
            c.wait()
        return

    def fan(buf, me, devs, k):
        for dev in devs:
            rcopy(buf.at[me], buf.at[me], sm_s.at[k], sm_r.at[k], dev).start()

    def fan_recv(buf, k, n):
        many = buf.at[pl.ds(0, n)]
        rcopy(many, many, sm_s.at[k], sm_r.at[k], mate).wait_recv()

    def fan_sent(buf, k, n):
        many = buf.at[pl.ds(0, n)]
        rcopy(many, many, sm_s.at[k], sm_r.at[k], mate).wait_send()

    for dev in fboth:
        rcopy(s1.at[core, f], s1.at[core, f], sm_s.at[1], sm_r.at[1], dev).start()
    for dev in edge:
        pl.semaphore_signal(known, inc=1, device_id=dev, device_id_type=MESH)
    block = ext.at[0:2, own_rows]
    to_mate = rcopy(block, block, halo_s.at[0], halo_r.at[0], mate)
    feats = rcopy(fx.at[core], fx.at[core], halo_s.at[1], halo_r.at[1], mate)
    edge_src, edge_dst = ext.at[0:2, 1 + (2 * rows - 1) * core], ext.at[0:2, (2 * rows + 1) * other]
    edges = [
        rcopy(edge_src, edge_dst, halo_s.at[2 + c], halo_r.at[2 + core], (f, zn * 2 + c)) for c in range(2)
    ]
    edge_in = [
        rcopy(ext.at[0:2, 2 * rows + 1], ext.at[0:2, 2 * rows + 1], halo_s.at[2], halo_r.at[2], mate),
        rcopy(ext.at[0:2, 0], ext.at[0:2, 0], halo_s.at[3], halo_r.at[3], mate),
    ]
    for c in [feats, to_mate] + edges:
        c.start()

    def combine(buf, each):
        m = buf[:, 0, :]
        n = m.shape[0]
        avg = jnp.sum(m, axis=0, keepdims=True) / n
        d = m - avg
        return avg, jnp.sum(buf[:, 1, :], axis=0, keepdims=True) + each * jnp.sum(
            d * d, axis=0, keepdims=True
        )

    before = (lax.rem(f - 1 + NF, NF), t)
    later = ext.at[2:4, own_rows]
    to_before = rcopy(block, later, halo_s.at[4], halo_r.at[4], before)
    to_before.start()

    for c in edge_in:
        c.wait_recv()

    @pl.when(z == 0)
    def _():
        ext[0:2, 0] = jnp.zeros((2, cols, ch), BF16)

    @pl.when(z == NZ - 1)
    def _():
        ext[0:2, 2 * rows + 1] = jnp.zeros((2, cols, ch), BF16)

    rims = [
        rcopy(ext.at[0:2, r], ext.at[2:4, r], halo_s.at[k], halo_r.at[k], before)
        for k, r in ((5, 0), (6, 2 * rows + 1))
    ]
    for c in rims:
        c.start()

    s1 = s1.reshape(2 * NF, 2, ch)
    fan_recv(s1, 1, 2 * NF - 1)
    avg, m2 = combine(s1, float(cells))
    s2[z, 0:1, :] = avg
    s2[z, 1:2, :] = m2
    pl.semaphore_wait(known, len(edge))
    fan(s2, z, zdevs, 2)

    to_before.wait_recv()
    relay = rcopy(later, later, halo_s.at[7], halo_r.at[7], mate)
    relay.start()
    feats.wait()

    @pl.loop(0, 2 * chunks)
    def _(k):
        c, kk = k // chunks, lax.rem(k, chunks)
        per = chunks // frames
        to = (kk // per) * (2 * per) + c * per + lax.rem(kk, per)
        feat_t[to] = flat[c, pl.ds(kk * CHUNK, CHUNK), :].T

    to_mate.wait()
    for c in edges:
        c.wait_send()
    to_before.wait_send()
    for c in rims:
        c.wait()
    relay.wait()
    fan_sent(s1, 1, 2 * NF - 1)

    @pl.when(f == NF - 1)
    def _():
        ext[2:4] = jnp.zeros((2, 2 * rows + 2, cols, ch), BF16)

    @pl.loop(0, 4 * (2 * rows + 2))
    def _(k):
        p, r = k // (2 * rows + 2), lax.rem(k, 2 * rows + 2)
        v = ext[p, r].astype(F32)
        col = lax.broadcasted_iota(jnp.int32, v.shape, 0)
        up = jnp.where(col == cols - 1, 0.0, pltpu.roll(v, cols - 1, 0))
        down = jnp.where(col == 0, 0.0, pltpu.roll(v, 1, 0))
        cotx[0, p, r] = up.astype(BF16)
        cotx[1, p, r] = ext[p, r]
        cotx[2, p, r] = down.astype(BF16)

    fan_recv(s2, 2, NZ - 1)
    fan_sent(s2, 2, NZ - 1)
    for c in loads[2:]:
        c.wait()
    if stop == 2:
        return
    avg, m2 = combine(s2, float(cells * 2 * NF))
    per_channel = float(cells * 2 * NF * NZ)
    group = ch // GROUPS
    g_avg = group_sum(avg) / group
    d = avg - g_avg
    spread = group_sum(m2 + per_channel * (d * d)) / (per_channel * group)
    inv = lax.rsqrt(spread + EPS)
    gw, bw = gain[...], bias[...]

    def normed(c, k):
        xh = (flat[c, pl.ds(k * CHUNK, CHUNK), :].astype(F32) - g_avg) * inv
        nrm = xh * gw + bw
        return xh, nrm, 1.0 / (1.0 + jnp.exp(-nrm))

    def down(v):
        return jnp.broadcast_to(v, (CHUNK, ch)).T

    avg_t, scale_t, bias_t = down(g_avg), down(inv * gw), down(bw)

    @pl.loop(0, 2 * chunks)
    def _(k):
        nrm = (feat_t[k].astype(F32) - avg_t) * scale_t + bias_t
        act_t[k] = (nrm * (1.0 / (1.0 + jnp.exp(-nrm)))).astype(BF16)

    def pair(q):
        got = []
        for n in range(2):
            tap = jnp.minimum(core * (2 * HALF) + 2 * q + n, LAST)
            a, b, e = tap // 9, lax.rem(tap // 3, 3), lax.rem(tap, 3)
            got.append(
                cotx[e, pl.ds(2 - a, frames), pl.ds(2 - b, 2 * rows)].reshape(2 * cells, ch)
            )
        acts = jnp.concatenate([act_t[i] for i in range(2 * chunks)], axis=1)
        out = jnp.dot(acts, jnp.concatenate(got, axis=1), preferred_element_type=F32)
        for n in range(2):
            j = 2 * q + n
            part[j // HALF, :, :, lax.rem(j, HALF)] = out[:, n * ch : (n + 1) * ch].reshape(NX, NY, 8, ch)

    pl.loop(0, 4)(pair)
    def pieces_out(h, order, take, devs, into):
        for p, o in enumerate(order):
            for i, (to, dev) in enumerate(devs):
                rcopy(take(to, o), into.at[p, i], rs_s.at[0], rs_r1.at[h, p], dev).start()

    pieces_out(0, ys + [y], lambda to, o: part.at[0, to, o], list(zip(xs, xdevs)), ra1)
    pl.loop(4, HALF)(pair)
    pieces_out(1, xs + [x], lambda to, o: part.at[1, o, to], list(zip(ys, ydevs)), rb1)

    gact[...] = jnp.zeros_like(gact)

    @pl.loop(0, 9)
    def _(k):
        a, b = k // 3, lax.rem(k, 3)
        p, r = pl.ds(2 - a, frames), pl.ds(2 - b + rows * core, rows)
        taps = jnp.concatenate([w[3 * k], w[3 * k + 1], w[3 * k + 2]], axis=1)
        patch = jnp.concatenate([cotx[e, p, r].reshape(cells, ch) for e in range(3)], axis=1)
        gact[...] += lax.dot_general(patch, taps, (((1,), (1,)), ((), ())), preferred_element_type=F32)

    def norm_grad(k, acc):
        at_rows = pl.ds(k * CHUNK, CHUNK)
        xh, nrm, s = normed(core, k)
        gn = gact[at_rows, :] * s * (1.0 + nrm * (1.0 - s))
        gact[at_rows, :] = gn
        xhat[at_rows, :] = xh
        return (
            acc[0] + jnp.sum(gn * xh, axis=0, keepdims=True),
            acc[1] + jnp.sum(gn, axis=0, keepdims=True),
        )

    zero = jnp.zeros((1, ch), F32)
    d_gain, d_shift = lax.fori_loop(0, chunks, norm_grad, (zero, zero))
    g0[core, 0:1, :] = d_gain
    g0[core, 1:2, :] = d_shift
    fan(g0, core, [mate], 3)

    def pass_on(buf, k, n, to, me, devs):
        fan_recv(buf, k, n)
        to[me, 0:1, :] = jnp.sum(buf[:, 0, :], axis=0, keepdims=True)
        to[me, 1:2, :] = jnp.sum(buf[:, 1, :], axis=0, keepdims=True)
        fan(to, me, devs, k + 1)
        fan_sent(buf, k, n)

    pass_on(g0, 3, 1, g1, f, fdevs)

    for p in range(NX):
        yo, xo = (ys + [y])[p], (xs + [x])[p]
        rcopy(ra1.at[p], ra1.at[p], rs_s.at[0], rs_r1.at[0, p], mate).wait_recv()
        part[0, x, yo] += ra1[p, 0] + ra1[p, 1] + ra1[p, 2]
        if p < NX - 1:
            rcopy(part.at[0, x, yo], ra2.at[p], rs_s.at[0], rs_r2.at[0], ydevs[p]).start()
        rcopy(rb1.at[p], rb1.at[p], rs_s.at[0], rs_r1.at[1, p], mate).wait_recv()
        part[1, xo, y] += rb1[p, 0] + rb1[p, 1] + rb1[p, 2]
        if p < NX - 1:
            rcopy(part.at[1, xo, y], rb2.at[p], rs_s.at[0], rs_r2.at[1], xdevs[p]).start()

    def z_send(h):
        for j in range(HALF):
            q = 2 * j + h

            @pl.when(z != q)
            def _():
                rcopy(zsrc.at[h, j], rz.at[z], z_s.at[0], z_r.at[0], (f, q * 2 + core)).start()

    rcopy(ra2, ra2, rs_s.at[0], rs_r2.at[0], mate).wait_recv()
    zsrc[0] = part[0, x, y] + (ra2[0] + ra2[1] + ra2[2])
    z_send(0)
    rcopy(rb2, rb2, rs_s.at[0], rs_r2.at[1], mate).wait_recv()
    zsrc[1] = part[1, x, y] + (rb2[0] + rb2[1] + rb2[2])
    z_send(1)

    pass_on(g1, 4, NF - 1, g2, z, zdevs)
    sent = part.reshape(2 * NX * NY, HALF, 8, ch).at[pl.ds(0, 30)]
    rcopy(sent, sent, rs_s.at[0], rs_r2.at[0], mate).wait_send()

    share = 2 * HALF * core

    def out_piece(h, px, py):
        return gk.at[pl.ds(share + h * HALF, HALF), px, py]

    def tiles(n):
        return rz.at[pl.ds(0, n)]

    @pl.when(z < 2 * HALF)
    def _():
        h, j = lax.rem(z, 2), z // 2
        rz[z] = zsrc[h, j]
        rcopy(tiles(NZ - 1), tiles(NZ - 1), z_s.at[0], z_r.at[0], mate).wait_recv()
        tile = gk.at[share + h * HALF + j, x, y]
        tile[...] = jnp.sum(rz[...], axis=0)
        for dev in zdevs:
            rcopy(tile, tile, z_s.at[1], z_r.at[1 + h], dev).start()

    fan_recv(g2, 5, NZ - 1)
    fan_sent(g2, 5, NZ - 1)
    d_gain = jnp.sum(g2[:, 0, :], axis=0, keepdims=True)
    d_shift = jnp.sum(g2[:, 1, :], axis=0, keepdims=True)
    gs[0:1, :] = d_gain
    gs[1:2, :] = d_shift
    count = per_channel * group
    g_mean = group_sum(gw * d_shift) / count
    g_proj = group_sum(gw * d_gain) / count
    out = fg.reshape(cells, ch)

    @pl.loop(0, chunks)
    def _(k):
        at_rows = pl.ds(pl.multiple_of(k * CHUNK, CHUNK), CHUNK)
        out[at_rows, :] = (
            inv * (gact[at_rows, :] * gw - g_mean - xhat[at_rows, :] * g_proj)
        ).astype(BF16)

    def z_recv(h):
        own = jnp.logical_and(z < 2 * HALF, lax.rem(z, 2) == h)

        @pl.when(own)
        def _():
            rcopy(tiles(HALF - 1), tiles(HALF - 1), z_s.at[1], z_r.at[1 + h], mate).wait_recv()

        @pl.when(jnp.logical_not(own))
        def _():
            rcopy(tiles(HALF), tiles(HALF), z_s.at[1], z_r.at[1 + h], mate).wait_recv()

    def behind(v, n):
        return [lax.rem(v - i + n, n) for i in range(1, n)]

    xb, yb = behind(x, NX), behind(y, NY)

    def put(piece, sem, dev):
        rcopy(piece, piece, ag_s.at[0], sem, dev).start()

    def come(piece, sem):
        rcopy(piece, piece, ag_s.at[0], sem, mate).wait_recv()

    def forward(piece):
        rcopy(piece, piece, fw_s.at[0], fw_r.at[0], mate).start()

    places = [[(x, yy) for yy in [y] + yb], [(xx, y) for xx in [x] + xb]]
    first_devs, second_devs = [ydevs, xdevs], [xdevs, ydevs]
    for p in range(NX):
        for h in range(2):
            piece = out_piece(h, *places[h][p])
            if p == 0:
                z_recv(h)
                for i, dev in enumerate(first_devs[h]):
                    put(piece, ag_r1.at[h, i], dev)
            else:
                come(piece, ag_r1.at[h, p - 1])
            for i, dev in enumerate(second_devs[h]):
                put(piece, ag_r2.at[h, p, i], dev)
            forward(piece)
    for p in range(NX):
        for i in range(NX - 1):
            for h in range(2):
                px, py = places[h][p]
                piece = out_piece(0, xb[i], py) if h == 0 else out_piece(1, px, yb[i])
                come(piece, ag_r2.at[h, p, i])
                forward(piece)

    @pl.when(z < 2 * HALF)
    def _():
        rcopy(tiles(NZ - 1), tiles(NZ - 1), z_s.at[1], z_r.at[0], mate).wait_send()
        rcopy(tiles(2 * HALF - 1), tiles(2 * HALF - 1), z_s.at[0], z_r.at[0], mate).wait_send()

    @pl.when(z >= 2 * HALF)
    def _():
        rcopy(tiles(2 * HALF), tiles(2 * HALF), z_s.at[0], z_r.at[0], mate).wait_send()

    rcopy(sent, sent, ag_s.at[0], ag_r1.at[0, 0], mate).wait_send()
    full = gk.at[pl.ds(share, 2 * HALF)]
    rcopy(full, full, fw_s.at[0], fw_r.at[0], mate).wait()


def place(fg, gk, gs, fg_o, gk_o, gain_o, shift_o, sem):
    copies = [
        pltpu.make_async_copy(gk.at[pl.ds(0, LAST + 1)], gk_o, sem.at[0]),
        pltpu.make_async_copy(fg, fg_o, sem.at[1]),
        pltpu.make_async_copy(gs.at[0:1], gain_o, sem.at[2]),
        pltpu.make_async_copy(gs.at[1:2], shift_o, sem.at[3]),
    ]
    for c in copies:
        c.start()
    for c in copies:
        c.wait()


def call(stop, cid, features, norm_gain_weight, norm_bias, kernel, cotangent):
    frames, rows, cols, ch = features.shape
    cells = frames * rows * cols
    vm = pl.BlockSpec(memory_space=pltpu.VMEM)
    hbm = pl.BlockSpec(memory_space=pltpu.HBM)
    dma = pltpu.SemaphoreType.DMA
    tile = (8, ch)
    return pl.pallas_call(
        functools.partial(body, stop),
        out_shape=(
            pltpu.VMEM(features.shape, BF16),
            pltpu.VMEM((4 * HALF, NX, NY) + tile, F32),
            pltpu.VMEM((2, ch), F32),
        ),
        in_specs=[hbm] * 5,
        out_specs=(vm, vm, vm),
        scratch_shapes=[
            pltpu.VMEM((2,) + features.shape, BF16),
            pltpu.VMEM((1, ch), F32),
            pltpu.VMEM((1, ch), F32),
            pltpu.VMEM((27, ch, ch), BF16),
            pltpu.VMEM((4, 2 * rows + 2, cols, ch), BF16),
            pltpu.VMEM((3, 4, 2 * rows + 2, cols, ch), BF16),
            pltpu.VMEM((cells, ch), F32),
            pltpu.VMEM((cells, ch), F32),
            pltpu.VMEM((2 * cells // CHUNK, ch, CHUNK), BF16),
            pltpu.VMEM((2 * cells // CHUNK, ch, CHUNK), BF16),
            pltpu.VMEM((2, NF, 2, ch), F32),
            pltpu.VMEM((NZ, 2, ch), F32),
            pltpu.VMEM((2, 2, ch), F32),
            pltpu.VMEM((NF, 2, ch), F32),
            pltpu.VMEM((NZ, 2, ch), F32),
            pltpu.VMEM((2, NX, NY, HALF) + tile, F32),
            pltpu.VMEM((NY, 3, HALF) + tile, F32),
            pltpu.VMEM((NX, 3, HALF) + tile, F32),
            pltpu.VMEM((3, HALF) + tile, F32),
            pltpu.VMEM((3, HALF) + tile, F32),
            pltpu.VMEM((2, HALF) + tile, F32),
            pltpu.VMEM((NZ,) + tile, F32),
            dma((5,)), dma((8,)), dma((8,)),
            dma((6,)), dma((6,)),
            dma((1,)), dma((2, NX)), dma((2,)),
            dma((2,)), dma((3,)),
            dma((1,)), dma((2, 3)), dma((2, NX, 3)),
            dma((1,)), dma((1,)),
            pltpu.SemaphoreType.REGULAR,
        ],
        compiler_params=pltpu.CompilerParams(
            collective_id=cid, has_side_effects=True, vmem_limit_bytes=24 * 2**20
        ),
    )(
        *(
            pltpu.with_memory_space_constraint(v, pltpu.HBM)
            for v in (
                features,
                norm_gain_weight.reshape(1, ch),
                norm_bias.reshape(1, ch),
                kernel.reshape(27, ch, ch),
                cotangent,
            )
        )
    )


def on_device(features, norm_gain_weight, norm_bias, kernel, cotangent):
    ch = features.shape[-1]
    made = call(0, 0, features, norm_gain_weight, norm_bias, kernel, cotangent)
    vm = pl.BlockSpec(memory_space=pltpu.VMEM)
    hbm = pl.BlockSpec(memory_space=pltpu.HBM)
    fg, taps, gain, shift = pl.pallas_call(
        place,
        out_shape=(
            jax.ShapeDtypeStruct(features.shape, BF16),
            jax.ShapeDtypeStruct((LAST + 1, NX, NY, 8, ch), F32),
            jax.ShapeDtypeStruct((1, ch), F32),
            jax.ShapeDtypeStruct((1, ch), F32),
        ),
        in_specs=[vm] * 3,
        out_specs=(hbm,) * 4,
        scratch_shapes=[pltpu.SemaphoreType.DMA((4,))],
        compiler_params=pltpu.CompilerParams(vmem_limit_bytes=4 * 2**20),
    )(*(pltpu.with_memory_space_constraint(v, pltpu.VMEM) for v in made))
    return fg, taps.reshape(3, 3, 3, ch, ch), gain.reshape(ch), shift.reshape(ch)


def solution(mesh):
    placed = (P("frame", "tile", None, None), P(), P(), P(), P("frame", "tile", None, None))
    return jax.shard_map(
        on_device,
        mesh=mesh,
        in_specs=placed,
        out_specs=(P("frame", "tile", None, None), P(), P(), P()),
        check_vma=False,
    )
```

```python
import functools

import jax
import jax.numpy as jnp
from jax import lax
from jax.experimental import pallas as pl
from jax.experimental.pallas import tpu as pltpu
from jax.sharding import PartitionSpec as P

MESH = pl.DeviceIdType.MESH
GROUPS = 32
EPS = 1e-06
NX = 4
NY = 4
NZ = 16
NF = NX * NY
LAST = 26
HALF = 7
F32 = jnp.float32
BF16 = jnp.bfloat16
CHUNK = 128
FIRST = NZ // 2 + 1
REACH = NZ // 4


def group_sum(v):
    lane = lax.broadcasted_iota(jnp.int32, v.shape, 1)
    v = v + jnp.where(lane % 2 == 0, pltpu.roll(v, 127, 1), pltpu.roll(v, 1, 1))
    return v + jnp.where(lane % 4 < 2, pltpu.roll(v, 126, 1), pltpu.roll(v, 2, 1))


def rcopy(src, dst, ss, rs, dev):
    return pltpu.make_async_remote_copy(
        src_ref=src, dst_ref=dst, send_sem=ss, recv_sem=rs, device_id=dev, device_id_type=MESH
    )


def body(
    stop,
    feat_h, gain_h, bias_h, w_h, cot_h,
    fg, gk, gs,
    fx, gain, bias, w, ext, cotx, gact, xhat, feat_t, act_t,
    s1, s2, g0, g1, g2,
    part, ra1, rb1, ra2, rb2, zsrc, rz,
    load_s, halo_s, halo_r, sm_s, sm_r, rs_s, rs_r1, rs_r2, z_s, z_r, ag_s, ag_r1, ag_r2, fw_s, fw_r, known,
):
    f, t = lax.axis_index("frame"), lax.axis_index("tile")
    y, x = f // NX, lax.rem(f, NX)
    z, core = t // 2, lax.rem(t, 2)
    other = 1 - core
    _, frames, rows, cols, ch = fx.shape
    cells = frames * rows * cols
    mate = (f, z * 2 + other)
    zn = lax.rem(z - 1 + 2 * core + NZ, NZ)
    fdevs = [(lax.rem(f + i, NF), t) for i in range(1, NF)]
    fboth = [mate] + [(dev[0], z * 2 + c) for dev in fdevs for c in (core, other)]
    far = sorted(range(1, NZ), key=lambda i: -min(i, NZ - i))
    zs = [lax.rem(z + i, NZ) for i in far]
    zdevs = [(f, j * 2 + core) for j in zs]
    xs = [lax.rem(x + i, NX) for i in range(1, NX)]
    ys = [lax.rem(y + i, NY) for i in range(1, NY)]
    xdevs = [(y * NX + i, t) for i in xs]
    ydevs = [(i * NX + x, t) for i in ys]
    own_rows = pl.ds(1 + rows * core, rows)
    mate_rows = pl.ds(1 + rows * other, rows)

    loads = [
        pltpu.make_async_copy(feat_h, fx.at[core], load_s.at[0]),
        pltpu.make_async_copy(cot_h, ext.at[0:2, own_rows], load_s.at[1]),
        pltpu.make_async_copy(w_h, w, load_s.at[2]),
        pltpu.make_async_copy(gain_h, gain, load_s.at[3]),
        pltpu.make_async_copy(bias_h, bias, load_s.at[4]),
    ]
    for c in loads:
        c.start()

    barrier = pltpu.get_barrier_semaphore()
    near = [dev for i, dev in zip(far, zdevs) if min(i, NZ - i) <= REACH]
    edge = [dev for i, dev in zip(far, zdevs) if min(i, NZ - i) == REACH]
    greet = near + fboth + [(f, zn * 2 + other)]
    for dev in greet:
        pl.semaphore_signal(barrier, inc=1, device_id=dev, device_id_type=MESH)

    loads[0].wait()
    flat = fx.reshape(2, cells, ch)
    chunks = cells // CHUNK

    def add_up(k, acc):
        return acc + jnp.sum(flat[core, pl.ds(k * CHUNK, CHUNK), :].astype(F32), axis=0, keepdims=True)

    mean = lax.fori_loop(0, chunks, add_up, jnp.zeros((1, ch), F32)) / cells

    def add_sq(k, acc):
        d = flat[core, pl.ds(k * CHUNK, CHUNK), :].astype(F32) - mean
        return acc + jnp.sum(d * d, axis=0, keepdims=True)

    m2 = lax.fori_loop(0, chunks, add_sq, jnp.zeros((1, ch), F32))
    s1[core, f, 0:1, :] = mean
    s1[core, f, 1:2, :] = m2
    loads[1].wait()

    pl.semaphore_wait(barrier, len(greet))
    if stop == 1:
        for c in loads[2:]:
            c.wait()
        return

    def fan(buf, me, devs, k):
        for dev in devs:
            rcopy(buf.at[me], buf.at[me], sm_s.at[k], sm_r.at[k], dev).start()

    def fan_recv(buf, k, n):
        many = buf.at[pl.ds(0, n)]
        rcopy(many, many, sm_s.at[k], sm_r.at[k], mate).wait_recv()

    def fan_sent(buf, k, n):
        many = buf.at[pl.ds(0, n)]
        rcopy(many, many, sm_s.at[k], sm_r.at[k], mate).wait_send()

    for dev in fboth:
        rcopy(s1.at[core, f], s1.at[core, f], sm_s.at[1], sm_r.at[1], dev).start()
    for dev in edge:
        pl.semaphore_signal(known, inc=1, device_id=dev, device_id_type=MESH)
    block = ext.at[0:2, own_rows]
    to_mate = rcopy(block, block, halo_s.at[0], halo_r.at[0], mate)
    feats = rcopy(fx.at[core], fx.at[core], halo_s.at[1], halo_r.at[1], mate)
    edge_src, edge_dst = ext.at[0:2, 1 + (2 * rows - 1) * core], ext.at[0:2, (2 * rows + 1) * other]
    edges = [
        rcopy(edge_src, edge_dst, halo_s.at[2 + c], halo_r.at[2 + core], (f, zn * 2 + c)) for c in range(2)
    ]
    edge_in = [
        rcopy(ext.at[0:2, 2 * rows + 1], ext.at[0:2, 2 * rows + 1], halo_s.at[2], halo_r.at[2], mate),
        rcopy(ext.at[0:2, 0], ext.at[0:2, 0], halo_s.at[3], halo_r.at[3], mate),
    ]
    for c in [feats, to_mate] + edges:
        c.start()

    def combine(buf, each):
        m = buf[:, 0, :]
        n = m.shape[0]
        avg = jnp.sum(m, axis=0, keepdims=True) / n
        d = m - avg
        return avg, jnp.sum(buf[:, 1, :], axis=0, keepdims=True) + each * jnp.sum(
            d * d, axis=0, keepdims=True
        )

    before = (lax.rem(f - 1 + NF, NF), t)
    later = ext.at[2:4, own_rows]
    to_before = rcopy(block, later, halo_s.at[4], halo_r.at[4], before)
    to_before.start()

    for c in edge_in:
        c.wait_recv()

    @pl.when(z == 0)
    def _():
        ext[0:2, 0] = jnp.zeros((2, cols, ch), BF16)

    @pl.when(z == NZ - 1)
    def _():
        ext[0:2, 2 * rows + 1] = jnp.zeros((2, cols, ch), BF16)

    rims = [
        rcopy(ext.at[0:2, r], ext.at[2:4, r], halo_s.at[k], halo_r.at[k], before)
        for k, r in ((5, 0), (6, 2 * rows + 1))
    ]
    for c in rims:
        c.start()

    s1 = s1.reshape(2 * NF, 2, ch)
    fan_recv(s1, 1, 2 * NF - 1)
    avg, m2 = combine(s1, float(cells))
    s2[z, 0:1, :] = avg
    s2[z, 1:2, :] = m2
    pl.semaphore_wait(known, len(edge))
    fan(s2, z, zdevs, 2)

    to_before.wait_recv()
    relay = rcopy(later, later, halo_s.at[7], halo_r.at[7], mate)
    relay.start()
    feats.wait()

    @pl.loop(0, 2 * chunks)
    def _(k):
        c, kk = k // chunks, lax.rem(k, chunks)
        per = chunks // frames
        to = (kk // per) * (2 * per) + c * per + lax.rem(kk, per)
        feat_t[to] = flat[c, pl.ds(kk * CHUNK, CHUNK), :].T

    to_mate.wait()
    for c in edges:
        c.wait_send()
    to_before.wait_send()
    for c in rims:
        c.wait()
    relay.wait()
    fan_sent(s1, 1, 2 * NF - 1)

    @pl.when(f == NF - 1)
    def _():
        ext[2:4] = jnp.zeros((2, 2 * rows + 2, cols, ch), BF16)

    @pl.loop(0, 4 * (2 * rows + 2))
    def _(k):
        p, r = k // (2 * rows + 2), lax.rem(k, 2 * rows + 2)
        v = ext[p, r].astype(F32)
        col = lax.broadcasted_iota(jnp.int32, v.shape, 0)
        up = jnp.where(col == cols - 1, 0.0, pltpu.roll(v, cols - 1, 0))
        down = jnp.where(col == 0, 0.0, pltpu.roll(v, 1, 0))
        cotx[0, p, r] = up.astype(BF16)
        cotx[1, p, r] = ext[p, r]
        cotx[2, p, r] = down.astype(BF16)

    for c in loads[2:]:
        c.wait()
    gw, bw = gain[...], bias[...]

    def down(v):
        return jnp.broadcast_to(v, (CHUNK, ch)).T

    bias_t = down(bw)
    fan_recv(s2, 2, NZ - 1)
    fan_sent(s2, 2, NZ - 1)
    if stop == 2:
        return
    avg, m2 = combine(s2, float(cells * 2 * NF))
    per_channel = float(cells * 2 * NF * NZ)
    group = ch // GROUPS
    g_avg = group_sum(avg) / group
    d = avg - g_avg
    spread = group_sum(m2 + per_channel * (d * d)) / (per_channel * group)
    inv = lax.rsqrt(spread + EPS)

    def normed(c, k):
        xh = (flat[c, pl.ds(k * CHUNK, CHUNK), :].astype(F32) - g_avg) * inv
        nrm = xh * gw + bw
        return xh, nrm, 1.0 / (1.0 + jnp.exp(-nrm))

    avg_t, scale_t = down(g_avg), down(inv * gw)

    @pl.loop(0, 2 * chunks, unroll=4)
    def _(k):
        nrm = (feat_t[k].astype(F32) - avg_t) * scale_t + bias_t
        act_t[k] = (nrm * (1.0 / (1.0 + jnp.exp(-nrm)))).astype(BF16)

    def pair(q):
        got = []
        for n in range(2):
            tap = jnp.minimum(core * (2 * HALF) + 2 * q + n, LAST)
            a, b, e = tap // 9, lax.rem(tap // 3, 3), lax.rem(tap, 3)
            got.append(
                cotx[e, pl.ds(2 - a, frames), pl.ds(2 - b, 2 * rows)].reshape(2 * cells, ch)
            )
        acts = jnp.concatenate([act_t[i] for i in range(2 * chunks)], axis=1)
        out = jnp.dot(acts, jnp.concatenate(got, axis=1), preferred_element_type=F32)
        for n in range(2):
            j = 2 * q + n
            part[j // HALF, :, :, lax.rem(j, HALF)] = out[:, n * ch : (n + 1) * ch].reshape(NX, NY, 8, ch)

    pl.loop(0, 4, unroll=True)(pair)
    def pieces_out(h, order, take, devs, into):
        for p, o in enumerate(order):
            for i, (to, dev) in enumerate(devs):
                rcopy(take(to, o), into.at[p, i], rs_s.at[0], rs_r1.at[h, p], dev).start()

    pieces_out(0, ys + [y], lambda to, o: part.at[0, to, o], list(zip(xs, xdevs)), ra1)
    pl.loop(4, HALF, unroll=True)(pair)
    pieces_out(1, xs + [x], lambda to, o: part.at[1, o, to], list(zip(ys, ydevs)), rb1)

    gact[...] = jnp.zeros_like(gact)

    @pl.loop(0, 9, unroll=3)
    def _(k):
        a, b = k // 3, lax.rem(k, 3)
        p, r = pl.ds(2 - a, frames), pl.ds(2 - b + rows * core, rows)
        taps = jnp.concatenate([w[3 * k], w[3 * k + 1], w[3 * k + 2]], axis=1)
        patch = jnp.concatenate([cotx[e, p, r].reshape(cells, ch) for e in range(3)], axis=1)
        gact[...] += lax.dot_general(patch, taps, (((1,), (1,)), ((), ())), preferred_element_type=F32)

    def norm_grad(k, acc):
        at_rows = pl.ds(k * CHUNK, CHUNK)
        xh, nrm, s = normed(core, k)
        gn = gact[at_rows, :] * s * (1.0 + nrm * (1.0 - s))
        gact[at_rows, :] = gn
        xhat[at_rows, :] = xh
        return (
            acc[0] + jnp.sum(gn * xh, axis=0, keepdims=True),
            acc[1] + jnp.sum(gn, axis=0, keepdims=True),
        )

    zero = jnp.zeros((1, ch), F32)
    d_gain, d_shift = lax.fori_loop(0, chunks, norm_grad, (zero, zero))
    g0[core, 0:1, :] = d_gain
    g0[core, 1:2, :] = d_shift
    fan(g0, core, [mate], 3)

    def pass_on(buf, k, n, to, me, devs):
        fan_recv(buf, k, n)
        to[me, 0:1, :] = jnp.sum(buf[:, 0, :], axis=0, keepdims=True)
        to[me, 1:2, :] = jnp.sum(buf[:, 1, :], axis=0, keepdims=True)
        fan(to, me, devs, k + 1)
        fan_sent(buf, k, n)

    pass_on(g0, 3, 1, g1, f, fdevs)

    for p in range(NX):
        yo, xo = (ys + [y])[p], (xs + [x])[p]
        rcopy(ra1.at[p], ra1.at[p], rs_s.at[0], rs_r1.at[0, p], mate).wait_recv()
        part[0, x, yo] += ra1[p, 0] + ra1[p, 1] + ra1[p, 2]
        if p < NX - 1:
            rcopy(part.at[0, x, yo], ra2.at[p], rs_s.at[0], rs_r2.at[0], ydevs[p]).start()
        rcopy(rb1.at[p], rb1.at[p], rs_s.at[0], rs_r1.at[1, p], mate).wait_recv()
        part[1, xo, y] += rb1[p, 0] + rb1[p, 1] + rb1[p, 2]
        if p < NX - 1:
            rcopy(part.at[1, xo, y], rb2.at[p], rs_s.at[0], rs_r2.at[1], xdevs[p]).start()

    rcopy(ra2, ra2, rs_s.at[0], rs_r2.at[0], mate).wait_recv()
    zsrc[0:HALF] = part[0, x, y] + (ra2[0] + ra2[1] + ra2[2])
    rcopy(rb2, rb2, rs_s.at[0], rs_r2.at[1], mate).wait_recv()
    zsrc[HALF : 2 * HALF] = part[1, x, y] + (rb2[0] + rb2[1] + rb2[2])
    for to, dev in zip(zs, zdevs):
        q = lax.rem(to + NZ - FIRST, NZ)

        @pl.when(q < 2 * HALF)
        def _():
            rcopy(zsrc.at[q], rz.at[z], z_s.at[0], z_r.at[0], dev).start()

    owned = lax.rem(z + NZ - FIRST, NZ)
    owner = owned < 2 * HALF

    pass_on(g1, 4, NF - 1, g2, z, zdevs)
    sent = part.reshape(2 * NX * NY, HALF, 8, ch).at[pl.ds(0, 30)]
    rcopy(sent, sent, rs_s.at[0], rs_r2.at[0], mate).wait_send()

    share = 2 * HALF * core

    def out_piece(h, px, py):
        return gk.at[pl.ds(share + h * HALF, HALF), px, py]

    def tiles(n):
        return rz.at[pl.ds(0, n)]

    @pl.when(owner)
    def _():
        rz[z] = zsrc[owned]
        rcopy(tiles(NZ - 1), tiles(NZ - 1), z_s.at[0], z_r.at[0], mate).wait_recv()
        tile = gk.at[share + owned, x, y]
        tile[...] = jnp.sum(rz[...], axis=0)
        for i in sorted(range(NZ), key=lambda i: min(i, NZ - i)):

            @pl.when(z != i)
            def _():
                rcopy(tile, tile, z_s.at[1], z_r.at[1 + owned // HALF], (f, i * 2 + core)).start()

    fan_recv(g2, 5, NZ - 1)
    fan_sent(g2, 5, NZ - 1)
    d_gain = jnp.sum(g2[:, 0, :], axis=0, keepdims=True)
    d_shift = jnp.sum(g2[:, 1, :], axis=0, keepdims=True)
    gs[0:1, :] = d_gain
    gs[1:2, :] = d_shift
    count = per_channel * group
    g_mean = group_sum(gw * d_shift) / count
    g_proj = group_sum(gw * d_gain) / count
    out = fg.reshape(cells, ch)

    @pl.loop(0, chunks)
    def _(k):
        at_rows = pl.ds(pl.multiple_of(k * CHUNK, CHUNK), CHUNK)
        out[at_rows, :] = (
            inv * (gact[at_rows, :] * gw - g_mean - xhat[at_rows, :] * g_proj)
        ).astype(BF16)

    def z_recv(h):
        own = jnp.logical_and(owner, owned // HALF == h)

        @pl.when(own)
        def _():
            rcopy(tiles(HALF - 1), tiles(HALF - 1), z_s.at[1], z_r.at[1 + h], mate).wait_recv()

        @pl.when(jnp.logical_not(own))
        def _():
            rcopy(tiles(HALF), tiles(HALF), z_s.at[1], z_r.at[1 + h], mate).wait_recv()

    def behind(v, n):
        return [lax.rem(v - i + n, n) for i in range(1, n)]

    xb, yb = behind(x, NX), behind(y, NY)

    def put(piece, sem, dev):
        rcopy(piece, piece, ag_s.at[0], sem, dev).start()

    def come(piece, sem):
        rcopy(piece, piece, ag_s.at[0], sem, mate).wait_recv()

    def forward(piece):
        rcopy(piece, piece, fw_s.at[0], fw_r.at[0], mate).start()

    places = [[(x, yy) for yy in [y] + yb], [(xx, y) for xx in [x] + xb]]
    first_devs, second_devs = [ydevs, xdevs], [xdevs, ydevs]
    for p in range(NX):
        for h in range(2):
            piece = out_piece(h, *places[h][p])
            if p == 0:
                z_recv(h)
                for i, dev in enumerate(first_devs[h]):
                    put(piece, ag_r1.at[h, i], dev)
            else:
                come(piece, ag_r1.at[h, p - 1])
            for i, dev in enumerate(second_devs[h]):
                put(piece, ag_r2.at[h, p, i], dev)
            forward(piece)
    for p in range(NX):
        for i in (0, 2, 1):
            for h in range(2):
                px, py = places[h][p]
                piece = out_piece(0, xb[i], py) if h == 0 else out_piece(1, px, yb[i])
                come(piece, ag_r2.at[h, p, i])
                forward(piece)

    @pl.when(owner)
    def _():
        rcopy(tiles(NZ - 1), tiles(NZ - 1), z_s.at[1], z_r.at[0], mate).wait_send()
        rcopy(tiles(2 * HALF - 1), tiles(2 * HALF - 1), z_s.at[0], z_r.at[0], mate).wait_send()

    @pl.when(jnp.logical_not(owner))
    def _():
        rcopy(tiles(2 * HALF), tiles(2 * HALF), z_s.at[0], z_r.at[0], mate).wait_send()

    rcopy(sent, sent, ag_s.at[0], ag_r1.at[0, 0], mate).wait_send()
    full = gk.at[pl.ds(share, 2 * HALF)]
    rcopy(full, full, fw_s.at[0], fw_r.at[0], mate).wait()


def place(fg, gk, gs, fg_o, gk_o, gain_o, shift_o, sem):
    copies = [
        pltpu.make_async_copy(gk.at[pl.ds(0, LAST + 1)], gk_o, sem.at[0]),
        pltpu.make_async_copy(fg, fg_o, sem.at[1]),
        pltpu.make_async_copy(gs.at[0:1], gain_o, sem.at[2]),
        pltpu.make_async_copy(gs.at[1:2], shift_o, sem.at[3]),
    ]
    for c in copies:
        c.start()
    for c in copies:
        c.wait()


def call(stop, cid, features, norm_gain_weight, norm_bias, kernel, cotangent):
    frames, rows, cols, ch = features.shape
    cells = frames * rows * cols
    vm = pl.BlockSpec(memory_space=pltpu.VMEM)
    hbm = pl.BlockSpec(memory_space=pltpu.HBM)
    dma = pltpu.SemaphoreType.DMA
    tile = (8, ch)
    return pl.pallas_call(
        functools.partial(body, stop),
        out_shape=(
            pltpu.VMEM(features.shape, BF16),
            pltpu.VMEM((4 * HALF, NX, NY) + tile, F32),
            pltpu.VMEM((2, ch), F32),
        ),
        in_specs=[hbm] * 5,
        out_specs=(vm, vm, vm),
        scratch_shapes=[
            pltpu.VMEM((2,) + features.shape, BF16),
            pltpu.VMEM((1, ch), F32),
            pltpu.VMEM((1, ch), F32),
            pltpu.VMEM((27, ch, ch), BF16),
            pltpu.VMEM((4, 2 * rows + 2, cols, ch), BF16),
            pltpu.VMEM((3, 4, 2 * rows + 2, cols, ch), BF16),
            pltpu.VMEM((cells, ch), F32),
            pltpu.VMEM((cells, ch), F32),
            pltpu.VMEM((2 * cells // CHUNK, ch, CHUNK), BF16),
            pltpu.VMEM((2 * cells // CHUNK, ch, CHUNK), BF16),
            pltpu.VMEM((2, NF, 2, ch), F32),
            pltpu.VMEM((NZ, 2, ch), F32),
            pltpu.VMEM((2, 2, ch), F32),
            pltpu.VMEM((NF, 2, ch), F32),
            pltpu.VMEM((NZ, 2, ch), F32),
            pltpu.VMEM((2, NX, NY, HALF) + tile, F32),
            pltpu.VMEM((NY, 3, HALF) + tile, F32),
            pltpu.VMEM((NX, 3, HALF) + tile, F32),
            pltpu.VMEM((3, HALF) + tile, F32),
            pltpu.VMEM((3, HALF) + tile, F32),
            pltpu.VMEM((2 * HALF,) + tile, F32),
            pltpu.VMEM((NZ,) + tile, F32),
            dma((5,)), dma((8,)), dma((8,)),
            dma((6,)), dma((6,)),
            dma((1,)), dma((2, NX)), dma((2,)),
            dma((2,)), dma((3,)),
            dma((1,)), dma((2, 3)), dma((2, NX, 3)),
            dma((1,)), dma((1,)),
            pltpu.SemaphoreType.REGULAR,
        ],
        compiler_params=pltpu.CompilerParams(
            collective_id=cid, has_side_effects=True, vmem_limit_bytes=24 * 2**20
        ),
    )(
        *(
            pltpu.with_memory_space_constraint(v, pltpu.HBM)
            for v in (
                features,
                norm_gain_weight.reshape(1, ch),
                norm_bias.reshape(1, ch),
                kernel.reshape(27, ch, ch),
                cotangent,
            )
        )
    )


def on_device(features, norm_gain_weight, norm_bias, kernel, cotangent):
    ch = features.shape[-1]
    made = call(0, 0, features, norm_gain_weight, norm_bias, kernel, cotangent)
    vm = pl.BlockSpec(memory_space=pltpu.VMEM)
    hbm = pl.BlockSpec(memory_space=pltpu.HBM)
    fg, taps, gain, shift = pl.pallas_call(
        place,
        out_shape=(
            jax.ShapeDtypeStruct(features.shape, BF16),
            jax.ShapeDtypeStruct((LAST + 1, NX, NY, 8, ch), F32),
            jax.ShapeDtypeStruct((1, ch), F32),
            jax.ShapeDtypeStruct((1, ch), F32),
        ),
        in_specs=[vm] * 3,
        out_specs=(hbm,) * 4,
        scratch_shapes=[pltpu.SemaphoreType.DMA((4,))],
        compiler_params=pltpu.CompilerParams(vmem_limit_bytes=4 * 2**20),
    )(*(pltpu.with_memory_space_constraint(v, pltpu.VMEM) for v in made))
    return fg, taps.reshape(3, 3, 3, ch, ch), gain.reshape(ch), shift.reshape(ch)


def solution(mesh):
    placed = (P("frame", "tile", None, None), P(), P(), P(), P("frame", "tile", None, None))
    return jax.shard_map(
        on_device,
        mesh=mesh,
        in_specs=placed,
        out_specs=(P("frame", "tile", None, None), P(), P(), P()),
        check_vma=False,
    )
```

```python
import functools

import jax
import jax.numpy as jnp
from jax import lax
from jax.experimental import pallas as pl
from jax.experimental.pallas import tpu as pltpu
from jax.sharding import PartitionSpec as P

MESH = pl.DeviceIdType.MESH
GROUPS = 32
EPS = 1e-06
NX = 4
NY = 4
NZ = 16
NF = NX * NY
LAST = 26
LENS = ((3, 3), (4, 4))
SHARE = tuple(2 * sum(n) for n in LENS)
BASE = (0, SHARE[0])
FROM = tuple(((0, n), (2 * n, 2 * n + m)) for n, m in LENS)
F32 = jnp.float32
BF16 = jnp.bfloat16
CHUNK = 128
FIRST = NZ // 2 + 1
REACH = NZ // 4


def group_sum(v):
    lane = lax.broadcasted_iota(jnp.int32, v.shape, 1)
    v = v + jnp.where(lane % 2 == 0, pltpu.roll(v, 127, 1), pltpu.roll(v, 1, 1))
    return v + jnp.where(lane % 4 < 2, pltpu.roll(v, 126, 1), pltpu.roll(v, 2, 1))


def rcopy(src, dst, ss, rs, dev):
    return pltpu.make_async_remote_copy(
        src_ref=src, dst_ref=dst, send_sem=ss, recv_sem=rs, device_id=dev, device_id_type=MESH
    )


def body(
    stop,
    feat_h, gain_h, bias_h, w_h, cot_h,
    fg, gk, gs,
    fx, gain, bias, w, ext, cotx, gact, xhat, feat_t, act_t,
    s1, s2, g0, g1, g2,
    part00, part01, part10, part11, ra00, ra01, ra10, ra11, rb00, rb01, rb10, rb11, zsrc, rz,
    load_s, halo_s, halo_r, sm_s, sm_r, rs_s, rs_r1, rs_r2, z_s, z_r, ag_s, ag_r1, ag_r2, fw_s, fw_r, known,
):
    f, t = lax.axis_index("frame"), lax.axis_index("tile")
    y, x = f // NX, lax.rem(f, NX)
    z, core = t // 2, lax.rem(t, 2)
    other = 1 - core
    _, frames, rows, cols, ch = fx.shape
    cells = frames * rows * cols
    mate = (f, z * 2 + other)
    zn = lax.rem(z - 1 + 2 * core + NZ, NZ)
    fdevs = [(lax.rem(f + i, NF), t) for i in range(1, NF)]
    fboth = [mate] + [(dev[0], z * 2 + c) for dev in fdevs for c in (core, other)]
    far = sorted(range(1, NZ), key=lambda i: -min(i, NZ - i))
    zs = [lax.rem(z + i, NZ) for i in far]
    zdevs = [(f, j * 2 + core) for j in zs]
    xs = [lax.rem(x + i, NX) for i in range(1, NX)]
    ys = [lax.rem(y + i, NY) for i in range(1, NY)]
    xdevs = [(y * NX + i, t) for i in xs]
    ydevs = [(i * NX + x, t) for i in ys]
    own_rows = pl.ds(1 + rows * core, rows)
    mate_rows = pl.ds(1 + rows * other, rows)

    loads = [
        pltpu.make_async_copy(feat_h, fx.at[core], load_s.at[0]),
        pltpu.make_async_copy(cot_h, ext.at[0:2, own_rows], load_s.at[1]),
        pltpu.make_async_copy(w_h, w, load_s.at[2]),
        pltpu.make_async_copy(gain_h, gain, load_s.at[3]),
        pltpu.make_async_copy(bias_h, bias, load_s.at[4]),
    ]
    for c in loads:
        c.start()

    barrier = pltpu.get_barrier_semaphore()
    near = [dev for i, dev in zip(far, zdevs) if min(i, NZ - i) <= REACH]
    edge = [dev for i, dev in zip(far, zdevs) if min(i, NZ - i) == REACH]
    greet = near + fboth + [(f, zn * 2 + other)]
    for dev in greet:
        pl.semaphore_signal(barrier, inc=1, device_id=dev, device_id_type=MESH)

    loads[0].wait()
    flat = fx.reshape(2, cells, ch)
    chunks = cells // CHUNK

    def add_up(k, acc):
        return acc + jnp.sum(flat[core, pl.ds(k * CHUNK, CHUNK), :].astype(F32), axis=0, keepdims=True)

    mean = lax.fori_loop(0, chunks, add_up, jnp.zeros((1, ch), F32)) / cells

    def add_sq(k, acc):
        d = flat[core, pl.ds(k * CHUNK, CHUNK), :].astype(F32) - mean
        return acc + jnp.sum(d * d, axis=0, keepdims=True)

    m2 = lax.fori_loop(0, chunks, add_sq, jnp.zeros((1, ch), F32))
    s1[core, f, 0:1, :] = mean
    s1[core, f, 1:2, :] = m2
    loads[1].wait()

    pl.semaphore_wait(barrier, len(greet))
    if stop == 1:
        for c in loads[2:]:
            c.wait()
        return

    def fan(buf, me, devs, k):
        for dev in devs:
            rcopy(buf.at[me], buf.at[me], sm_s.at[k], sm_r.at[k], dev).start()

    def fan_recv(buf, k, n):
        many = buf.at[pl.ds(0, n)]
        rcopy(many, many, sm_s.at[k], sm_r.at[k], mate).wait_recv()

    def fan_sent(buf, k, n):
        many = buf.at[pl.ds(0, n)]
        rcopy(many, many, sm_s.at[k], sm_r.at[k], mate).wait_send()

    for dev in fboth:
        rcopy(s1.at[core, f], s1.at[core, f], sm_s.at[1], sm_r.at[1], dev).start()
    for dev in edge:
        pl.semaphore_signal(known, inc=1, device_id=dev, device_id_type=MESH)
    block = ext.at[0:2, own_rows]
    to_mate = rcopy(block, block, halo_s.at[0], halo_r.at[0], mate)
    feats = rcopy(fx.at[core], fx.at[core], halo_s.at[1], halo_r.at[1], mate)
    edge_src, edge_dst = ext.at[0:2, 1 + (2 * rows - 1) * core], ext.at[0:2, (2 * rows + 1) * other]
    edges = [
        rcopy(edge_src, edge_dst, halo_s.at[2 + c], halo_r.at[2 + core], (f, zn * 2 + c)) for c in range(2)
    ]
    edge_in = [
        rcopy(ext.at[0:2, 2 * rows + 1], ext.at[0:2, 2 * rows + 1], halo_s.at[2], halo_r.at[2], mate),
        rcopy(ext.at[0:2, 0], ext.at[0:2, 0], halo_s.at[3], halo_r.at[3], mate),
    ]
    for c in [feats, to_mate] + edges:
        c.start()

    def combine(buf, each):
        m = buf[:, 0, :]
        n = m.shape[0]
        avg = jnp.sum(m, axis=0, keepdims=True) / n
        d = m - avg
        return avg, jnp.sum(buf[:, 1, :], axis=0, keepdims=True) + each * jnp.sum(
            d * d, axis=0, keepdims=True
        )

    before = (lax.rem(f - 1 + NF, NF), t)
    later = ext.at[2:4, own_rows]
    to_before = rcopy(block, later, halo_s.at[4], halo_r.at[4], before)
    to_before.start()

    for c in edge_in:
        c.wait_recv()

    @pl.when(z == 0)
    def _():
        ext[0:2, 0] = jnp.zeros((2, cols, ch), BF16)

    @pl.when(z == NZ - 1)
    def _():
        ext[0:2, 2 * rows + 1] = jnp.zeros((2, cols, ch), BF16)

    rims = [
        rcopy(ext.at[0:2, r], ext.at[2:4, r], halo_s.at[k], halo_r.at[k], before)
        for k, r in ((5, 0), (6, 2 * rows + 1))
    ]
    for c in rims:
        c.start()

    s1 = s1.reshape(2 * NF, 2, ch)
    fan_recv(s1, 1, 2 * NF - 1)
    avg, m2 = combine(s1, float(cells))
    s2[z, 0:1, :] = avg
    s2[z, 1:2, :] = m2
    pl.semaphore_wait(known, len(edge))
    fan(s2, z, zdevs, 2)

    to_before.wait_recv()
    relay = rcopy(later, later, halo_s.at[7], halo_r.at[7], mate)
    relay.start()
    feats.wait()

    @pl.loop(0, 2 * chunks)
    def _(k):
        c, kk = k // chunks, lax.rem(k, chunks)
        per = chunks // frames
        to = (kk // per) * (2 * per) + c * per + lax.rem(kk, per)
        feat_t[to] = flat[c, pl.ds(kk * CHUNK, CHUNK), :].T

    to_mate.wait()
    for c in edges:
        c.wait_send()
    to_before.wait_send()
    for c in rims:
        c.wait()
    relay.wait()
    fan_sent(s1, 1, 2 * NF - 1)

    @pl.when(f == NF - 1)
    def _():
        ext[2:4] = jnp.zeros((2, 2 * rows + 2, cols, ch), BF16)

    @pl.loop(0, 4 * (2 * rows + 2))
    def _(k):
        p, r = k // (2 * rows + 2), lax.rem(k, 2 * rows + 2)
        v = ext[p, r].astype(F32)
        col = lax.broadcasted_iota(jnp.int32, v.shape, 0)
        up = jnp.where(col == cols - 1, 0.0, pltpu.roll(v, cols - 1, 0))
        down = jnp.where(col == 0, 0.0, pltpu.roll(v, 1, 0))
        cotx[0, p, r] = up.astype(BF16)
        cotx[1, p, r] = ext[p, r]
        cotx[2, p, r] = down.astype(BF16)

    for c in loads[2:]:
        c.wait()
    gw, bw = gain[...], bias[...]

    def down(v):
        return jnp.broadcast_to(v, (CHUNK, ch)).T

    bias_t = down(bw)
    fan_recv(s2, 2, NZ - 1)
    fan_sent(s2, 2, NZ - 1)
    if stop == 2:
        return
    avg, m2 = combine(s2, float(cells * 2 * NF))
    per_channel = float(cells * 2 * NF * NZ)
    group = ch // GROUPS
    g_avg = group_sum(avg) / group
    d = avg - g_avg
    spread = group_sum(m2 + per_channel * (d * d)) / (per_channel * group)
    inv = lax.rsqrt(spread + EPS)

    def normed(c, k):
        xh = (flat[c, pl.ds(k * CHUNK, CHUNK), :].astype(F32) - g_avg) * inv
        nrm = xh * gw + bw
        return xh, nrm, 1.0 / (1.0 + jnp.exp(-nrm))

    avg_t, scale_t = down(g_avg), down(inv * gw)

    @pl.loop(0, 2 * chunks, unroll=4)
    def _(k):
        nrm = (feat_t[k].astype(F32) - avg_t) * scale_t + bias_t
        act_t[k] = (nrm * (1.0 / (1.0 + jnp.exp(-nrm)))).astype(BF16)

    def finish(who):
        parts = [[part00, part01], [part10, part11]][who]
        ra = [[ra00, ra01], [ra10, ra11]][who]
        rb = [[rb00, rb01], [rb10, rb11]][who]
        lens, first, share, base = LENS[who], FROM[who], SHARE[who], BASE[who]
        early, late = [x, y], [y, x]

        def early_dev(h, i):
            return (y * NX + lax.rem(x + i, NX), t) if h == 0 else (lax.rem(y + i, NY) * NX + x, t)

        def late_dev(h, i):
            return early_dev(1 - h, i)

        def row(ref, h, at):
            return ref.at[h, at] if h == 0 else ref.at[h, :, at]

        acts = jnp.concatenate([act_t[i] for i in range(2 * chunks)], axis=1)

        def first_stage(g):
            for j in range(lens[g]):
                got = []
                for h in range(2):
                    tap = min(base + first[g][h] + j, LAST)
                    a, b, e = tap // 9, tap // 3 % 3, tap % 3
                    got.append(
                        cotx[e, pl.ds(2 - a, frames), pl.ds(2 - b, 2 * rows)].reshape(2 * cells, ch)
                    )
                out = jnp.dot(acts, jnp.concatenate(got, axis=1), preferred_element_type=F32)
                for h in range(2):
                    parts[g][h, :, :, j] = out[:, h * ch : (h + 1) * ch].reshape(NX, NY, 8, ch)
            for h in range(2):
                for i in (2, 1, 3):
                    to = lax.rem(early[h] + i, NX)
                    rcopy(
                        row(parts[g], h, to), ra[g].at[h, i - 1], rs_s.at[g], rs_r1.at[g, h], early_dev(h, i)
                    ).start()

        first_stage(0)
        first_stage(1)

        gact[...] = jnp.zeros_like(gact)

        @pl.loop(0, 9, unroll=3)
        def _(k):
            a, b = k // 3, lax.rem(k, 3)
            p, r = pl.ds(2 - a, frames), pl.ds(2 - b + rows * core, rows)
            taps = jnp.concatenate([w[3 * k], w[3 * k + 1], w[3 * k + 2]], axis=1)
            patch = jnp.concatenate([cotx[e, p, r].reshape(cells, ch) for e in range(3)], axis=1)
            gact[...] += lax.dot_general(patch, taps, (((1,), (1,)), ((), ())), preferred_element_type=F32)

        def norm_grad(k, acc):
            at_rows = pl.ds(k * CHUNK, CHUNK)
            xh, nrm, s = normed(core, k)
            gn = gact[at_rows, :] * s * (1.0 + nrm * (1.0 - s))
            gact[at_rows, :] = gn
            xhat[at_rows, :] = xh
            return (
                acc[0] + jnp.sum(gn * xh, axis=0, keepdims=True),
                acc[1] + jnp.sum(gn, axis=0, keepdims=True),
            )

        zero = jnp.zeros((1, ch), F32)
        d_gain, d_shift = lax.fori_loop(0, chunks, norm_grad, (zero, zero))
        g0[core, 0:1, :] = d_gain
        g0[core, 1:2, :] = d_shift
        fan(g0, core, [mate], 3)

        def pass_on(buf, k, n, to, me, devs):
            fan_recv(buf, k, n)
            to[me, 0:1, :] = jnp.sum(buf[:, 0, :], axis=0, keepdims=True)
            to[me, 1:2, :] = jnp.sum(buf[:, 1, :], axis=0, keepdims=True)
            fan(to, me, devs, k + 1)
            fan_sent(buf, k, n)

        pass_on(g0, 3, 1, g1, f, fdevs)

        def second_stage(g):
            for h in range(2):
                got = ra[g].at[h]
                rcopy(got, got, rs_s.at[g], rs_r1.at[g, h], mate).wait_recv()
                mine = row(parts[g], h, early[h])
                mine[...] += got[0] + got[1] + got[2]
                for i in (2, 1, 3):
                    rcopy(
                        mine.at[lax.rem(late[h] + i, NX)], rb[g].at[h, i - 1], rs_s.at[g], rs_r2.at[g, h],
                        late_dev(h, i),
                    ).start()

        def z_stage(g):
            for h in range(2):
                got = rb[g].at[h]
                rcopy(got, got, rs_s.at[g], rs_r2.at[g, h], mate).wait_recv()
                zsrc[first[g][h] : first[g][h] + lens[g]] = parts[g][h, x, y] + (got[0] + got[1] + got[2])
            for to, dev in zip(zs, zdevs):
                q = lax.rem(to + NZ - FIRST, NZ)

                @pl.when(jnp.logical_and(q >= first[g][0], q < first[g][0] + 2 * lens[g]))
                def _():
                    rcopy(zsrc.at[q], rz.at[z], z_s.at[0], z_r.at[0], dev).start()

        second_stage(0)
        second_stage(1)
        z_stage(0)
        z_stage(1)
        owned = lax.rem(z + NZ - FIRST, NZ)
        owner = owned < share

        pass_on(g1, 4, NF - 1, g2, z, zdevs)
        sent = [parts[g].reshape(2 * NX * NY, lens[g], 8, ch).at[pl.ds(0, 30)] for g in range(2)]
        for g in range(2):
            rcopy(sent[g], sent[g], rs_s.at[g], rs_r2.at[g, 0], mate).wait_send()

        def out_taps(g, h):
            return gk.at[pl.ds(base + first[g][h], lens[g])]

        def tiles(n):
            return rz.at[pl.ds(0, n)]

        @pl.when(owner)
        def _():
            rz[z] = zsrc[owned]
            rcopy(tiles(NZ - 1), tiles(NZ - 1), z_s.at[0], z_r.at[0], mate).wait_recv()
            tile = gk.at[base + owned, x, y]
            tile[...] = jnp.sum(rz[...], axis=0)
            for dev in zdevs:
                rcopy(tile, tile, z_s.at[1], z_r.at[1 + owned // first[1][0]], dev).start()

        fan_recv(g2, 5, NZ - 1)
        fan_sent(g2, 5, NZ - 1)
        d_gain = jnp.sum(g2[:, 0, :], axis=0, keepdims=True)
        d_shift = jnp.sum(g2[:, 1, :], axis=0, keepdims=True)
        gs[0:1, :] = d_gain
        gs[1:2, :] = d_shift
        count = per_channel * group
        g_mean = group_sum(gw * d_shift) / count
        g_proj = group_sum(gw * d_gain) / count
        out = fg.reshape(cells, ch)

        @pl.loop(0, chunks)
        def _(k):
            at_rows = pl.ds(pl.multiple_of(k * CHUNK, CHUNK), CHUNK)
            out[at_rows, :] = (
                inv * (gact[at_rows, :] * gw - g_mean - xhat[at_rows, :] * g_proj)
            ).astype(BF16)

        def z_recv(g):
            n = 2 * lens[g]
            own = jnp.logical_and(owned >= first[g][0], owned < first[g][0] + n)

            @pl.when(own)
            def _():
                rcopy(tiles(n - 1), tiles(n - 1), z_s.at[1], z_r.at[1 + g], mate).wait_recv()

            @pl.when(jnp.logical_not(own))
            def _():
                rcopy(tiles(n), tiles(n), z_s.at[1], z_r.at[1 + g], mate).wait_recv()

        def come(piece, sem):
            rcopy(piece, piece, ag_s.at[0], sem, mate).wait_recv()

        def forward(piece):
            rcopy(piece, piece, fw_s.at[0], fw_r.at[0], mate).start()

        def out_row(g, h, at):
            return out_taps(g, h).at[:, at] if h == 0 else out_taps(g, h).at[:, :, at]

        def behind(v, i):
            return lax.rem(v - i + NX, NX)

        for g in range(2):
            z_recv(g)
            for h in range(2):
                piece = out_taps(g, h).at[:, x, y]
                for i in (2, 1, 3):
                    rcopy(piece, piece, ag_s.at[g], ag_r1.at[g, h, i - 1], late_dev(h, i)).start()
        for g in range(2):
            for h in range(2):
                mine = out_row(g, h, early[h])
                for i in (1, 3, 2):
                    come(mine.at[:, behind(late[h], i)], ag_r1.at[g, h, i - 1])
                forward(mine)
                for i in (2, 1, 3):
                    rcopy(mine, mine, ag_s.at[g], ag_r2.at[g, h, i - 1], early_dev(h, i)).start()
        for g in range(2):
            for i in (1, 3, 2):
                for h in range(2):
                    theirs = out_row(g, h, behind(early[h], i))
                    come(theirs, ag_r2.at[g, h, i - 1])
                    forward(theirs)

        @pl.when(owner)
        def _():
            rcopy(tiles(NZ - 1), tiles(NZ - 1), z_s.at[1], z_r.at[0], mate).wait_send()
            rcopy(tiles(share - 1), tiles(share - 1), z_s.at[0], z_r.at[0], mate).wait_send()

        @pl.when(jnp.logical_not(owner))
        def _():
            rcopy(tiles(share), tiles(share), z_s.at[0], z_r.at[0], mate).wait_send()

        for g in range(2):
            rcopy(sent[g], sent[g], ag_s.at[g], ag_r1.at[g, 0, 0], mate).wait_send()
        full = gk.at[pl.ds(base, share)]
        rcopy(full, full, fw_s.at[0], fw_r.at[0], mate).wait_send()
        theirs = gk.at[pl.ds(BASE[1 - who], SHARE[1 - who])]
        rcopy(theirs, theirs, fw_s.at[0], fw_r.at[0], mate).wait_recv()

    for who in range(2):
        pl.when(core == who)(functools.partial(finish, who))


def place(fg, gk, gs, fg_o, gk_o, gain_o, shift_o, sem):
    copies = [
        pltpu.make_async_copy(gk.at[pl.ds(0, LAST + 1)], gk_o, sem.at[0]),
        pltpu.make_async_copy(fg, fg_o, sem.at[1]),
        pltpu.make_async_copy(gs.at[0:1], gain_o, sem.at[2]),
        pltpu.make_async_copy(gs.at[1:2], shift_o, sem.at[3]),
    ]
    for c in copies:
        c.start()
    for c in copies:
        c.wait()


def call(stop, cid, features, norm_gain_weight, norm_bias, kernel, cotangent):
    frames, rows, cols, ch = features.shape
    cells = frames * rows * cols
    vm = pl.BlockSpec(memory_space=pltpu.VMEM)
    hbm = pl.BlockSpec(memory_space=pltpu.HBM)
    dma = pltpu.SemaphoreType.DMA
    tile = (8, ch)
    return pl.pallas_call(
        functools.partial(body, stop),
        out_shape=(
            pltpu.VMEM(features.shape, BF16),
            pltpu.VMEM((sum(SHARE), NX, NY) + tile, F32),
            pltpu.VMEM((2, ch), F32),
        ),
        in_specs=[hbm] * 5,
        out_specs=(vm, vm, vm),
        scratch_shapes=[
            pltpu.VMEM((2,) + features.shape, BF16),
            pltpu.VMEM((1, ch), F32),
            pltpu.VMEM((1, ch), F32),
            pltpu.VMEM((27, ch, ch), BF16),
            pltpu.VMEM((4, 2 * rows + 2, cols, ch), BF16),
            pltpu.VMEM((3, 4, 2 * rows + 2, cols, ch), BF16),
            pltpu.VMEM((cells, ch), F32),
            pltpu.VMEM((cells, ch), F32),
            pltpu.VMEM((2 * cells // CHUNK, ch, CHUNK), BF16),
            pltpu.VMEM((2 * cells // CHUNK, ch, CHUNK), BF16),
            pltpu.VMEM((2, NF, 2, ch), F32),
            pltpu.VMEM((NZ, 2, ch), F32),
            pltpu.VMEM((2, 2, ch), F32),
            pltpu.VMEM((NF, 2, ch), F32),
            pltpu.VMEM((NZ, 2, ch), F32),
            *(pltpu.VMEM((2, NX, NY, n) + tile, F32) for of in LENS for n in of),
            *(pltpu.VMEM((2, 3, NX, n) + tile, F32) for of in LENS for n in of),
            *(pltpu.VMEM((2, 3, n) + tile, F32) for of in LENS for n in of),
            pltpu.VMEM((NZ,) + tile, F32),
            pltpu.VMEM((NZ,) + tile, F32),
            dma((5,)), dma((8,)), dma((8,)),
            dma((6,)), dma((6,)),
            dma((2,)), dma((2, 2)), dma((2, 2)),
            dma((2,)), dma((3,)),
            dma((2,)), dma((2, 2, 3)), dma((2, 2, 3)),
            dma((1,)), dma((1,)),
            pltpu.SemaphoreType.REGULAR,
        ],
        compiler_params=pltpu.CompilerParams(
            collective_id=cid, has_side_effects=True, vmem_limit_bytes=24 * 2**20
        ),
    )(
        *(
            pltpu.with_memory_space_constraint(v, pltpu.HBM)
            for v in (
                features,
                norm_gain_weight.reshape(1, ch),
                norm_bias.reshape(1, ch),
                kernel.reshape(27, ch, ch),
                cotangent,
            )
        )
    )


def on_device(features, norm_gain_weight, norm_bias, kernel, cotangent):
    ch = features.shape[-1]
    made = call(0, 0, features, norm_gain_weight, norm_bias, kernel, cotangent)
    vm = pl.BlockSpec(memory_space=pltpu.VMEM)
    hbm = pl.BlockSpec(memory_space=pltpu.HBM)
    fg, taps, gain, shift = pl.pallas_call(
        place,
        out_shape=(
            jax.ShapeDtypeStruct(features.shape, BF16),
            jax.ShapeDtypeStruct((LAST + 1, NX, NY, 8, ch), F32),
            jax.ShapeDtypeStruct((1, ch), F32),
            jax.ShapeDtypeStruct((1, ch), F32),
        ),
        in_specs=[vm] * 3,
        out_specs=(hbm,) * 4,
        scratch_shapes=[pltpu.SemaphoreType.DMA((4,))],
        compiler_params=pltpu.CompilerParams(vmem_limit_bytes=4 * 2**20),
    )(*(pltpu.with_memory_space_constraint(v, pltpu.VMEM) for v in made))
    return fg, taps.reshape(3, 3, 3, ch, ch), gain.reshape(ch), shift.reshape(ch)


def solution(mesh):
    placed = (P("frame", "tile", None, None), P(), P(), P(), P("frame", "tile", None, None))
    return jax.shard_map(
        on_device,
        mesh=mesh,
        in_specs=placed,
        out_specs=(P("frame", "tile", None, None), P(), P(), P()),
        check_vma=False,
    )
```

```python
import functools

import jax
import jax.numpy as jnp
from jax import lax
from jax.experimental import pallas as pl
from jax.experimental.pallas import tpu as pltpu
from jax.sharding import PartitionSpec as P

MESH = pl.DeviceIdType.MESH
GROUPS = 32
EPS = 1e-06
NX = 4
NY = 4
NZ = 16
NF = NX * NY
LAST = 26
LENS = (((3, 3), (3, 3)), ((4, 4), (4, 3)))
SHARE = tuple(sum(map(sum, of)) for of in LENS)
BASE = (0, SHARE[0])
FROM = tuple(((0, p[0]), (sum(p), sum(p) + q[0])) for p, q in LENS)
FIRST = (11, 9)
F32 = jnp.float32
BF16 = jnp.bfloat16
CHUNK = 128
REACH = NZ // 4


def group_sum(v):
    lane = lax.broadcasted_iota(jnp.int32, v.shape, 1)
    v = v + jnp.where(lane % 2 == 0, pltpu.roll(v, 127, 1), pltpu.roll(v, 1, 1))
    return v + jnp.where(lane % 4 < 2, pltpu.roll(v, 126, 1), pltpu.roll(v, 2, 1))


def rcopy(src, dst, ss, rs, dev):
    return pltpu.make_async_remote_copy(
        src_ref=src, dst_ref=dst, send_sem=ss, recv_sem=rs, device_id=dev, device_id_type=MESH
    )


def body(
    stop,
    feat_h, gain_h, bias_h, w_h, cot_h,
    fg, gk, gs,
    fx, gain, bias, w, ext, cotx, gact, xhat, feat_t, act_t,
    s1, s2, g0, g1, g2,
    zsrc, rz,
    load_s, halo_s, halo_r, sm_s, sm_r, rs_s, rs_r1, rs_r2, z_s, z_r, ag_s, ag_r1, ag_r2, fw_s, fw_r, known, *bufs,
):
    f, t = lax.axis_index("frame"), lax.axis_index("tile")
    y, x = f // NX, lax.rem(f, NX)
    z, core = t // 2, lax.rem(t, 2)
    other = 1 - core
    _, frames, rows, cols, ch = fx.shape
    cells = frames * rows * cols
    mate = (f, z * 2 + other)
    zn = lax.rem(z - 1 + 2 * core + NZ, NZ)
    fdevs = [(lax.rem(f + i, NF), t) for i in range(1, NF)]
    fboth = [mate] + [(dev[0], z * 2 + c) for dev in fdevs for c in (core, other)]
    far = sorted(range(1, NZ), key=lambda i: -min(i, NZ - i))
    zs = [lax.rem(z + i, NZ) for i in far]
    zdevs = [(f, j * 2 + core) for j in zs]
    xs = [lax.rem(x + i, NX) for i in range(1, NX)]
    ys = [lax.rem(y + i, NY) for i in range(1, NY)]
    xdevs = [(y * NX + i, t) for i in xs]
    ydevs = [(i * NX + x, t) for i in ys]
    own_rows = pl.ds(1 + rows * core, rows)
    mate_rows = pl.ds(1 + rows * other, rows)

    loads = [
        pltpu.make_async_copy(feat_h, fx.at[core], load_s.at[0]),
        pltpu.make_async_copy(cot_h, ext.at[0:2, own_rows], load_s.at[1]),
        pltpu.make_async_copy(w_h, w, load_s.at[2]),
        pltpu.make_async_copy(gain_h, gain, load_s.at[3]),
        pltpu.make_async_copy(bias_h, bias, load_s.at[4]),
    ]
    for c in loads:
        c.start()

    barrier = pltpu.get_barrier_semaphore()
    near = [dev for i, dev in zip(far, zdevs) if min(i, NZ - i) <= REACH]
    edge = [dev for i, dev in zip(far, zdevs) if min(i, NZ - i) == REACH]
    greet = near + fboth + [(f, zn * 2 + other)]
    for dev in greet:
        pl.semaphore_signal(barrier, inc=1, device_id=dev, device_id_type=MESH)

    loads[0].wait()
    flat = fx.reshape(2, cells, ch)
    chunks = cells // CHUNK

    def add_up(k, acc):
        return acc + jnp.sum(flat[core, pl.ds(k * CHUNK, CHUNK), :].astype(F32), axis=0, keepdims=True)

    mean = lax.fori_loop(0, chunks, add_up, jnp.zeros((1, ch), F32)) / cells

    def add_sq(k, acc):
        d = flat[core, pl.ds(k * CHUNK, CHUNK), :].astype(F32) - mean
        return acc + jnp.sum(d * d, axis=0, keepdims=True)

    m2 = lax.fori_loop(0, chunks, add_sq, jnp.zeros((1, ch), F32))
    s1[core, f, 0:1, :] = mean
    s1[core, f, 1:2, :] = m2
    loads[1].wait()

    pl.semaphore_wait(barrier, len(greet))
    if stop == 1:
        for c in loads[2:]:
            c.wait()
        return

    def fan(buf, me, devs, k):
        for dev in devs:
            rcopy(buf.at[me], buf.at[me], sm_s.at[k], sm_r.at[k], dev).start()

    def fan_recv(buf, k, n):
        many = buf.at[pl.ds(0, n)]
        rcopy(many, many, sm_s.at[k], sm_r.at[k], mate).wait_recv()

    def fan_sent(buf, k, n):
        many = buf.at[pl.ds(0, n)]
        rcopy(many, many, sm_s.at[k], sm_r.at[k], mate).wait_send()

    for dev in fboth:
        rcopy(s1.at[core, f], s1.at[core, f], sm_s.at[1], sm_r.at[1], dev).start()
    for dev in edge:
        pl.semaphore_signal(known, inc=1, device_id=dev, device_id_type=MESH)
    block = ext.at[0:2, own_rows]
    to_mate = rcopy(block, block, halo_s.at[0], halo_r.at[0], mate)
    feats = rcopy(fx.at[core], fx.at[core], halo_s.at[1], halo_r.at[1], mate)
    edge_src, edge_dst = ext.at[0:2, 1 + (2 * rows - 1) * core], ext.at[0:2, (2 * rows + 1) * other]
    edges = [
        rcopy(edge_src, edge_dst, halo_s.at[2 + c], halo_r.at[2 + core], (f, zn * 2 + c)) for c in range(2)
    ]
    edge_in = [
        rcopy(ext.at[0:2, 2 * rows + 1], ext.at[0:2, 2 * rows + 1], halo_s.at[2], halo_r.at[2], mate),
        rcopy(ext.at[0:2, 0], ext.at[0:2, 0], halo_s.at[3], halo_r.at[3], mate),
    ]
    for c in [feats, to_mate] + edges:
        c.start()

    def combine(buf, each):
        m = buf[:, 0, :]
        n = m.shape[0]
        avg = jnp.sum(m, axis=0, keepdims=True) / n
        d = m - avg
        return avg, jnp.sum(buf[:, 1, :], axis=0, keepdims=True) + each * jnp.sum(
            d * d, axis=0, keepdims=True
        )

    before = (lax.rem(f - 1 + NF, NF), t)
    later = ext.at[2:4, own_rows]
    to_before = rcopy(block, later, halo_s.at[4], halo_r.at[4], before)
    to_before.start()

    for c in edge_in:
        c.wait_recv()

    @pl.when(z == 0)
    def _():
        ext[0:2, 0] = jnp.zeros((2, cols, ch), BF16)

    @pl.when(z == NZ - 1)
    def _():
        ext[0:2, 2 * rows + 1] = jnp.zeros((2, cols, ch), BF16)

    rims = [
        rcopy(ext.at[0:2, r], ext.at[2:4, r], halo_s.at[k], halo_r.at[k], before)
        for k, r in ((5, 0), (6, 2 * rows + 1))
    ]
    for c in rims:
        c.start()

    s1 = s1.reshape(2 * NF, 2, ch)
    fan_recv(s1, 1, 2 * NF - 1)
    avg, m2 = combine(s1, float(cells))
    s2[z, 0:1, :] = avg
    s2[z, 1:2, :] = m2
    pl.semaphore_wait(known, len(edge))
    fan(s2, z, zdevs, 2)

    to_before.wait_recv()
    relay = rcopy(later, later, halo_s.at[7], halo_r.at[7], mate)
    relay.start()
    feats.wait()

    @pl.loop(0, 2 * chunks)
    def _(k):
        c, kk = k // chunks, lax.rem(k, chunks)
        per = chunks // frames
        to = (kk // per) * (2 * per) + c * per + lax.rem(kk, per)
        feat_t[to] = flat[c, pl.ds(kk * CHUNK, CHUNK), :].T

    to_mate.wait()
    for c in edges:
        c.wait_send()
    to_before.wait_send()
    for c in rims:
        c.wait()
    relay.wait()
    fan_sent(s1, 1, 2 * NF - 1)

    @pl.when(f == NF - 1)
    def _():
        ext[2:4] = jnp.zeros((2, 2 * rows + 2, cols, ch), BF16)

    @pl.loop(0, 4 * (2 * rows + 2))
    def _(k):
        p, r = k // (2 * rows + 2), lax.rem(k, 2 * rows + 2)
        v = ext[p, r].astype(F32)
        col = lax.broadcasted_iota(jnp.int32, v.shape, 0)
        up = jnp.where(col == cols - 1, 0.0, pltpu.roll(v, cols - 1, 0))
        down = jnp.where(col == 0, 0.0, pltpu.roll(v, 1, 0))
        cotx[0, p, r] = up.astype(BF16)
        cotx[1, p, r] = ext[p, r]
        cotx[2, p, r] = down.astype(BF16)

    for c in loads[2:]:
        c.wait()
    gw, bw = gain[...], bias[...]

    def down(v):
        return jnp.broadcast_to(v, (CHUNK, ch)).T

    bias_t = down(bw)
    fan_recv(s2, 2, NZ - 1)
    fan_sent(s2, 2, NZ - 1)
    if stop == 2:
        return
    avg, m2 = combine(s2, float(cells * 2 * NF))
    per_channel = float(cells * 2 * NF * NZ)
    group = ch // GROUPS
    g_avg = group_sum(avg) / group
    d = avg - g_avg
    spread = group_sum(m2 + per_channel * (d * d)) / (per_channel * group)
    inv = lax.rsqrt(spread + EPS)

    def normed(c, k):
        xh = (flat[c, pl.ds(k * CHUNK, CHUNK), :].astype(F32) - g_avg) * inv
        nrm = xh * gw + bw
        return xh, nrm, 1.0 / (1.0 + jnp.exp(-nrm))

    avg_t, scale_t = down(g_avg), down(inv * gw)

    @pl.loop(0, 2 * chunks, unroll=4)
    def _(k):
        nrm = (feat_t[k].astype(F32) - avg_t) * scale_t + bias_t
        act_t[k] = (nrm * (1.0 / (1.0 + jnp.exp(-nrm)))).astype(BF16)

    def finish(who):
        parts, ra, rb = (
            [[bufs[8 * kind + 4 * who + 2 * g + h] for h in range(2)] for g in range(2)]
            for kind in range(3)
        )
        lens, first, share, base = LENS[who], FROM[who], SHARE[who], BASE[who]
        early, late = [x, y], [y, x]

        def early_dev(h, i):
            return (y * NX + lax.rem(x + i, NX), t) if h == 0 else (lax.rem(y + i, NY) * NX + x, t)

        def late_dev(h, i):
            return early_dev(1 - h, i)

        def row(ref, h, at):
            return ref.at[at] if h == 0 else ref.at[:, at]

        acts = jnp.concatenate([act_t[i] for i in range(2 * chunks)], axis=1)

        def first_stage(g):
            for j in range(max(lens[g])):
                halves = [h for h in range(2) if j < lens[g][h]]
                got = []
                for h in halves:
                    tap = base + first[g][h] + j
                    a, b, e = tap // 9, tap // 3 % 3, tap % 3
                    got.append(
                        cotx[e, pl.ds(2 - a, frames), pl.ds(2 - b, 2 * rows)].reshape(2 * cells, ch)
                    )
                out = jnp.dot(acts, jnp.concatenate(got, axis=1), preferred_element_type=F32)
                for n, h in enumerate(halves):
                    parts[g][h][:, :, j] = out[:, n * ch : (n + 1) * ch].reshape(NX, NY, 8, ch)
            for h in range(2):
                for i in (2, 1, 3):
                    to = lax.rem(early[h] + i, NX)
                    rcopy(
                        row(parts[g][h], h, to), ra[g][h].at[i - 1], rs_s.at[g, h], rs_r1.at[g, h], early_dev(h, i)
                    ).start()

        first_stage(0)
        first_stage(1)

        gact[...] = jnp.zeros_like(gact)

        @pl.loop(0, 9, unroll=3)
        def _(k):
            a, b = k // 3, lax.rem(k, 3)
            p, r = pl.ds(2 - a, frames), pl.ds(2 - b + rows * core, rows)
            taps = jnp.concatenate([w[3 * k], w[3 * k + 1], w[3 * k + 2]], axis=1)
            patch = jnp.concatenate([cotx[e, p, r].reshape(cells, ch) for e in range(3)], axis=1)
            gact[...] += lax.dot_general(patch, taps, (((1,), (1,)), ((), ())), preferred_element_type=F32)

        def norm_grad(k, acc):
            at_rows = pl.ds(k * CHUNK, CHUNK)
            xh, nrm, s = normed(core, k)
            gn = gact[at_rows, :] * s * (1.0 + nrm * (1.0 - s))
            gact[at_rows, :] = gn
            xhat[at_rows, :] = xh
            return (
                acc[0] + jnp.sum(gn * xh, axis=0, keepdims=True),
                acc[1] + jnp.sum(gn, axis=0, keepdims=True),
            )

        zero = jnp.zeros((1, ch), F32)
        d_gain, d_shift = lax.fori_loop(0, chunks, norm_grad, (zero, zero))
        g0[core, 0:1, :] = d_gain
        g0[core, 1:2, :] = d_shift
        fan(g0, core, [mate], 3)

        def pass_on(buf, k, n, to, me, devs):
            fan_recv(buf, k, n)
            to[me, 0:1, :] = jnp.sum(buf[:, 0, :], axis=0, keepdims=True)
            to[me, 1:2, :] = jnp.sum(buf[:, 1, :], axis=0, keepdims=True)
            fan(to, me, devs, k + 1)
            fan_sent(buf, k, n)

        pass_on(g0, 3, 1, g1, f, fdevs)

        def second_stage(g):
            for h in range(2):
                got = ra[g][h]
                rcopy(got, got, rs_s.at[g, h], rs_r1.at[g, h], mate).wait_recv()
                mine = row(parts[g][h], h, early[h])
                mine[...] += got[0] + got[1] + got[2]
                for i in (2, 1, 3):
                    rcopy(
                        mine.at[lax.rem(late[h] + i, NX)], rb[g][h].at[i - 1], rs_s.at[g, h], rs_r2.at[g, h],
                        late_dev(h, i),
                    ).start()

        def z_stage(g):
            for h in range(2):
                got = rb[g][h]
                rcopy(got, got, rs_s.at[g, h], rs_r2.at[g, h], mate).wait_recv()
                zsrc[first[g][h] : first[g][h] + lens[g][h]] = parts[g][h][x, y] + (got[0] + got[1] + got[2])
            for to, dev in zip(zs, zdevs):
                q = lax.rem(to + NZ - FIRST[who], NZ)

                @pl.when(jnp.logical_and(q >= first[g][0], q < first[g][0] + sum(lens[g])))
                def _():
                    rcopy(zsrc.at[q], rz.at[z], z_s.at[0], z_r.at[0], dev).start()

        second_stage(0)
        second_stage(1)
        z_stage(0)
        z_stage(1)
        owned = lax.rem(z + NZ - FIRST[who], NZ)
        owner = owned < share

        pass_on(g1, 4, NF - 1, g2, z, zdevs)
        sent = [
            [parts[g][h].reshape(NX * NY, lens[g][h], 8, ch).at[pl.ds(0, NX * NY - 1)] for h in range(2)]
            for g in range(2)
        ]
        for g in range(2):
            for h in range(2):
                rcopy(sent[g][h], sent[g][h], rs_s.at[g, h], rs_r2.at[g, h], mate).wait_send()

        def out_taps(g, h):
            return gk.at[pl.ds(base + first[g][h], lens[g][h])]

        def tiles(n):
            return rz.at[pl.ds(0, n)]

        @pl.when(owner)
        def _():
            rz[z] = zsrc[owned]
            rcopy(tiles(NZ - 1), tiles(NZ - 1), z_s.at[0], z_r.at[0], mate).wait_recv()
            tile = gk.at[base + owned, x, y]
            tile[...] = jnp.sum(rz[...], axis=0)
            for dev in zdevs:
                rcopy(tile, tile, z_s.at[1], z_r.at[1 + owned // first[1][0]], dev).start()

        fan_recv(g2, 5, NZ - 1)
        fan_sent(g2, 5, NZ - 1)
        d_gain = jnp.sum(g2[:, 0, :], axis=0, keepdims=True)
        d_shift = jnp.sum(g2[:, 1, :], axis=0, keepdims=True)
        gs[0:1, :] = d_gain
        gs[1:2, :] = d_shift
        count = per_channel * group
        g_mean = group_sum(gw * d_shift) / count
        g_proj = group_sum(gw * d_gain) / count
        out = fg.reshape(cells, ch)

        @pl.loop(0, chunks)
        def _(k):
            at_rows = pl.ds(pl.multiple_of(k * CHUNK, CHUNK), CHUNK)
            out[at_rows, :] = (
                inv * (gact[at_rows, :] * gw - g_mean - xhat[at_rows, :] * g_proj)
            ).astype(BF16)

        def z_recv(g):
            n = sum(lens[g])
            own = jnp.logical_and(owned >= first[g][0], owned < first[g][0] + n)

            @pl.when(own)
            def _():
                rcopy(tiles(n - 1), tiles(n - 1), z_s.at[1], z_r.at[1 + g], mate).wait_recv()

            @pl.when(jnp.logical_not(own))
            def _():
                rcopy(tiles(n), tiles(n), z_s.at[1], z_r.at[1 + g], mate).wait_recv()

        def come(piece, sem):
            rcopy(piece, piece, ag_s.at[0, 0], sem, mate).wait_recv()

        def forward(piece):
            rcopy(piece, piece, fw_s.at[0], fw_r.at[0], mate).start()

        def out_row(g, h, at):
            return out_taps(g, h).at[:, at] if h == 0 else out_taps(g, h).at[:, :, at]

        def behind(v, i):
            return lax.rem(v - i + NX, NX)

        for g in range(2):
            z_recv(g)
            for h in range(2):
                piece = out_taps(g, h).at[:, x, y]
                for i in (2, 1, 3):
                    rcopy(piece, piece, ag_s.at[g, h], ag_r1.at[g, h, i - 1], late_dev(h, i)).start()
        for g in range(2):
            for h in range(2):
                mine = out_row(g, h, early[h])
                for i in (1, 3, 2):
                    come(mine.at[:, behind(late[h], i)], ag_r1.at[g, h, i - 1])
                forward(mine)
                for i in (2, 1, 3):
                    rcopy(mine, mine, ag_s.at[g, h], ag_r2.at[g, h, i - 1], early_dev(h, i)).start()
        for g in range(2):
            for i in (1, 3, 2):
                for h in range(2):
                    theirs = out_row(g, h, behind(early[h], i))
                    come(theirs, ag_r2.at[g, h, i - 1])
                    forward(theirs)

        @pl.when(owner)
        def _():
            rcopy(tiles(NZ - 1), tiles(NZ - 1), z_s.at[1], z_r.at[0], mate).wait_send()
            rcopy(tiles(share - 1), tiles(share - 1), z_s.at[0], z_r.at[0], mate).wait_send()

        @pl.when(jnp.logical_not(owner))
        def _():
            rcopy(tiles(share), tiles(share), z_s.at[0], z_r.at[0], mate).wait_send()

        for g in range(2):
            for h in range(2):
                rcopy(sent[g][h], sent[g][h], ag_s.at[g, h], ag_r1.at[g, h, 0], mate).wait_send()
        full = gk.at[pl.ds(base, share)]
        rcopy(full, full, fw_s.at[0], fw_r.at[0], mate).wait_send()
        theirs = gk.at[pl.ds(BASE[1 - who], SHARE[1 - who])]
        rcopy(theirs, theirs, fw_s.at[0], fw_r.at[0], mate).wait_recv()

    for who in range(2):
        pl.when(core == who)(functools.partial(finish, who))


def place(fg, gk, gs, fg_o, gk_o, gain_o, shift_o, sem):
    copies = [
        pltpu.make_async_copy(gk.at[pl.ds(0, LAST + 1)], gk_o, sem.at[0]),
        pltpu.make_async_copy(fg, fg_o, sem.at[1]),
        pltpu.make_async_copy(gs.at[0:1], gain_o, sem.at[2]),
        pltpu.make_async_copy(gs.at[1:2], shift_o, sem.at[3]),
    ]
    for c in copies:
        c.start()
    for c in copies:
        c.wait()


def call(stop, cid, features, norm_gain_weight, norm_bias, kernel, cotangent):
    frames, rows, cols, ch = features.shape
    cells = frames * rows * cols
    vm = pl.BlockSpec(memory_space=pltpu.VMEM)
    hbm = pl.BlockSpec(memory_space=pltpu.HBM)
    dma = pltpu.SemaphoreType.DMA
    tile = (8, ch)
    return pl.pallas_call(
        functools.partial(body, stop),
        out_shape=(
            pltpu.VMEM(features.shape, BF16),
            pltpu.VMEM((sum(SHARE), NX, NY) + tile, F32),
            pltpu.VMEM((2, ch), F32),
        ),
        in_specs=[hbm] * 5,
        out_specs=(vm, vm, vm),
        scratch_shapes=[
            pltpu.VMEM((2,) + features.shape, BF16),
            pltpu.VMEM((1, ch), F32),
            pltpu.VMEM((1, ch), F32),
            pltpu.VMEM((27, ch, ch), BF16),
            pltpu.VMEM((4, 2 * rows + 2, cols, ch), BF16),
            pltpu.VMEM((3, 4, 2 * rows + 2, cols, ch), BF16),
            pltpu.VMEM((cells, ch), F32),
            pltpu.VMEM((cells, ch), F32),
            pltpu.VMEM((2 * cells // CHUNK, ch, CHUNK), BF16),
            pltpu.VMEM((2 * cells // CHUNK, ch, CHUNK), BF16),
            pltpu.VMEM((2, NF, 2, ch), F32),
            pltpu.VMEM((NZ, 2, ch), F32),
            pltpu.VMEM((2, 2, ch), F32),
            pltpu.VMEM((NF, 2, ch), F32),
            pltpu.VMEM((NZ, 2, ch), F32),
            pltpu.VMEM((NZ,) + tile, F32),
            pltpu.VMEM((NZ,) + tile, F32),
            dma((5,)), dma((8,)), dma((8,)),
            dma((6,)), dma((6,)),
            dma((2, 2)), dma((2, 2)), dma((2, 2)),
            dma((2,)), dma((3,)),
            dma((2, 2)), dma((2, 2, 3)), dma((2, 2, 3)),
            dma((1,)), dma((1,)),
            pltpu.SemaphoreType.REGULAR,
            *(
                pltpu.VMEM(dims + (n,) + tile, F32)
                for dims in ((NX, NY), (3, NX), (3,))
                for of in LENS
                for pair in of
                for n in pair
            ),
        ],
        compiler_params=pltpu.CompilerParams(
            collective_id=cid, has_side_effects=True, vmem_limit_bytes=24 * 2**20
        ),
    )(
        *(
            pltpu.with_memory_space_constraint(v, pltpu.HBM)
            for v in (
                features,
                norm_gain_weight.reshape(1, ch),
                norm_bias.reshape(1, ch),
                kernel.reshape(27, ch, ch),
                cotangent,
            )
        )
    )


def on_device(features, norm_gain_weight, norm_bias, kernel, cotangent):
    ch = features.shape[-1]
    made = call(0, 0, features, norm_gain_weight, norm_bias, kernel, cotangent)
    vm = pl.BlockSpec(memory_space=pltpu.VMEM)
    hbm = pl.BlockSpec(memory_space=pltpu.HBM)
    fg, taps, gain, shift = pl.pallas_call(
        place,
        out_shape=(
            jax.ShapeDtypeStruct(features.shape, BF16),
            jax.ShapeDtypeStruct((LAST + 1, NX, NY, 8, ch), F32),
            jax.ShapeDtypeStruct((1, ch), F32),
            jax.ShapeDtypeStruct((1, ch), F32),
        ),
        in_specs=[vm] * 3,
        out_specs=(hbm,) * 4,
        scratch_shapes=[pltpu.SemaphoreType.DMA((4,))],
        compiler_params=pltpu.CompilerParams(vmem_limit_bytes=4 * 2**20),
    )(*(pltpu.with_memory_space_constraint(v, pltpu.VMEM) for v in made))
    return fg, taps.reshape(3, 3, 3, ch, ch), gain.reshape(ch), shift.reshape(ch)


def solution(mesh):
    placed = (P("frame", "tile", None, None), P(), P(), P(), P("frame", "tile", None, None))
    return jax.shard_map(
        on_device,
        mesh=mesh,
        in_specs=placed,
        out_specs=(P("frame", "tile", None, None), P(), P(), P()),
        check_vma=False,
    )
```

```python
import functools

import jax
import jax.numpy as jnp
from jax import lax
from jax.experimental import pallas as pl
from jax.experimental.pallas import tpu as pltpu
from jax.sharding import PartitionSpec as P

MESH = pl.DeviceIdType.MESH
GROUPS = 32
EPS = 1e-06
NX = 4
NY = 4
NZ = 16
NF = NX * NY
LAST = 26
LENS = (((3, 3), (3, 3)), ((4, 4), (4, 3)))
SHARE = tuple(sum(map(sum, of)) for of in LENS)
BASE = (0, SHARE[0])
FROM = tuple(((0, p[0]), (sum(p), sum(p) + q[0])) for p, q in LENS)
FIRST = (11, 9)
F32 = jnp.float32
BF16 = jnp.bfloat16
CHUNK = 128
REACH = NZ // 4


def group_sum(v):
    lane = lax.broadcasted_iota(jnp.int32, v.shape, 1)
    v = v + jnp.where(lane % 2 == 0, pltpu.roll(v, 127, 1), pltpu.roll(v, 1, 1))
    return v + jnp.where(lane % 4 < 2, pltpu.roll(v, 126, 1), pltpu.roll(v, 2, 1))


def rcopy(src, dst, ss, rs, dev):
    return pltpu.make_async_remote_copy(
        src_ref=src, dst_ref=dst, send_sem=ss, recv_sem=rs, device_id=dev, device_id_type=MESH
    )


def body(
    stop,
    feat_h, gain_h, bias_h, w_h, cot_h,
    fg, gk, gs,
    fx, gain, bias, w, ext, cotx, gact, xhat, feat_t, act_t,
    s1, s2, s3, g0, g1, g2,
    zsrc, rz,
    load_s, halo_s, halo_r, sm_s, sm_r, rs_s, rs_r1, rs_r2, z_s, z_r, ag_s, ag_r1, ag_r2, fw_s, fw_r, known, *bufs,
):
    f, t = lax.axis_index("frame"), lax.axis_index("tile")
    y, x = f // NX, lax.rem(f, NX)
    z, core = t // 2, lax.rem(t, 2)
    other = 1 - core
    _, frames, rows, cols, ch = fx.shape
    cells = frames * rows * cols
    mate = (f, z * 2 + other)
    zn = lax.rem(z - 1 + 2 * core + NZ, NZ)
    fdevs = [(lax.rem(f + i, NF), t) for i in range(1, NF)]
    fboth = [mate] + [(dev[0], z * 2 + c) for dev in fdevs for c in (core, other)]
    far = sorted(range(1, NZ), key=lambda i: -min(i, NZ - i))
    zs = [lax.rem(z + i, NZ) for i in far]
    zdevs = [(f, j * 2 + core) for j in zs]
    xs = [lax.rem(x + i, NX) for i in range(1, NX)]
    ys = [lax.rem(y + i, NY) for i in range(1, NY)]
    xdevs = [(y * NX + i, t) for i in xs]
    ydevs = [(i * NX + x, t) for i in ys]
    own_rows = pl.ds(1 + rows * core, rows)
    mate_rows = pl.ds(1 + rows * other, rows)

    loads = [
        pltpu.make_async_copy(feat_h, fx.at[core], load_s.at[0]),
        pltpu.make_async_copy(cot_h, ext.at[0:2, own_rows], load_s.at[1]),
        pltpu.make_async_copy(w_h, w, load_s.at[2]),
        pltpu.make_async_copy(gain_h, gain, load_s.at[3]),
        pltpu.make_async_copy(bias_h, bias, load_s.at[4]),
    ]
    for c in loads:
        c.start()

    barrier = pltpu.get_barrier_semaphore()
    near = [dev for i, dev in zip(far, zdevs) if min(i, NZ - i) <= REACH]
    edge = [dev for i, dev in zip(far, zdevs) if min(i, NZ - i) == REACH]
    greet = near + fboth + [(f, zn * 2 + other)]
    for dev in greet:
        pl.semaphore_signal(barrier, inc=1, device_id=dev, device_id_type=MESH)

    loads[0].wait()
    flat = fx.reshape(2, cells, ch)
    chunks = cells // CHUNK

    def add_up(k, acc):
        return acc + jnp.sum(flat[core, pl.ds(k * CHUNK, CHUNK), :].astype(F32), axis=0, keepdims=True)

    mean = lax.fori_loop(0, chunks, add_up, jnp.zeros((1, ch), F32)) / cells

    def add_sq(k, acc):
        d = flat[core, pl.ds(k * CHUNK, CHUNK), :].astype(F32) - mean
        return acc + jnp.sum(d * d, axis=0, keepdims=True)

    m2 = lax.fori_loop(0, chunks, add_sq, jnp.zeros((1, ch), F32))
    s1[core, f, 0:1, :] = mean
    s1[core, f, 1:2, :] = m2
    loads[1].wait()

    pl.semaphore_wait(barrier, len(greet))
    if stop == 1:
        for c in loads[2:]:
            c.wait()
        return

    def fan(buf, me, devs, k):
        for dev in devs:
            rcopy(buf.at[me], buf.at[me], sm_s.at[k], sm_r.at[k], dev).start()

    def fan_recv(buf, k, n):
        many = buf.at[pl.ds(0, n)]
        rcopy(many, many, sm_s.at[k], sm_r.at[k], mate).wait_recv()

    def fan_sent(buf, k, n):
        many = buf.at[pl.ds(0, n)]
        rcopy(many, many, sm_s.at[k], sm_r.at[k], mate).wait_send()

    def send_moments(dev):
        rcopy(s1.at[core, f], s1.at[core, f], sm_s.at[1], sm_r.at[1], dev).start()

    pl.when(core == 0)(lambda: send_moments(mate))
    for dev in fdevs:
        send_moments((dev[0], z * 2 + 1))
    for dev in edge:
        pl.semaphore_signal(known, inc=1, device_id=dev, device_id_type=MESH)
    block = ext.at[0:2, own_rows]
    to_mate = rcopy(block, block, halo_s.at[0], halo_r.at[0], mate)
    feats = rcopy(fx.at[core], fx.at[core], halo_s.at[1], halo_r.at[1], mate)
    edge_src, edge_dst = ext.at[0:2, 1 + (2 * rows - 1) * core], ext.at[0:2, (2 * rows + 1) * other]
    edges = [
        rcopy(edge_src, edge_dst, halo_s.at[2 + c], halo_r.at[2 + core], (f, zn * 2 + c)) for c in range(2)
    ]
    edge_in = [
        rcopy(ext.at[0:2, 2 * rows + 1], ext.at[0:2, 2 * rows + 1], halo_s.at[2], halo_r.at[2], mate),
        rcopy(ext.at[0:2, 0], ext.at[0:2, 0], halo_s.at[3], halo_r.at[3], mate),
    ]
    for c in [feats, to_mate] + edges:
        c.start()

    def combine(buf, each):
        m = buf[:, 0, :]
        n = m.shape[0]
        avg = jnp.sum(m, axis=0, keepdims=True) / n
        d = m - avg
        return avg, jnp.sum(buf[:, 1, :], axis=0, keepdims=True) + each * jnp.sum(
            d * d, axis=0, keepdims=True
        )

    before = (lax.rem(f - 1 + NF, NF), t)
    later = ext.at[2:4, own_rows]
    to_before = rcopy(block, later, halo_s.at[4], halo_r.at[4], before)
    to_before.start()

    for c in edge_in:
        c.wait_recv()

    @pl.when(z == 0)
    def _():
        ext[0:2, 0] = jnp.zeros((2, cols, ch), BF16)

    @pl.when(z == NZ - 1)
    def _():
        ext[0:2, 2 * rows + 1] = jnp.zeros((2, cols, ch), BF16)

    rims = [
        rcopy(ext.at[0:2, r], ext.at[2:4, r], halo_s.at[k], halo_r.at[k], before)
        for k, r in ((5, 0), (6, 2 * rows + 1))
    ]
    for c in rims:
        c.start()

    pl.semaphore_wait(known, len(edge))

    @pl.when(core == 1)
    def _():
        moments = s1.reshape(2 * NF, 2, ch)
        fan_recv(moments, 1, 2 * NF - 1)
        avg, m2 = combine(moments, float(cells))
        s2[z, 0:1, :] = avg
        s2[z, 1:2, :] = m2
        fan(s2, z, zdevs, 2)
        fan_sent(moments, 1, NF - 1)

    pl.when(core == 0)(lambda: fan_sent(s1.reshape(2 * NF, 2, ch), 1, NF))

    to_before.wait_recv()
    relay = rcopy(later, later, halo_s.at[7], halo_r.at[7], mate)
    relay.start()
    feats.wait()

    @pl.loop(0, 2 * chunks)
    def _(k):
        c, kk = k // chunks, lax.rem(k, chunks)
        per = chunks // frames
        to = (kk // per) * (2 * per) + c * per + lax.rem(kk, per)
        feat_t[to] = flat[c, pl.ds(kk * CHUNK, CHUNK), :].T

    to_mate.wait()
    for c in edges:
        c.wait_send()
    to_before.wait_send()
    for c in rims:
        c.wait()
    relay.wait()

    @pl.when(f == NF - 1)
    def _():
        ext[2:4] = jnp.zeros((2, 2 * rows + 2, cols, ch), BF16)

    @pl.loop(0, 4 * (2 * rows + 2))
    def _(k):
        p, r = k // (2 * rows + 2), lax.rem(k, 2 * rows + 2)
        v = ext[p, r].astype(F32)
        col = lax.broadcasted_iota(jnp.int32, v.shape, 0)
        up = jnp.where(col == cols - 1, 0.0, pltpu.roll(v, cols - 1, 0))
        down = jnp.where(col == 0, 0.0, pltpu.roll(v, 1, 0))
        cotx[0, p, r] = up.astype(BF16)
        cotx[1, p, r] = ext[p, r]
        cotx[2, p, r] = down.astype(BF16)

    for c in loads[2:]:
        c.wait()
    gw, bw = gain[...], bias[...]

    def down(v):
        return jnp.broadcast_to(v, (CHUNK, ch)).T

    bias_t = down(bw)
    to_mate = rcopy(s3, s3, sm_s.at[0], sm_r.at[0], mate)

    @pl.when(core == 1)
    def _():
        fan_recv(s2, 2, NZ - 1)
        avg, m2 = combine(s2, float(cells * 2 * NF))
        s3[0:1, :] = avg
        s3[1:2, :] = m2
        to_mate.start()
        fan_sent(s2, 2, NZ - 1)
        to_mate.wait_send()

    pl.when(core == 0)(to_mate.wait_recv)
    avg, m2 = s3[0:1, :], s3[1:2, :]
    per_channel = float(cells * 2 * NF * NZ)
    group = ch // GROUPS
    g_avg = group_sum(avg) / group
    d = avg - g_avg
    spread = group_sum(m2 + per_channel * (d * d)) / (per_channel * group)
    inv = lax.rsqrt(spread + EPS)

    def normed(c, k):
        xh = (flat[c, pl.ds(k * CHUNK, CHUNK), :].astype(F32) - g_avg) * inv
        nrm = xh * gw + bw
        return xh, nrm, 1.0 / (1.0 + jnp.exp(-nrm))

    avg_t, scale_t = down(g_avg), down(inv * gw)

    @pl.loop(0, 2 * chunks, unroll=4)
    def _(k):
        nrm = (feat_t[k].astype(F32) - avg_t) * scale_t + bias_t
        act_t[k] = (nrm * (1.0 / (1.0 + jnp.exp(-nrm)))).astype(BF16)

    def finish(who):
        parts, ra, rb = (
            [[bufs[8 * kind + 4 * who + 2 * g + h] for h in range(2)] for g in range(2)]
            for kind in range(3)
        )
        lens, first, share, base = LENS[who], FROM[who], SHARE[who], BASE[who]
        early, late = [x, y], [y, x]

        def early_dev(h, i):
            return (y * NX + lax.rem(x + i, NX), t) if h == 0 else (lax.rem(y + i, NY) * NX + x, t)

        def late_dev(h, i):
            return early_dev(1 - h, i)

        def row(ref, h, at):
            return ref.at[at] if h == 0 else ref.at[:, at]

        acts = jnp.concatenate([act_t[i] for i in range(2 * chunks)], axis=1)

        def first_stage(g):
            for j in range(max(lens[g])):
                halves = [h for h in range(2) if j < lens[g][h]]
                got = []
                for h in halves:
                    tap = base + first[g][h] + j
                    a, b, e = tap // 9, tap // 3 % 3, tap % 3
                    got.append(
                        cotx[e, pl.ds(2 - a, frames), pl.ds(2 - b, 2 * rows)].reshape(2 * cells, ch)
                    )
                out = jnp.dot(acts, jnp.concatenate(got, axis=1), preferred_element_type=F32)
                for n, h in enumerate(halves):
                    parts[g][h][:, :, j] = out[:, n * ch : (n + 1) * ch].reshape(NX, NY, 8, ch)
            for h in range(2):
                for i in (2, 1, 3):
                    to = lax.rem(early[h] + i, NX)
                    rcopy(
                        row(parts[g][h], h, to), ra[g][h].at[i - 1], rs_s.at[g, h], rs_r1.at[g, h], early_dev(h, i)
                    ).start()

        first_stage(0)
        first_stage(1)

        gact[...] = jnp.zeros_like(gact)

        @pl.loop(0, 9, unroll=3)
        def _(k):
            a, b = k // 3, lax.rem(k, 3)
            p, r = pl.ds(2 - a, frames), pl.ds(2 - b + rows * core, rows)
            taps = jnp.concatenate([w[3 * k], w[3 * k + 1], w[3 * k + 2]], axis=1)
            patch = jnp.concatenate([cotx[e, p, r].reshape(cells, ch) for e in range(3)], axis=1)
            gact[...] += lax.dot_general(patch, taps, (((1,), (1,)), ((), ())), preferred_element_type=F32)

        def norm_grad(k, acc):
            at_rows = pl.ds(k * CHUNK, CHUNK)
            xh, nrm, s = normed(core, k)
            gn = gact[at_rows, :] * s * (1.0 + nrm * (1.0 - s))
            gact[at_rows, :] = gn
            xhat[at_rows, :] = xh
            return (
                acc[0] + jnp.sum(gn * xh, axis=0, keepdims=True),
                acc[1] + jnp.sum(gn, axis=0, keepdims=True),
            )

        zero = jnp.zeros((1, ch), F32)
        d_gain, d_shift = lax.fori_loop(0, chunks, norm_grad, (zero, zero))
        g0[core, 0:1, :] = d_gain
        g0[core, 1:2, :] = d_shift
        fan(g0, core, [mate], 3)

        def pass_on(buf, k, n, to, me, devs):
            fan_recv(buf, k, n)
            to[me, 0:1, :] = jnp.sum(buf[:, 0, :], axis=0, keepdims=True)
            to[me, 1:2, :] = jnp.sum(buf[:, 1, :], axis=0, keepdims=True)
            fan(to, me, devs, k + 1)
            fan_sent(buf, k, n)

        pass_on(g0, 3, 1, g1, f, fdevs)

        def second_stage(g):
            for h in range(2):
                got = ra[g][h]
                rcopy(got, got, rs_s.at[g, h], rs_r1.at[g, h], mate).wait_recv()
                mine = row(parts[g][h], h, early[h])
                mine[...] += got[0] + got[1] + got[2]
                for i in (2, 1, 3):
                    rcopy(
                        mine.at[lax.rem(late[h] + i, NX)], rb[g][h].at[i - 1], rs_s.at[g, h], rs_r2.at[g, h],
                        late_dev(h, i),
                    ).start()

        def z_stage(g):
            for h in range(2):
                got = rb[g][h]
                rcopy(got, got, rs_s.at[g, h], rs_r2.at[g, h], mate).wait_recv()
                zsrc[first[g][h] : first[g][h] + lens[g][h]] = parts[g][h][x, y] + (got[0] + got[1] + got[2])
            for to, dev in zip(zs, zdevs):
                q = lax.rem(to + NZ - FIRST[who], NZ)

                @pl.when(jnp.logical_and(q >= first[g][0], q < first[g][0] + sum(lens[g])))
                def _():
                    rcopy(zsrc.at[q], rz.at[z], z_s.at[0], z_r.at[0], dev).start()

        second_stage(0)
        second_stage(1)
        z_stage(0)
        z_stage(1)
        owned = lax.rem(z + NZ - FIRST[who], NZ)
        owner = owned < share

        pass_on(g1, 4, NF - 1, g2, z, zdevs)
        sent = [
            [parts[g][h].reshape(NX * NY, lens[g][h], 8, ch).at[pl.ds(0, NX * NY - 1)] for h in range(2)]
            for g in range(2)
        ]
        for g in range(2):
            for h in range(2):
                rcopy(sent[g][h], sent[g][h], rs_s.at[g, h], rs_r2.at[g, h], mate).wait_send()

        def out_taps(g, h):
            return gk.at[pl.ds(base + first[g][h], lens[g][h])]

        def tiles(n):
            return rz.at[pl.ds(0, n)]

        @pl.when(owner)
        def _():
            rz[z] = zsrc[owned]
            rcopy(tiles(NZ - 1), tiles(NZ - 1), z_s.at[0], z_r.at[0], mate).wait_recv()
            tile = gk.at[base + owned, x, y]
            tile[...] = jnp.sum(rz[...], axis=0)
            for dev in zdevs:
                rcopy(tile, tile, z_s.at[1], z_r.at[1 + owned // first[1][0]], dev).start()

        fan_recv(g2, 5, NZ - 1)
        fan_sent(g2, 5, NZ - 1)
        d_gain = jnp.sum(g2[:, 0, :], axis=0, keepdims=True)
        d_shift = jnp.sum(g2[:, 1, :], axis=0, keepdims=True)
        gs[0:1, :] = d_gain
        gs[1:2, :] = d_shift
        count = per_channel * group
        g_mean = group_sum(gw * d_shift) / count
        g_proj = group_sum(gw * d_gain) / count
        out = fg.reshape(cells, ch)

        @pl.loop(0, chunks)
        def _(k):
            at_rows = pl.ds(pl.multiple_of(k * CHUNK, CHUNK), CHUNK)
            out[at_rows, :] = (
                inv * (gact[at_rows, :] * gw - g_mean - xhat[at_rows, :] * g_proj)
            ).astype(BF16)

        def z_recv(g):
            n = sum(lens[g])
            own = jnp.logical_and(owned >= first[g][0], owned < first[g][0] + n)

            @pl.when(own)
            def _():
                rcopy(tiles(n - 1), tiles(n - 1), z_s.at[1], z_r.at[1 + g], mate).wait_recv()

            @pl.when(jnp.logical_not(own))
            def _():
                rcopy(tiles(n), tiles(n), z_s.at[1], z_r.at[1 + g], mate).wait_recv()

        def come(piece, sem):
            rcopy(piece, piece, ag_s.at[0, 0], sem, mate).wait_recv()

        def forward(piece):
            rcopy(piece, piece, fw_s.at[0], fw_r.at[0], mate).start()

        def out_row(g, h, at):
            return out_taps(g, h).at[:, at] if h == 0 else out_taps(g, h).at[:, :, at]

        def behind(v, i):
            return lax.rem(v - i + NX, NX)

        for g in range(2):
            z_recv(g)
            for h in range(2):
                piece = out_taps(g, h).at[:, x, y]
                for i in (2, 1, 3):
                    rcopy(piece, piece, ag_s.at[g, h], ag_r1.at[g, h, i - 1], late_dev(h, i)).start()
        for g in range(2):
            for h in range(2):
                mine = out_row(g, h, early[h])
                for i in (1, 3, 2):
                    come(mine.at[:, behind(late[h], i)], ag_r1.at[g, h, i - 1])
                forward(mine)
                for i in (2, 1, 3):
                    rcopy(mine, mine, ag_s.at[g, h], ag_r2.at[g, h, i - 1], early_dev(h, i)).start()
        for g in range(2):
            for i in (1, 3, 2):
                for h in range(2):
                    theirs = out_row(g, h, behind(early[h], i))
                    come(theirs, ag_r2.at[g, h, i - 1])
                    forward(theirs)

        @pl.when(owner)
        def _():
            rcopy(tiles(NZ - 1), tiles(NZ - 1), z_s.at[1], z_r.at[0], mate).wait_send()
            rcopy(tiles(share - 1), tiles(share - 1), z_s.at[0], z_r.at[0], mate).wait_send()

        @pl.when(jnp.logical_not(owner))
        def _():
            rcopy(tiles(share), tiles(share), z_s.at[0], z_r.at[0], mate).wait_send()

        for g in range(2):
            for h in range(2):
                rcopy(sent[g][h], sent[g][h], ag_s.at[g, h], ag_r1.at[g, h, 0], mate).wait_send()
        full = gk.at[pl.ds(base, share)]
        rcopy(full, full, fw_s.at[0], fw_r.at[0], mate).wait_send()
        theirs = gk.at[pl.ds(BASE[1 - who], SHARE[1 - who])]
        rcopy(theirs, theirs, fw_s.at[0], fw_r.at[0], mate).wait_recv()

    for who in range(2):
        pl.when(core == who)(functools.partial(finish, who))


def place(fg, gk, gs, fg_o, gk_o, gain_o, shift_o, sem):
    copies = [
        pltpu.make_async_copy(gk.at[pl.ds(0, LAST + 1)], gk_o, sem.at[0]),
        pltpu.make_async_copy(fg, fg_o, sem.at[1]),
        pltpu.make_async_copy(gs.at[0:1], gain_o, sem.at[2]),
        pltpu.make_async_copy(gs.at[1:2], shift_o, sem.at[3]),
    ]
    for c in copies:
        c.start()
    for c in copies:
        c.wait()


def call(stop, cid, features, norm_gain_weight, norm_bias, kernel, cotangent):
    frames, rows, cols, ch = features.shape
    cells = frames * rows * cols
    vm = pl.BlockSpec(memory_space=pltpu.VMEM)
    hbm = pl.BlockSpec(memory_space=pltpu.HBM)
    dma = pltpu.SemaphoreType.DMA
    tile = (8, ch)
    return pl.pallas_call(
        functools.partial(body, stop),
        out_shape=(
            pltpu.VMEM(features.shape, BF16),
            pltpu.VMEM((sum(SHARE), NX, NY) + tile, F32),
            pltpu.VMEM((2, ch), F32),
        ),
        in_specs=[hbm] * 5,
        out_specs=(vm, vm, vm),
        scratch_shapes=[
            pltpu.VMEM((2,) + features.shape, BF16),
            pltpu.VMEM((1, ch), F32),
            pltpu.VMEM((1, ch), F32),
            pltpu.VMEM((27, ch, ch), BF16),
            pltpu.VMEM((4, 2 * rows + 2, cols, ch), BF16),
            pltpu.VMEM((3, 4, 2 * rows + 2, cols, ch), BF16),
            pltpu.VMEM((cells, ch), F32),
            pltpu.VMEM((cells, ch), F32),
            pltpu.VMEM((2 * cells // CHUNK, ch, CHUNK), BF16),
            pltpu.VMEM((2 * cells // CHUNK, ch, CHUNK), BF16),
            pltpu.VMEM((2, NF, 2, ch), F32),
            pltpu.VMEM((NZ, 2, ch), F32),
            pltpu.VMEM((2, ch), F32),
            pltpu.VMEM((2, 2, ch), F32),
            pltpu.VMEM((NF, 2, ch), F32),
            pltpu.VMEM((NZ, 2, ch), F32),
            pltpu.VMEM((NZ,) + tile, F32),
            pltpu.VMEM((NZ,) + tile, F32),
            dma((5,)), dma((8,)), dma((8,)),
            dma((6,)), dma((6,)),
            dma((2, 2)), dma((2, 2)), dma((2, 2)),
            dma((2,)), dma((3,)),
            dma((2, 2)), dma((2, 2, 3)), dma((2, 2, 3)),
            dma((1,)), dma((1,)),
            pltpu.SemaphoreType.REGULAR,
            *(
                pltpu.VMEM(dims + (n,) + tile, F32)
                for dims in ((NX, NY), (3, NX), (3,))
                for of in LENS
                for pair in of
                for n in pair
            ),
        ],
        compiler_params=pltpu.CompilerParams(
            collective_id=cid, has_side_effects=True, vmem_limit_bytes=24 * 2**20
        ),
    )(
        *(
            pltpu.with_memory_space_constraint(v, pltpu.HBM)
            for v in (
                features,
                norm_gain_weight.reshape(1, ch),
                norm_bias.reshape(1, ch),
                kernel.reshape(27, ch, ch),
                cotangent,
            )
        )
    )


def on_device(features, norm_gain_weight, norm_bias, kernel, cotangent):
    ch = features.shape[-1]
    made = call(0, 0, features, norm_gain_weight, norm_bias, kernel, cotangent)
    vm = pl.BlockSpec(memory_space=pltpu.VMEM)
    hbm = pl.BlockSpec(memory_space=pltpu.HBM)
    fg, taps, gain, shift = pl.pallas_call(
        place,
        out_shape=(
            jax.ShapeDtypeStruct(features.shape, BF16),
            jax.ShapeDtypeStruct((LAST + 1, NX, NY, 8, ch), F32),
            jax.ShapeDtypeStruct((1, ch), F32),
            jax.ShapeDtypeStruct((1, ch), F32),
        ),
        in_specs=[vm] * 3,
        out_specs=(hbm,) * 4,
        scratch_shapes=[pltpu.SemaphoreType.DMA((4,))],
        compiler_params=pltpu.CompilerParams(vmem_limit_bytes=4 * 2**20),
    )(*(pltpu.with_memory_space_constraint(v, pltpu.VMEM) for v in made))
    return fg, taps.reshape(3, 3, 3, ch, ch), gain.reshape(ch), shift.reshape(ch)


def solution(mesh):
    placed = (P("frame", "tile", None, None), P(), P(), P(), P("frame", "tile", None, None))
    return jax.shard_map(
        on_device,
        mesh=mesh,
        in_specs=placed,
        out_specs=(P("frame", "tile", None, None), P(), P(), P()),
        check_vma=False,
    )
```

```python
import functools

import jax
import jax.numpy as jnp
from jax import lax
from jax.experimental import pallas as pl
from jax.experimental.pallas import tpu as pltpu
from jax.sharding import PartitionSpec as P

MESH = pl.DeviceIdType.MESH
GROUPS = 32
EPS = 1e-06
NX = 4
NY = 4
NZ = 16
NF = NX * NY
LAST = 26
LENS = (((3, 3), (3, 3)), ((4, 4), (4, 3)))
SHARE = tuple(sum(map(sum, of)) for of in LENS)
BASE = (0, SHARE[0])
FROM = tuple(((0, p[0]), (sum(p), sum(p) + q[0])) for p, q in LENS)
FIRST = (11, 9)
F32 = jnp.float32
BF16 = jnp.bfloat16
CHUNK = 128
REACH = NZ // 4


def group_sum(v):
    lane = lax.broadcasted_iota(jnp.int32, v.shape, 1)
    v = v + jnp.where(lane % 2 == 0, pltpu.roll(v, 127, 1), pltpu.roll(v, 1, 1))
    return v + jnp.where(lane % 4 < 2, pltpu.roll(v, 126, 1), pltpu.roll(v, 2, 1))


def rcopy(src, dst, ss, rs, dev):
    return pltpu.make_async_remote_copy(
        src_ref=src, dst_ref=dst, send_sem=ss, recv_sem=rs, device_id=dev, device_id_type=MESH
    )


def body(
    stop,
    feat_h, gain_h, bias_h, w_h, cot_h,
    fg, gk, gs,
    fx, gain, bias, w, ext, cotx, gact, xhat, feat_t, act_t,
    s1, s2, s3, g0, g1, g2,
    zsrc, rz,
    load_s, halo_s, halo_r, sm_s, sm_r, rs_s, rs_r1, rs_r2, z_s, z_r, ag_s, ag_r1, ag_r2, fw_s, fw_r, known, *bufs,
):
    f, t = lax.axis_index("frame"), lax.axis_index("tile")
    y, x = f // NX, lax.rem(f, NX)
    z, core = t // 2, lax.rem(t, 2)
    other = 1 - core
    _, frames, rows, cols, ch = fx.shape
    cells = frames * rows * cols
    mate = (f, z * 2 + other)
    zn = lax.rem(z - 1 + 2 * core + NZ, NZ)
    fdevs = [(lax.rem(f + i, NF), t) for i in range(1, NF)]
    fboth = [mate] + [(dev[0], z * 2 + c) for dev in fdevs for c in (core, other)]
    far = sorted(range(1, NZ), key=lambda i: -min(i, NZ - i))
    zs = [lax.rem(z + i, NZ) for i in far]
    zdevs = [(f, j * 2 + core) for j in zs]
    xs = [lax.rem(x + i, NX) for i in range(1, NX)]
    ys = [lax.rem(y + i, NY) for i in range(1, NY)]
    xdevs = [(y * NX + i, t) for i in xs]
    ydevs = [(i * NX + x, t) for i in ys]
    own_rows = pl.ds(1 + rows * core, rows)
    mate_rows = pl.ds(1 + rows * other, rows)

    loads = [
        pltpu.make_async_copy(feat_h, fx.at[core], load_s.at[0]),
        pltpu.make_async_copy(cot_h, ext.at[0:2, own_rows], load_s.at[1]),
        pltpu.make_async_copy(w_h, w, load_s.at[2]),
        pltpu.make_async_copy(gain_h, gain, load_s.at[3]),
        pltpu.make_async_copy(bias_h, bias, load_s.at[4]),
    ]
    for c in loads:
        c.start()

    barrier = pltpu.get_barrier_semaphore()
    near = [dev for i, dev in zip(far, zdevs) if min(i, NZ - i) <= REACH]
    edge = [dev for i, dev in zip(far, zdevs) if min(i, NZ - i) == REACH]
    greet = near + fboth + [(f, zn * 2 + other)]
    for dev in greet:
        pl.semaphore_signal(barrier, inc=1, device_id=dev, device_id_type=MESH)

    loads[0].wait()
    flat = fx.reshape(2, cells, ch)
    chunks = cells // CHUNK

    def add_up(k, acc):
        return acc + jnp.sum(flat[core, pl.ds(k * CHUNK, CHUNK), :].astype(F32), axis=0, keepdims=True)

    mean = lax.fori_loop(0, chunks, add_up, jnp.zeros((1, ch), F32)) / cells

    def add_sq(k, acc):
        d = flat[core, pl.ds(k * CHUNK, CHUNK), :].astype(F32) - mean
        return acc + jnp.sum(d * d, axis=0, keepdims=True)

    m2 = lax.fori_loop(0, chunks, add_sq, jnp.zeros((1, ch), F32))
    s1[core, f, 0:1, :] = mean
    s1[core, f, 1:2, :] = m2
    loads[1].wait()

    pl.semaphore_wait(barrier, len(greet))
    if stop == 1:
        for c in loads[2:]:
            c.wait()
        return

    def fan(buf, me, devs, k):
        for dev in devs:
            rcopy(buf.at[me], buf.at[me], sm_s.at[k], sm_r.at[k], dev).start()

    def fan_recv(buf, k, n):
        many = buf.at[pl.ds(0, n)]
        rcopy(many, many, sm_s.at[k], sm_r.at[k], mate).wait_recv()

    def fan_sent(buf, k, n):
        many = buf.at[pl.ds(0, n)]
        rcopy(many, many, sm_s.at[k], sm_r.at[k], mate).wait_send()

    def send_moments(dev):
        rcopy(s1.at[core, f], s1.at[core, f], sm_s.at[1], sm_r.at[1], dev).start()

    pl.when(core == 0)(lambda: send_moments(mate))
    for dev in fdevs:
        send_moments((dev[0], z * 2 + 1))
    for dev in edge:
        pl.semaphore_signal(known, inc=1, device_id=dev, device_id_type=MESH)
    block = ext.at[0:2, own_rows]
    to_mate = rcopy(block, block, halo_s.at[0], halo_r.at[0], mate)
    feats = rcopy(fx.at[core], fx.at[core], halo_s.at[1], halo_r.at[1], mate)
    edge_src, edge_dst = ext.at[0:2, 1 + (2 * rows - 1) * core], ext.at[0:2, (2 * rows + 1) * other]
    edges = [
        rcopy(edge_src, edge_dst, halo_s.at[2 + c], halo_r.at[2 + core], (f, zn * 2 + c)) for c in range(2)
    ]
    edge_in = [
        rcopy(ext.at[0:2, 2 * rows + 1], ext.at[0:2, 2 * rows + 1], halo_s.at[2], halo_r.at[2], mate),
        rcopy(ext.at[0:2, 0], ext.at[0:2, 0], halo_s.at[3], halo_r.at[3], mate),
    ]
    for c in [feats, to_mate] + edges:
        c.start()

    def combine(buf, each):
        m = buf[:, 0, :]
        n = m.shape[0]
        avg = jnp.sum(m, axis=0, keepdims=True) / n
        d = m - avg
        return avg, jnp.sum(buf[:, 1, :], axis=0, keepdims=True) + each * jnp.sum(
            d * d, axis=0, keepdims=True
        )

    before = (lax.rem(f - 1 + NF, NF), t)
    later = ext.at[2:4, own_rows]
    to_before = rcopy(block, later, halo_s.at[4], halo_r.at[4], before)
    to_before.start()

    for c in edge_in:
        c.wait_recv()

    @pl.when(z == 0)
    def _():
        ext[0:2, 0] = jnp.zeros((2, cols, ch), BF16)

    @pl.when(z == NZ - 1)
    def _():
        ext[0:2, 2 * rows + 1] = jnp.zeros((2, cols, ch), BF16)

    rims = [
        rcopy(ext.at[0:2, r], ext.at[2:4, r], halo_s.at[k], halo_r.at[k], before)
        for k, r in ((5, 0), (6, 2 * rows + 1))
    ]
    for c in rims:
        c.start()

    pl.semaphore_wait(known, len(edge))

    @pl.when(core == 1)
    def _():
        moments = s1.reshape(2 * NF, 2, ch)
        fan_recv(moments, 1, 2 * NF - 1)
        avg, m2 = combine(moments, float(cells))
        s2[z, 0:1, :] = avg
        s2[z, 1:2, :] = m2
        fan(s2, z, zdevs, 2)
        fan_sent(moments, 1, NF - 1)

    pl.when(core == 0)(lambda: fan_sent(s1.reshape(2 * NF, 2, ch), 1, NF))

    to_before.wait_recv()
    relay = rcopy(later, later, halo_s.at[7], halo_r.at[7], mate)
    relay.start()
    feats.wait()

    @pl.loop(0, 2 * chunks)
    def _(k):
        c, kk = k // chunks, lax.rem(k, chunks)
        per = chunks // frames
        to = (kk // per) * (2 * per) + c * per + lax.rem(kk, per)
        feat_t[to] = flat[c, pl.ds(kk * CHUNK, CHUNK), :].T

    to_mate.wait()
    for c in edges:
        c.wait_send()
    to_before.wait_send()
    for c in rims:
        c.wait()
    relay.wait()

    @pl.when(f == NF - 1)
    def _():
        ext[2:4] = jnp.zeros((2, 2 * rows + 2, cols, ch), BF16)

    @pl.loop(0, 4 * (2 * rows + 2))
    def _(k):
        p, r = k // (2 * rows + 2), lax.rem(k, 2 * rows + 2)
        v = ext[p, r].astype(F32)
        col = lax.broadcasted_iota(jnp.int32, v.shape, 0)
        up = jnp.where(col == cols - 1, 0.0, pltpu.roll(v, cols - 1, 0))
        down = jnp.where(col == 0, 0.0, pltpu.roll(v, 1, 0))
        cotx[0, p, r] = up.astype(BF16)
        cotx[1, p, r] = ext[p, r]
        cotx[2, p, r] = down.astype(BF16)

    for c in loads[2:]:
        c.wait()
    gw, bw = gain[...], bias[...]

    def down(v):
        return jnp.broadcast_to(v, (CHUNK, ch)).T

    bias_t = down(bw)
    to_mate = rcopy(s3, s3, sm_s.at[0], sm_r.at[0], mate)

    @pl.when(core == 1)
    def _():
        fan_recv(s2, 2, NZ - 1)
        avg, m2 = combine(s2, float(cells * 2 * NF))
        s3[0:1, :] = avg
        s3[1:2, :] = m2
        to_mate.start()
        fan_sent(s2, 2, NZ - 1)
        to_mate.wait_send()

    pl.when(core == 0)(to_mate.wait_recv)
    avg, m2 = s3[0:1, :], s3[1:2, :]
    per_channel = float(cells * 2 * NF * NZ)
    group = ch // GROUPS
    g_avg = group_sum(avg) / group
    d = avg - g_avg
    spread = group_sum(m2 + per_channel * (d * d)) / (per_channel * group)
    inv = lax.rsqrt(spread + EPS)

    def normed(c, k):
        xh = (flat[c, pl.ds(k * CHUNK, CHUNK), :].astype(F32) - g_avg) * inv
        nrm = xh * gw + bw
        return xh, nrm, 1.0 / (1.0 + jnp.exp(-nrm))

    avg_t, scale_t = down(g_avg), down(inv * gw)

    @pl.loop(0, 2 * chunks, unroll=4)
    def _(k):
        nrm = (feat_t[k].astype(F32) - avg_t) * scale_t + bias_t
        act_t[k] = (nrm * (1.0 / (1.0 + jnp.exp(-nrm)))).astype(BF16)

    def finish(who):
        parts, ra, rb = (
            [[bufs[8 * kind + 4 * who + 2 * g + h] for h in range(2)] for g in range(2)]
            for kind in range(3)
        )
        lens, first, share, base = LENS[who], FROM[who], SHARE[who], BASE[who]
        early, late = [x, y], [y, x]

        def early_dev(h, i):
            return (y * NX + lax.rem(x + i, NX), t) if h == 0 else (lax.rem(y + i, NY) * NX + x, t)

        def late_dev(h, i):
            return early_dev(1 - h, i)

        def row(ref, h, at):
            return ref.at[at] if h == 0 else ref.at[:, at]

        acts = jnp.concatenate([act_t[i] for i in range(2 * chunks)], axis=1)

        def first_stage(g):
            for j in range(max(lens[g])):
                halves = [h for h in range(2) if j < lens[g][h]]
                got = []
                for h in halves:
                    tap = base + first[g][h] + j
                    a, b, e = tap // 9, tap // 3 % 3, tap % 3
                    got.append(
                        cotx[e, pl.ds(2 - a, frames), pl.ds(2 - b, 2 * rows)].reshape(2 * cells, ch)
                    )
                out = jnp.dot(acts, jnp.concatenate(got, axis=1), preferred_element_type=F32)
                for n, h in enumerate(halves):
                    parts[g][h][:, :, j] = out[:, n * ch : (n + 1) * ch].reshape(NX, NY, 8, ch)
            for h in range(2):
                for i in (2, 1, 3):
                    to = lax.rem(early[h] + i, NX)
                    rcopy(
                        row(parts[g][h], h, to), ra[g][h].at[i - 1], rs_s.at[g, h], rs_r1.at[g, h], early_dev(h, i)
                    ).start()

        first_stage(0)
        first_stage(1)

        gact[...] = jnp.zeros_like(gact)

        @pl.loop(0, 9, unroll=3)
        def _(k):
            a, b = k // 3, lax.rem(k, 3)
            p, r = pl.ds(2 - a, frames), pl.ds(2 - b + rows * core, rows)
            taps = jnp.concatenate([w[3 * k], w[3 * k + 1], w[3 * k + 2]], axis=1)
            patch = jnp.concatenate([cotx[e, p, r].reshape(cells, ch) for e in range(3)], axis=1)
            gact[...] += lax.dot_general(patch, taps, (((1,), (1,)), ((), ())), preferred_element_type=F32)

        def norm_grad(k, acc):
            at_rows = pl.ds(k * CHUNK, CHUNK)
            xh, nrm, s = normed(core, k)
            gn = gact[at_rows, :] * s * (1.0 + nrm * (1.0 - s))
            gact[at_rows, :] = gn
            xhat[at_rows, :] = xh
            return (
                acc[0] + jnp.sum(gn * xh, axis=0, keepdims=True),
                acc[1] + jnp.sum(gn, axis=0, keepdims=True),
            )

        zero = jnp.zeros((1, ch), F32)
        d_gain, d_shift = lax.fori_loop(0, chunks, norm_grad, (zero, zero))
        g0[core, 0:1, :] = d_gain
        g0[core, 1:2, :] = d_shift
        fan(g0, core, [mate], 3)

        def pass_on(buf, k, n, to, me, devs):
            fan_recv(buf, k, n)
            to[me, 0:1, :] = jnp.sum(buf[:, 0, :], axis=0, keepdims=True)
            to[me, 1:2, :] = jnp.sum(buf[:, 1, :], axis=0, keepdims=True)
            fan(to, me, devs, k + 1)
            fan_sent(buf, k, n)


        def second_stage(g):
            for h in range(2):
                got = ra[g][h]
                rcopy(got, got, rs_s.at[g, h], rs_r1.at[g, h], mate).wait_recv()
                mine = row(parts[g][h], h, early[h])
                mine[...] += got[0] + got[1] + got[2]
                for i in (2, 1, 3):
                    rcopy(
                        mine.at[lax.rem(late[h] + i, NX)], rb[g][h].at[i - 1], rs_s.at[g, h], rs_r2.at[g, h],
                        late_dev(h, i),
                    ).start()

        def z_stage(g):
            for h in range(2):
                got = rb[g][h]
                rcopy(got, got, rs_s.at[g, h], rs_r2.at[g, h], mate).wait_recv()
                zsrc[first[g][h] : first[g][h] + lens[g][h]] = parts[g][h][x, y] + (got[0] + got[1] + got[2])
            for to, dev in zip(zs, zdevs):
                q = lax.rem(to + NZ - FIRST[who], NZ)

                @pl.when(jnp.logical_and(q >= first[g][0], q < first[g][0] + sum(lens[g])))
                def _():
                    rcopy(zsrc.at[q], rz.at[z], z_s.at[0], z_r.at[0], dev).start()

        second_stage(0)
        pass_on(g0, 3, 1, g1, f, fdevs)
        second_stage(1)
        z_stage(0)
        z_stage(1)
        owned = lax.rem(z + NZ - FIRST[who], NZ)
        owner = owned < share

        pass_on(g1, 4, NF - 1, g2, z, zdevs)
        sent = [
            [parts[g][h].reshape(NX * NY, lens[g][h], 8, ch).at[pl.ds(0, NX * NY - 1)] for h in range(2)]
            for g in range(2)
        ]
        for g in range(2):
            for h in range(2):
                rcopy(sent[g][h], sent[g][h], rs_s.at[g, h], rs_r2.at[g, h], mate).wait_send()

        def out_taps(g, h):
            return gk.at[pl.ds(base + first[g][h], lens[g][h])]

        def tiles(n):
            return rz.at[pl.ds(0, n)]

        @pl.when(owner)
        def _():
            rz[z] = zsrc[owned]
            rcopy(tiles(NZ - 1), tiles(NZ - 1), z_s.at[0], z_r.at[0], mate).wait_recv()
            tile = gk.at[base + owned, x, y]
            tile[...] = jnp.sum(rz[...], axis=0)
            for dev in zdevs:
                rcopy(tile, tile, z_s.at[1], z_r.at[1 + owned // first[1][0]], dev).start()

        fan_recv(g2, 5, NZ - 1)
        fan_sent(g2, 5, NZ - 1)
        d_gain = jnp.sum(g2[:, 0, :], axis=0, keepdims=True)
        d_shift = jnp.sum(g2[:, 1, :], axis=0, keepdims=True)
        gs[0:1, :] = d_gain
        gs[1:2, :] = d_shift
        count = per_channel * group
        g_mean = group_sum(gw * d_shift) / count
        g_proj = group_sum(gw * d_gain) / count
        out = fg.reshape(cells, ch)

        @pl.loop(0, chunks)
        def _(k):
            at_rows = pl.ds(pl.multiple_of(k * CHUNK, CHUNK), CHUNK)
            out[at_rows, :] = (
                inv * (gact[at_rows, :] * gw - g_mean - xhat[at_rows, :] * g_proj)
            ).astype(BF16)

        def z_recv(g):
            n = sum(lens[g])
            own = jnp.logical_and(owned >= first[g][0], owned < first[g][0] + n)

            @pl.when(own)
            def _():
                rcopy(tiles(n - 1), tiles(n - 1), z_s.at[1], z_r.at[1 + g], mate).wait_recv()

            @pl.when(jnp.logical_not(own))
            def _():
                rcopy(tiles(n), tiles(n), z_s.at[1], z_r.at[1 + g], mate).wait_recv()

        def come(piece, sem):
            rcopy(piece, piece, ag_s.at[0, 0], sem, mate).wait_recv()

        def forward(piece):
            rcopy(piece, piece, fw_s.at[0], fw_r.at[0], mate).start()

        def out_row(g, h, at):
            return out_taps(g, h).at[:, at] if h == 0 else out_taps(g, h).at[:, :, at]

        def behind(v, i):
            return lax.rem(v - i + NX, NX)

        for g in range(2):
            z_recv(g)
            for h in range(2):
                piece = out_taps(g, h).at[:, x, y]
                for i in (2, 1, 3):
                    rcopy(piece, piece, ag_s.at[g, h], ag_r1.at[g, h, i - 1], late_dev(h, i)).start()
        for g in range(2):
            for h in range(2):
                mine = out_row(g, h, early[h])
                for i in (1, 3, 2):
                    come(mine.at[:, behind(late[h], i)], ag_r1.at[g, h, i - 1])
                forward(mine)
                for i in (2, 1, 3):
                    rcopy(mine, mine, ag_s.at[g, h], ag_r2.at[g, h, i - 1], early_dev(h, i)).start()
        for g in range(2):
            for i in (1, 3, 2):
                for h in range(2):
                    theirs = out_row(g, h, behind(early[h], i))
                    come(theirs, ag_r2.at[g, h, i - 1])
                    forward(theirs)

        @pl.when(owner)
        def _():
            rcopy(tiles(NZ - 1), tiles(NZ - 1), z_s.at[1], z_r.at[0], mate).wait_send()
            rcopy(tiles(share - 1), tiles(share - 1), z_s.at[0], z_r.at[0], mate).wait_send()

        @pl.when(jnp.logical_not(owner))
        def _():
            rcopy(tiles(share), tiles(share), z_s.at[0], z_r.at[0], mate).wait_send()

        for g in range(2):
            for h in range(2):
                rcopy(sent[g][h], sent[g][h], ag_s.at[g, h], ag_r1.at[g, h, 0], mate).wait_send()
        full = gk.at[pl.ds(base, share)]
        rcopy(full, full, fw_s.at[0], fw_r.at[0], mate).wait_send()
        theirs = gk.at[pl.ds(BASE[1 - who], SHARE[1 - who])]
        rcopy(theirs, theirs, fw_s.at[0], fw_r.at[0], mate).wait_recv()

    for who in range(2):
        pl.when(core == who)(functools.partial(finish, who))


def place(fg, gk, gs, fg_o, gk_o, gain_o, shift_o, sem):
    copies = [
        pltpu.make_async_copy(gk.at[pl.ds(0, LAST + 1)], gk_o, sem.at[0]),
        pltpu.make_async_copy(fg, fg_o, sem.at[1]),
        pltpu.make_async_copy(gs.at[0:1], gain_o, sem.at[2]),
        pltpu.make_async_copy(gs.at[1:2], shift_o, sem.at[3]),
    ]
    for c in copies:
        c.start()
    for c in copies:
        c.wait()


def call(stop, cid, features, norm_gain_weight, norm_bias, kernel, cotangent):
    frames, rows, cols, ch = features.shape
    cells = frames * rows * cols
    vm = pl.BlockSpec(memory_space=pltpu.VMEM)
    hbm = pl.BlockSpec(memory_space=pltpu.HBM)
    dma = pltpu.SemaphoreType.DMA
    tile = (8, ch)
    return pl.pallas_call(
        functools.partial(body, stop),
        out_shape=(
            pltpu.VMEM(features.shape, BF16),
            pltpu.VMEM((sum(SHARE), NX, NY) + tile, F32),
            pltpu.VMEM((2, ch), F32),
        ),
        in_specs=[hbm] * 5,
        out_specs=(vm, vm, vm),
        scratch_shapes=[
            pltpu.VMEM((2,) + features.shape, BF16),
            pltpu.VMEM((1, ch), F32),
            pltpu.VMEM((1, ch), F32),
            pltpu.VMEM((27, ch, ch), BF16),
            pltpu.VMEM((4, 2 * rows + 2, cols, ch), BF16),
            pltpu.VMEM((3, 4, 2 * rows + 2, cols, ch), BF16),
            pltpu.VMEM((cells, ch), F32),
            pltpu.VMEM((cells, ch), F32),
            pltpu.VMEM((2 * cells // CHUNK, ch, CHUNK), BF16),
            pltpu.VMEM((2 * cells // CHUNK, ch, CHUNK), BF16),
            pltpu.VMEM((2, NF, 2, ch), F32),
            pltpu.VMEM((NZ, 2, ch), F32),
            pltpu.VMEM((2, ch), F32),
            pltpu.VMEM((2, 2, ch), F32),
            pltpu.VMEM((NF, 2, ch), F32),
            pltpu.VMEM((NZ, 2, ch), F32),
            pltpu.VMEM((NZ,) + tile, F32),
            pltpu.VMEM((NZ,) + tile, F32),
            dma((5,)), dma((8,)), dma((8,)),
            dma((6,)), dma((6,)),
            dma((2, 2)), dma((2, 2)), dma((2, 2)),
            dma((2,)), dma((3,)),
            dma((2, 2)), dma((2, 2, 3)), dma((2, 2, 3)),
            dma((1,)), dma((1,)),
            pltpu.SemaphoreType.REGULAR,
            *(
                pltpu.VMEM(dims + (n,) + tile, F32)
                for dims in ((NX, NY), (3, NX), (3,))
                for of in LENS
                for pair in of
                for n in pair
            ),
        ],
        compiler_params=pltpu.CompilerParams(
            collective_id=cid, has_side_effects=True, vmem_limit_bytes=24 * 2**20
        ),
    )(
        *(
            pltpu.with_memory_space_constraint(v, pltpu.HBM)
            for v in (
                features,
                norm_gain_weight.reshape(1, ch),
                norm_bias.reshape(1, ch),
                kernel.reshape(27, ch, ch),
                cotangent,
            )
        )
    )


def on_device(features, norm_gain_weight, norm_bias, kernel, cotangent):
    ch = features.shape[-1]
    made = call(0, 0, features, norm_gain_weight, norm_bias, kernel, cotangent)
    vm = pl.BlockSpec(memory_space=pltpu.VMEM)
    hbm = pl.BlockSpec(memory_space=pltpu.HBM)
    fg, taps, gain, shift = pl.pallas_call(
        place,
        out_shape=(
            jax.ShapeDtypeStruct(features.shape, BF16),
            jax.ShapeDtypeStruct((LAST + 1, NX, NY, 8, ch), F32),
            jax.ShapeDtypeStruct((1, ch), F32),
            jax.ShapeDtypeStruct((1, ch), F32),
        ),
        in_specs=[vm] * 3,
        out_specs=(hbm,) * 4,
        scratch_shapes=[pltpu.SemaphoreType.DMA((4,))],
        compiler_params=pltpu.CompilerParams(vmem_limit_bytes=4 * 2**20),
    )(*(pltpu.with_memory_space_constraint(v, pltpu.VMEM) for v in made))
    return fg, taps.reshape(3, 3, 3, ch, ch), gain.reshape(ch), shift.reshape(ch)


def solution(mesh):
    placed = (P("frame", "tile", None, None), P(), P(), P(), P("frame", "tile", None, None))
    return jax.shard_map(
        on_device,
        mesh=mesh,
        in_specs=placed,
        out_specs=(P("frame", "tile", None, None), P(), P(), P()),
        check_vma=False,
    )
```
